32 devices in a mesh: dp: 4 (over x, core), wide: 8 (over z, y).
Axes of the slice: x: 2, y: 2, z: 4, core: 2. Of those that a mesh axis runs over, the one named last changes fastest.
Arguments:
- images: bfloat16 [768, 7, 7, 2048], P(('dp', 'wide')), may hold values from -6 to 6
- crop_pixels: bfloat16 [512, 2, 2, 2048], P(('dp', 'wide')), may hold values from -6 to 6
- thresholds: bfloat16 [39680, 2048], P(('dp', 'wide')), may hold values from 0 to 1
- cotangent: bfloat16 [39680, 384], P(('dp', 'wide')), may hold values from -6 to 6
- image_count: int32 [32], P(('dp', 'wide')), may hold values from 1 to 24, as said below
- crop_count: int32 [32], P(('dp', 'wide')), may hold values from 1 to 16, as said below
- reduce_weight: float32 [2048, 512], P('wide'), may hold values from -0.125 to 0.125
- spatial_weight: float32 [4608, 512], P('wide'), may hold values from -0.09375 to 0.09375
- expand_weight: float32 [512, 2048], P('wide'), may hold values from -0.25 to 0.25
- heads_weight: float32 [2048, 384], P('wide'), may hold values from -0.125 to 0.125
- norm_gains: float32 [3072], P('wide'), may hold values from 0.3 to 2.5
- norm_shifts: float32 [3072], P('wide'), may hold values from -3 to 3
- first_reduce: float32 [2048, 512], P('wide'), may hold values from -0.00036621094 to 0.00036621094
- first_spatial: float32 [4608, 512], P('wide'), may hold values from -0.00036621094 to 0.00036621094
- first_expand: float32 [512, 2048], P('wide'), may hold values from -0.00036621094 to 0.00036621094
- first_heads: float32 [2048, 384], P('wide'), may hold values from -0.0017089844 to 0.0017089844
- first_norm: float32 [2, 3072], P(None, 'wide'), may hold values from -0.00036621094 to 0.00036621094
- second_reduce: float32 [2048, 512], P('wide'), may hold values from 4.76279e-11 to 1.905116e-10
- second_spatial: float32 [4608, 512], P('wide'), may hold values from 4.76279e-11 to 1.905116e-10
- second_expand: float32 [512, 2048], P('wide'), may hold values from 4.76279e-11 to 1.905116e-10
- second_heads: float32 [2048, 384], P('wide'), may hold values from 9.52558e-10 to 3.810232e-09
- second_norm: float32 [2, 3072], P(None, 'wide'), may hold values from 4.76279e-11 to 1.905116e-10
Outputs:
- norm_before: float32 [], replicated
- predictions: bfloat16 [39680, 384], P(('dp', 'wide'))
- grad_images: bfloat16 [768, 7, 7, 2048], P(('dp', 'wide'))
- grad_crops: bfloat16 [512, 2, 2, 2048], P(('dp', 'wide'))
- new_reduce: float32 [2048, 512], P('wide')
- new_spatial: float32 [4608, 512], P('wide')
- new_expand: float32 [512, 2048], P('wide')
- new_heads: float32 [2048, 384], P('wide')
- new_norm: float32 [2, 3072], P(None, 'wide')
- moment_reduce: float32 [2048, 512], P('wide')
- moment_spatial: float32 [4608, 512], P('wide')
- moment_expand: float32 [512, 2048], P('wide')
- moment_heads: float32 [2048, 384], P('wide')
- moment_norm: float32 [2, 3072], P(None, 'wide')
- square_reduce: float32 [2048, 512], P('wide')
- square_spatial: float32 [4608, 512], P('wide')
- square_expand: float32 [512, 2048], P('wide')
- square_heads: float32 [2048, 384], P('wide')
- square_norm: float32 [2, 3072], P(None, 'wide')
The draws below stay inside these ranges and needn't reach their ends.
Inputs may be any that keep to these rules, and one draw needn't show every extreme that they name: `image_count`: live image slots of a device come first; on some device all 24 are live. `crop_count`: live crop slots of a device come first; on some device all 16 are live.
All inputs are finite; a program needn't handle non-finite values.
Results may differ from the reference program's by a relative error of at most 0.011.
The reference program's roundings to bfloat16 on the way count: a program that leaves them out, or rounds other values in their place, can miss the bound.
Values may be sent and summed in bfloat16 or wider, within the bound.
No kernel may reach another device: no remote copies, remote signals or barrier semaphores. Data moves between devices by JAX's collectives and lax.ppermute only.
A program may use at most 320 MiB of HBM per device.

```python
import math
from functools import partial
import jax
import jax.numpy as jnp
from jax import lax

C_IN = 2048
C_MID = 512
HEAD = 128
TASKS = 3
SIDE = 7
CROP_SIDE = 2
STEP = 10
IMG_CAP = 24
CROP_CAP = 16
IMAGES = 768
CROPS = 512
ROWS_DEV = 1240
ROWS = 39680
NORM_W = 3072
OUT_W = 384
NPARAM = 5249024
N_WIDE = 8
DEVICES = 32


def rising_count(key, capacity):
    device_index = jnp.arange(DEVICES, dtype=jnp.int32)
    group_count = DEVICES // N_WIDE
    group_index = device_index // N_WIDE
    wide_index = device_index % N_WIDE
    divisor = 3 * (N_WIDE - 1) * (group_count - 1)
    baseline = capacity * ((N_WIDE - 1) * (group_count - 1) + wide_index * (group_count - 1) + group_index * (N_WIDE - 1)) // divisor
    jitter_key, full_key = jax.random.split(key)
    jitter = jax.random.randint(jitter_key, (DEVICES,), -2, 1, dtype=jnp.int32)
    counts = jnp.clip(baseline + jitter, 1, capacity)
    chosen = jax.random.randint(full_key, (), 0, DEVICES, dtype=jnp.int32)
    return jnp.where(device_index == chosen, capacity, counts).astype(jnp.int32)


def draw_image_count(key, part):
    key = jax.random.fold_in(key, 11)
    return rising_count(key, IMG_CAP)


def draw_crop_count(key, part):
    key = jax.random.fold_in(key, 12)
    return rising_count(key, CROP_CAP)


def draw_norm_gains(key, part):
    key = jax.random.fold_in(key, 21)
    channel = jnp.arange(NORM_W)
    segment_start = jnp.where(channel < C_MID, 0, jnp.where(channel < 2 * C_MID, C_MID, 2 * C_MID))
    segment_length = jnp.where(channel < 2 * C_MID, C_MID, C_IN)
    position = (channel - segment_start).astype(jnp.float32) / (segment_length - 1).astype(jnp.float32)
    jitter = jax.random.uniform(key, (NORM_W,), jnp.float32, 0.8, 1.25)
    return ((0.6 + 1.2 * position) * jitter).astype(jnp.float32)


def block_levels(own_key, shape, cuts, low, largest):
    loudness = 1.0
    for dim, parts in cuts:
        steps = jax.random.uniform(jax.random.fold_in(jax.random.fold_in(own_key, 6), dim), (parts,), jnp.float32, low / len(cuts), largest / len(cuts))
        loudness = loudness * jnp.repeat(jnp.exp(steps), shape[dim] // parts).reshape((-1,) + (1,) * (len(shape) - 1 - dim))
    return loudness


def scatter_about(own_key, dims, scale, limit, cuts=(), held_as=jnp.bfloat16):
    factor_of = block_levels(own_key, dims, cuts, -0.22, 0.18) if cuts else 1.0
    drawn = jax.random.normal(own_key, dims, jnp.float32) * scale * factor_of
    return jnp.minimum(jnp.maximum(drawn, -limit), limit).astype(held_as)


def setup_inputs(seed: int = 0) -> dict:
    key_of = jax.random.split(jax.random.key(seed), 23)
    return {
        "images": scatter_about(key_of[0], (IMAGES, SIDE, SIDE, C_IN), 1.0, 6.0, ((0, 32),)),
        "crop_pixels": scatter_about(key_of[1], (CROPS, CROP_SIDE, CROP_SIDE, C_IN), 1.0, 6.0, ((0, 32),)),
        "thresholds": jnp.clip(1.0 * jax.random.uniform(key_of[2], (ROWS, C_IN), jnp.float32) ** block_levels(key_of[2], (ROWS, C_IN), ((0, 32),), -0.2, 0.2), 0.0, 1.0).astype(jnp.bfloat16),
        "cotangent": scatter_about(key_of[3], (ROWS, OUT_W), 1.0, 6.0, ((0, 32),)),
        "image_count": draw_image_count(jax.random.fold_in(key_of[22], 71), 0),
        "crop_count": draw_crop_count(jax.random.fold_in(key_of[22], 71), 0),
        "reduce_weight": scatter_about(key_of[6], (C_IN, C_MID), C_IN ** -0.5, 0.125, ((0, 8),), jnp.float32),
        "spatial_weight": scatter_about(key_of[7], (9 * C_MID, C_MID), (9 * C_MID) ** -0.5, 0.09375, ((0, 8),), jnp.float32),
        "expand_weight": scatter_about(key_of[8], (C_MID, C_IN), C_MID ** -0.5, 0.25, ((0, 8),), jnp.float32),
        "heads_weight": scatter_about(key_of[9], (C_IN, OUT_W), C_IN ** -0.5, 0.125, ((0, 8),), jnp.float32),
        "norm_gains": draw_norm_gains(jax.random.fold_in(key_of[22], 71), 0),
        "norm_shifts": scatter_about(key_of[11], (NORM_W,), 0.5, 3.0, ((0, 8),), jnp.float32),
        "first_reduce": scatter_about(key_of[12], (C_IN, C_MID), (0.055 * NPARAM ** -0.5), 0.00036621094, ((0, 8),), jnp.float32),
        "first_spatial": scatter_about(key_of[13], (9 * C_MID, C_MID), (0.055 * NPARAM ** -0.5), 0.00036621094, ((0, 8),), jnp.float32),
        "first_expand": scatter_about(key_of[14], (C_MID, C_IN), (0.055 * NPARAM ** -0.5), 0.00036621094, ((0, 8),), jnp.float32),
        "first_heads": scatter_about(key_of[15], (C_IN, OUT_W), (0.25 * NPARAM ** -0.5), 0.0017089844, ((0, 8),), jnp.float32),
        "first_norm": scatter_about(key_of[16], (2, NORM_W), (0.055 * NPARAM ** -0.5), 0.00036621094, ((1, 8),), jnp.float32),
        "second_reduce": jnp.clip(jnp.exp(math.log(1.9051160649041776e-10) - 1.3862944 * jax.random.uniform(key_of[17], (C_IN, C_MID), jnp.float32) ** block_levels(key_of[17], (C_IN, C_MID), ((0, 8),), -0.2, 0.2)), 4.762790162260444e-11, 1.9051160649041776e-10),
        "second_spatial": jnp.clip(jnp.exp(math.log(1.9051160649041776e-10) - 1.3862944 * jax.random.uniform(key_of[18], (9 * C_MID, C_MID), jnp.float32) ** block_levels(key_of[18], (9 * C_MID, C_MID), ((0, 8),), -0.2, 0.2)), 4.762790162260444e-11, 1.9051160649041776e-10),
        "second_expand": jnp.clip(jnp.exp(math.log(1.9051160649041776e-10) - 1.3862944 * jax.random.uniform(key_of[19], (C_MID, C_IN), jnp.float32) ** block_levels(key_of[19], (C_MID, C_IN), ((0, 8),), -0.2, 0.2)), 4.762790162260444e-11, 1.9051160649041776e-10),
        "second_heads": jnp.clip(jnp.exp(math.log(3.810232129808355e-09) - 1.3862944 * jax.random.uniform(key_of[20], (C_IN, OUT_W), jnp.float32) ** block_levels(key_of[20], (C_IN, OUT_W), ((0, 8),), -0.2, 0.2)), 9.525580324520888e-10, 3.810232129808355e-09),
        "second_norm": jnp.clip(jnp.exp(math.log(1.9051160649041776e-10) - 1.3862944 * jax.random.uniform(key_of[21], (2, NORM_W), jnp.float32) ** block_levels(key_of[21], (2, NORM_W), ((1, 8),), -0.2, 0.2)), 4.762790162260444e-11, 1.9051160649041776e-10),
    }


@jax.custom_vjp
def low(v):
    return lax.optimization_barrier(v.astype(jnp.bfloat16)).astype(jnp.float32)

@jax.custom_vjp
def low_back(v):
    return v

def low_keep(v):
    return (low(v), None)

def low_pass(kept, grad):
    return (grad,)

def back_keep(v):
    return (v, None)

def back_low(kept, grad):
    return (low(grad),)
low.defvjp(low_keep, low_pass)
low_back.defvjp(back_keep, back_low)
norm_eps = 1e-05
soft_scale = 0.05
purity_temper = 0.1
clip_bound = 1.0
first_decay = 0.9
second_decay = 0.999
adam_eps = 1e-08
weight_rate = 0.02
norm_rate = 0.5
weight_decay = 0.1

def exact_dot(left, right):
    return jnp.dot(left, right, precision=lax.Precision.HIGHEST, preferred_element_type=jnp.float32)

def live_rows(image_count, crop_count):
    image_flags = jnp.arange(IMG_CAP * SIDE * SIDE) < image_count * (SIDE * SIDE)
    crop_flags = jnp.arange(CROP_CAP * CROP_SIDE * CROP_SIDE) < crop_count * (CROP_SIDE * CROP_SIDE)
    return jnp.concatenate([image_flags, crop_flags]).astype(jnp.float32)[:, None]

def unfold_grid(grid):
    slot_count, grid_height, grid_width, channels = grid.shape
    padded = jnp.pad(grid, ((0, 0), (1, 1), (1, 1), (0, 0)))
    pieces = [padded[:, offset_y:offset_y + grid_height, offset_x:offset_x + grid_width, :] for offset_y in range(3) for offset_x in range(3)]
    return jnp.concatenate(pieces, axis=-1).reshape(slot_count * grid_height * grid_width, 9 * channels)

def unfold_rows(hidden):
    image_rows = IMG_CAP * SIDE * SIDE
    channels = hidden.shape[-1]
    image_part = hidden[:image_rows].reshape(IMG_CAP, SIDE, SIDE, channels)
    crop_part = hidden[image_rows:].reshape(CROP_CAP, CROP_SIDE, CROP_SIDE, channels)
    return jnp.concatenate([unfold_grid(image_part), unfold_grid(crop_part)], axis=0)

def soft_drop(task_grads, thresh):
    together = task_grads[0]
    magnitude = jnp.sqrt(task_grads[0] * task_grads[0] + soft_scale * soft_scale)
    for further in task_grads[1:]:
        together = together + further
        magnitude = magnitude + jnp.sqrt(further * further + soft_scale * soft_scale)
    purity = 0.5 * (1.0 + together / magnitude)
    upward = jax.nn.sigmoid((purity - thresh) / purity_temper)
    combined = jnp.zeros_like(together)
    for grad_part in task_grads:
        keeping = upward * jax.nn.sigmoid(grad_part / soft_scale) + (1.0 - upward) * jax.nn.sigmoid(-grad_part / soft_scale)
        combined = combined + grad_part * keeping
    return combined

def adamw_step(weights, gradient, moment, square, step_rate, decay_rate):
    moment_new = first_decay * moment + (1.0 - first_decay) * gradient
    square_new = second_decay * square + (1.0 - second_decay) * gradient * gradient
    moment_hat = moment_new / (1.0 - first_decay ** STEP)
    square_hat = square_new / (1.0 - second_decay ** STEP)
    updated = weights - step_rate * (moment_hat / (jnp.sqrt(square_hat) + adam_eps) + decay_rate * weights)
    return (updated, moment_new, square_new)

def mapped_dot(weight_low, block_rows):
    return exact_dot(block_rows, weight_low)

def mapped_conv(weight_low, block_rows):
    return exact_dot(unfold_rows(block_rows), weight_low)

def reference(images, crop_pixels, thresholds, cotangent, image_count, crop_count, reduce_weight, spatial_weight, expand_weight, heads_weight, norm_gains, norm_shifts, first_reduce, first_spatial, first_expand, first_heads, first_norm, second_reduce, second_spatial, second_expand, second_heads, second_norm):
    image_rows = IMG_CAP * SIDE * SIDE
    inputs = jnp.concatenate([images.astype(jnp.float32).reshape(DEVICES, image_rows, C_IN), crop_pixels.astype(jnp.float32).reshape(DEVICES, CROP_CAP * CROP_SIDE * CROP_SIDE, C_IN)], axis=1)
    live_mask = jax.vmap(live_rows)(image_count, crop_count)
    total_live = jnp.sum(live_mask)

    def batch_norm(values, gain_part, shift_part):
        centre = lax.optimization_barrier(jnp.sum(values * live_mask, axis=(0, 1))) / total_live
        spread = lax.optimization_barrier(jnp.sum(jnp.square((values - centre) * live_mask), axis=(0, 1))) / total_live
        return (values - centre) * lax.rsqrt(spread + norm_eps) * gain_part + shift_part

    def tail_part(third_act, rows_in, gain_part, shift_part):
        return jax.nn.silu(batch_norm(third_act, gain_part, shift_part) + rows_in)

    def trunk_pass(rows_in, reduce_full, spatial_full, expand_full, gain_full, shift_full):
        reduce_low = low(reduce_full)
        spatial_low = low(spatial_full)
        expand_low = low(expand_full)
        gain_low = low(gain_full)
        shift_low = low(shift_full)
        first_act = low_back(lax.map(partial(jax.checkpoint(mapped_dot), reduce_low), rows_in))
        first_hidden = low(jax.nn.silu(batch_norm(first_act, gain_low[:C_MID], shift_low[:C_MID])))
        second_act = low_back(lax.map(partial(jax.checkpoint(mapped_conv), spatial_low), first_hidden))
        second_hidden = low(jax.nn.silu(batch_norm(second_act, gain_low[C_MID:2 * C_MID], shift_low[C_MID:2 * C_MID])))
        third_act = low_back(lax.map(partial(jax.checkpoint(mapped_dot), expand_low), second_hidden))
        return jax.checkpoint(tail_part)(third_act, rows_in, gain_low[2 * C_MID:], shift_low[2 * C_MID:])
    trunk_out, trunk_pull = jax.vjp(trunk_pass, inputs, reduce_weight, spatial_weight, expand_weight, norm_gains, norm_shifts)
    heads_low = low(heads_weight)
    task_of = jnp.arange(TASKS * HEAD) // HEAD

    def head_fn(rows_in, weight_low):
        return exact_dot(low(rows_in), weight_low)

    def head_step(weight_grad, packed):
        trunk_rows, cot_rows, thresh_rows, mask_rows = packed
        outputs, head_pull = jax.vjp(head_fn, trunk_rows, heads_low)
        cot_live = cot_rows.astype(jnp.float32) * mask_rows
        task_grads = []
        for task_index in range(TASKS):
            grad_rows, grad_weight = head_pull(cot_live * (task_of == task_index).astype(jnp.float32))
            task_grads.append(grad_rows)
            weight_grad = weight_grad + grad_weight
        combined = soft_drop(task_grads, thresh_rows.astype(jnp.float32))
        return (weight_grad, ((outputs * mask_rows).astype(jnp.bfloat16), combined))
    grad_heads, (predictions, combined) = lax.scan(head_step, jnp.zeros((C_IN, TASKS * HEAD), jnp.float32), (trunk_out, cotangent.reshape(DEVICES, ROWS_DEV, TASKS * HEAD), thresholds.reshape(DEVICES, ROWS_DEV, C_IN), live_mask))
    grad_inputs, grad_reduce, grad_spatial, grad_expand, grad_gains, grad_shifts = trunk_pull(combined)
    grad_norm_params = jnp.stack([grad_gains, grad_shifts])
    squares = jnp.zeros((), jnp.float32)
    for grad_item in (grad_reduce, grad_spatial, grad_expand, grad_heads, grad_norm_params):
        squares = squares + jnp.sum(jnp.square(grad_item))
    norm_before = jnp.sqrt(squares)
    factor = clip_bound / jnp.maximum(norm_before, clip_bound)
    new_reduce, moment_reduce, square_reduce = adamw_step(reduce_weight, grad_reduce * factor, first_reduce, second_reduce, weight_rate, weight_decay)
    new_spatial, moment_spatial, square_spatial = adamw_step(spatial_weight, grad_spatial * factor, first_spatial, second_spatial, weight_rate, weight_decay)
    new_expand, moment_expand, square_expand = adamw_step(expand_weight, grad_expand * factor, first_expand, second_expand, weight_rate, weight_decay)
    new_heads, moment_heads, square_heads = adamw_step(heads_weight, grad_heads * factor, first_heads, second_heads, weight_rate, weight_decay)
    new_norm, moment_norm, square_norm = adamw_step(jnp.stack([norm_gains, norm_shifts]), grad_norm_params * factor, first_norm, second_norm, norm_rate, 0.0)
    grad_images = grad_inputs[:, :image_rows].reshape(IMAGES, SIDE, SIDE, C_IN).astype(jnp.bfloat16)
    grad_crops = grad_inputs[:, image_rows:].reshape(CROPS, CROP_SIDE, CROP_SIDE, C_IN).astype(jnp.bfloat16)
    return (norm_before, predictions.reshape(-1, TASKS * HEAD), grad_images, grad_crops, new_reduce, new_spatial, new_expand, new_heads, new_norm, moment_reduce, moment_spatial, moment_expand, moment_heads, moment_norm, square_reduce, square_spatial, square_expand, square_heads, square_norm)
```

```python
import functools

import jax
import jax.numpy as jnp
from jax import lax
from jax.sharding import PartitionSpec as P

C_IN = 2048
C_MID = 512
HEAD = 128
TASKS = 3
SIDE = 7
CROP_SIDE = 2
STEP = 10
IMG_CAP = 24
CROP_CAP = 16


norm_eps = 1e-05
soft_scale = 0.05
purity_temper = 0.1
clip_bound = 1.0
first_decay = 0.9
second_decay = 0.999
adam_eps = 1e-08
weight_rate = 0.02
norm_rate = 0.5
weight_decay = 0.1


def silu_slope(values):
    sigma = jax.nn.sigmoid(values)
    return sigma * (1.0 + values * (1.0 - sigma))


def soft_drop(task_grads, thresh):
    together = task_grads[0]
    magnitude = jnp.sqrt(task_grads[0] * task_grads[0] + soft_scale * soft_scale)
    for further in task_grads[1:]:
        together = together + further
        magnitude = magnitude + jnp.sqrt(further * further + soft_scale * soft_scale)
    purity = 0.5 * (1.0 + together / magnitude)
    upward = jax.nn.sigmoid((purity - thresh) / purity_temper)
    combined = jnp.zeros_like(together)
    for grad_part in task_grads:
        keeping = upward * jax.nn.sigmoid(grad_part / soft_scale) + (1.0 - upward) * jax.nn.sigmoid(
            -grad_part / soft_scale
        )
        combined = combined + grad_part * keeping
    return combined


def adamw_step(weights, gradient, moment, square, step_rate, decay_rate):
    moment_new = first_decay * moment + (1.0 - first_decay) * gradient
    square_new = second_decay * square + (1.0 - second_decay) * gradient * gradient
    moment_hat = moment_new / (1.0 - first_decay**STEP)
    square_hat = square_new / (1.0 - second_decay**STEP)
    updated = weights - step_rate * (
        moment_hat / (jnp.sqrt(square_hat) + adam_eps) + decay_rate * weights
    )
    return (updated, moment_new, square_new)


BOTH = ("dp", "wide")


def bits_of(size):
    return [1 << k for k in range(size.bit_length() - 1)]


def swap_dp(sizes, values, mask):
    return lax.ppermute(values, "dp", [(i, i ^ mask) for i in range(sizes[0])])


def swap_wide(sizes, values, mask):
    return lax.ppermute(values, "wide", [(i, i ^ mask) for i in range(sizes[1])])


def rounds_of(size):
    left = bits_of(size)[::-1]
    rounds = []
    while left:
        pair, left = left[:2], left[2:]
        rounds.append((pair[1], pair[0], pair[0] | pair[1]) if len(pair) == 2 else (pair[0],))
    return rounds


def all_rounds(sizes):
    return [(swap_wide, masks) for masks in rounds_of(sizes[1])] + [
        (swap_dp, masks) for masks in rounds_of(sizes[0])
    ]


def sum_rounds(sizes, values, rounds):
    for swap, masks in rounds:
        got = [swap(sizes, values, mask) for mask in masks]
        if len(masks) == 3:
            values = (values + got[0]) + (got[1] + got[2])
        else:
            values = values + got[0]
    return values


def sum_all(sizes, values):
    return sum_rounds(sizes, values, all_rounds(sizes))


def pool(first, second):
    count_a, total_a, spread_a = first
    count_b, total_b, spread_b = second
    count = count_a + count_b
    apart = total_a / count_a - total_b / count_b
    weight = count_a * count_b / count
    return (count, total_a + total_b, (spread_a + spread_b) + (apart * apart) * weight)


def pool_all(sizes, own, counts):
    seen = []
    count, total, spread = own
    for level, (swap, masks) in enumerate(all_rounds(sizes)):
        if counts is None:
            packet = jnp.stack([total, spread, jnp.broadcast_to(count, total.shape)])
            got = [swap(sizes, packet, mask) for mask in masks]
            seen.append((count, [g[2, 0] for g in got]))
        else:
            packet = jnp.stack([total, spread])
            got = [swap(sizes, packet, mask) for mask in masks]
            seen.append(counts[level])
        sets = [(seen[-1][0], total, spread)] + [
            (c, g[0], g[1]) for c, g in zip(seen[-1][1], got)
        ]
        if len(sets) == 4:
            sets = [pool(sets[0], sets[1]), pool(sets[2], sets[3])]
        count, total, spread = pool(sets[0], sets[1])
    return (count, total, spread, seen)


def batch_norm(sizes, values, live_mask, live_count, counts):
    total = jnp.sum(values * live_mask, axis=0)
    deviation = (values - total / live_count) * live_mask
    spread = jnp.sum(deviation * deviation, axis=0)
    counted, total, spread, counts = pool_all(sizes, (live_count, total, spread), counts)
    inv_std = lax.rsqrt(spread / counted + norm_eps)
    return ((values - total / counted) * inv_std, inv_std, counted, counts)


def norm_back(sizes, upstream, normed, gain_part, inv_std, live_mask, counted):
    sums = sum_all(
        sizes, jnp.stack([jnp.sum(upstream * normed, axis=0), jnp.sum(upstream, axis=0)])
    )
    grad_gain, grad_shift = sums[0], sums[1]
    grad_act = (
        live_mask * gain_part * inv_std * (upstream - (grad_shift + normed * grad_gain) / counted)
    )
    return (grad_act.astype(jnp.bfloat16), grad_gain, grad_shift)


def orders(size):
    down = bits_of(size)[::-1]
    return (down, [1] + [bit for bit in down if bit != 1])


def crossing(sizes, step):
    pair = orders(sizes[1])
    return [
        (dp * sizes[1] + place, dp * sizes[1] + (place ^ pair[dp & 1][step]))
        for dp in range(sizes[0])
        for place in range(sizes[1])
    ]


def slot_of(sizes, core, apart):
    shifts = [[bit.bit_length() - 1 for bit in order] for order in orders(sizes[1])]
    index = 0
    for k in range(len(shifts[0])):
        shift = jnp.where(core == 0, shifts[0][k], shifts[1][k])
        index = index + (((apart >> shift) & 1) << k)
    return index


def apart_of(sizes, core, slot):
    masks = []
    for order in orders(sizes[1]):
        mask = 0
        for k, bit in enumerate(order):
            if slot >> k & 1:
                mask ^= bit
        masks.append(mask)
    return jnp.where(core == 0, masks[0], masks[1])


def pick(blocks, index):
    return lax.dynamic_index_in_dim(blocks, index, 0, keepdims=True)


def gather_ring(sizes, shard):
    core, place = lax.axis_index("dp") & 1, lax.axis_index("wide")
    halves = shard.reshape(2, shard.shape[0] // 2, shard.shape[1])
    held = pick(halves, core)
    for step in range(len(bits_of(sizes[1]))):
        got = lax.ppermute(held, BOTH, crossing(sizes, step))
        held = jnp.concatenate([held, got], axis=0)
    other = swap_dp(sizes, held, 1)
    both = jnp.concatenate([held, other], axis=0)
    parts = []
    for target in range(sizes[1]):
        for half in range(2):
            slot = slot_of(sizes, half, place ^ target)
            parts.append(pick(both, slot + jnp.where(core == half, 0, sizes[1])))
    return jnp.concatenate(parts, axis=0).reshape((sizes[1],) + shard.shape)


def gather_wide(sizes, shard):
    core = lax.axis_index("dp") & 1
    halves = shard.reshape(2, shard.shape[0] // 2, shard.shape[1])
    held = lax.all_gather(pick(halves, core), "wide", axis=0, tiled=True)
    other = swap_dp(sizes, held, 1)
    low = jnp.where(core == 0, held, other)
    high = jnp.where(core == 0, other, held)
    return jnp.stack([low, high], axis=1).reshape((sizes[1],) + shard.shape)


def finish_sum(sizes, held):
    core = lax.axis_index("dp") & 1
    for bit in bits_of(sizes[0])[1:]:
        low = held.astype(jnp.bfloat16)
        held = low.astype(jnp.float32) + swap_dp(sizes, low, bit).astype(jnp.float32)
    other = swap_dp(sizes, held, 1)
    return jnp.where(
        core == 0,
        jnp.concatenate([held, other], axis=0),
        jnp.concatenate([other, held], axis=0),
    )


def scatter_ring(sizes, grads):
    core, place = lax.axis_index("dp") & 1, lax.axis_index("wide")
    count, rows, width = grads.shape
    blocks = grads.reshape(count * 2, rows // 2, width)
    mine = [pick(blocks, (place ^ apart_of(sizes, core, j)) * 2 + core) for j in range(count)]
    theirs = [
        pick(blocks, (place ^ apart_of(sizes, 1 - core, j)) * 2 + 1 - core) for j in range(count)
    ]
    sent = jnp.concatenate(theirs, axis=0).astype(jnp.bfloat16)
    held = jnp.concatenate(mine, axis=0) + swap_dp(sizes, sent, 1).astype(jnp.float32)
    for step in reversed(range(len(bits_of(sizes[1])))):
        half = held.shape[0] // 2
        got = lax.ppermute(held[half:].astype(jnp.bfloat16), BOTH, crossing(sizes, step))
        held = held[:half] + got.astype(jnp.float32)
    return finish_sum(sizes, held[0])


def scatter_wide(sizes, grads):
    core = lax.axis_index("dp") & 1
    count, rows, width = grads.shape
    halves = grads.reshape(count, 2, rows // 2, width)
    sent = lax.dynamic_index_in_dim(halves, 1 - core, 1, keepdims=False).astype(jnp.bfloat16)
    kept = lax.dynamic_index_in_dim(halves, core, 1, keepdims=False)
    held = (kept + swap_dp(sizes, sent, 1).astype(jnp.float32)).astype(jnp.bfloat16)
    shard = lax.psum_scatter(held, "wide", scatter_dimension=0, tiled=True)
    return finish_sum(sizes, shard[0].astype(jnp.float32))


def side_by_side(expand, heads):
    count, rows, _ = expand.shape
    four = jnp.concatenate(
        [expand[:, :, part * C_MID : (part + 1) * C_MID] for part in range(4)], axis=1
    )
    return jnp.concatenate([four, heads], axis=2)


def apart_again(both, rows):
    four, heads = both[:, :, :C_MID], both[:, :, C_MID:]
    expand = jnp.concatenate(
        [four[:, part * rows : (part + 1) * rows] for part in range(4)], axis=2
    )
    return (expand, heads)


def pixel_order(rows, slots, pixels):
    return rows.reshape(slots, pixels, -1).transpose(1, 0, 2).reshape(slots * pixels, -1)


def slot_order(rows, slots, pixels):
    return rows.reshape(pixels, slots, -1).transpose(1, 0, 2).reshape(slots * pixels, -1)


def both_kinds(order, rows, image_slots, crop_slots):
    cut = image_slots * SIDE * SIDE
    return jnp.concatenate(
        [
            order(rows[:cut], image_slots, SIDE * SIDE),
            order(rows[cut:], crop_slots, CROP_SIDE * CROP_SIDE),
        ],
        axis=0,
    )


def neighbours(rows, image_slots, crop_slots):
    width = rows.shape[1]
    cut = image_slots * SIDE * SIDE
    images = jnp.pad(
        rows[:cut].reshape(SIDE, SIDE, image_slots, width), ((1, 1), (1, 1), (0, 0), (0, 0))
    )
    crops = jnp.pad(
        rows[cut:].reshape(CROP_SIDE, CROP_SIDE, crop_slots, width),
        ((1, 1), (1, 1), (0, 0), (0, 0)),
    )
    return [
        jnp.concatenate(
            [
                images[oy : oy + SIDE, ox : ox + SIDE].reshape(-1, width),
                crops[oy : oy + CROP_SIDE, ox : ox + CROP_SIDE].reshape(-1, width),
            ],
            axis=0,
        )
        for oy in range(3)
        for ox in range(3)
    ]


def soft_drop(task_grads, thresh):
    together = task_grads[0]
    magnitude = jnp.sqrt(task_grads[0] * task_grads[0] + soft_scale * soft_scale)
    for further in task_grads[1:]:
        together = together + further
        magnitude = magnitude + jnp.sqrt(further * further + soft_scale * soft_scale)
    purity = 0.5 * (1.0 + together / magnitude)
    upward = jax.nn.sigmoid((purity - thresh) / purity_temper)
    combined = jnp.zeros_like(together)
    for grad_part in task_grads:
        keeping = jax.nn.sigmoid(grad_part / soft_scale)
        combined = combined + grad_part * (upward * keeping + (1.0 - upward) * (1.0 - keeping))
    return combined


def local(
    sizes,
    images,
    crop_pixels,
    thresholds,
    cotangent,
    image_count,
    crop_count,
    reduce_weight,
    spatial_weight,
    expand_weight,
    heads_weight,
    norm_gains,
    norm_shifts,
    first_reduce,
    first_spatial,
    first_expand,
    first_heads,
    first_norm,
    second_reduce,
    second_spatial,
    second_expand,
    second_heads,
    second_norm,
):
    low = jnp.bfloat16
    image_slots, crop_slots = images.shape[0], crop_pixels.shape[0]
    image_rows = image_slots * SIDE * SIDE
    places = sizes[1]
    slot_rows = functools.partial(
        both_kinds, slot_order, image_slots=image_slots, crop_slots=crop_slots
    )
    pixel_rows = functools.partial(
        both_kinds, pixel_order, image_slots=image_slots, crop_slots=crop_slots
    )

    reduce_rows, norm_width = reduce_weight.shape[0], norm_gains.shape[0]
    norms = jnp.pad(
        jnp.stack([norm_gains, norm_shifts]).astype(low), ((0, 14), (0, C_MID - norm_width))
    )
    first_blocks = gather_ring(
        sizes, jnp.concatenate([reduce_weight.astype(low), norms], axis=0)
    )
    reduce_full = first_blocks[:, :reduce_rows].reshape(C_IN, C_MID)
    gain_full = first_blocks[:, reduce_rows, :norm_width].reshape(-1).astype(jnp.float32)
    shift_full = first_blocks[:, reduce_rows + 1, :norm_width].reshape(-1).astype(jnp.float32)
    spatial_full = gather_ring(sizes, spatial_weight.astype(low)).reshape(9 * C_MID, C_MID)
    third_blocks = gather_wide(
        sizes,
        side_by_side(expand_weight.astype(low)[None], heads_weight.astype(low)[None])[0],
    )
    expand_full, heads_full = apart_again(third_blocks, expand_weight.shape[0])
    expand_full = expand_full.reshape(C_MID, C_IN)
    heads_full = heads_full.reshape(C_IN, TASKS * HEAD)

    inputs = jnp.concatenate(
        [
            images.transpose(1, 2, 0, 3).reshape(image_rows, C_IN),
            crop_pixels.transpose(1, 2, 0, 3).reshape(-1, C_IN),
        ],
        axis=0,
    )
    live_mask = jnp.concatenate(
        [
            jnp.tile(jnp.arange(image_slots) < image_count[0], SIDE * SIDE),
            jnp.tile(jnp.arange(crop_slots) < crop_count[0], CROP_SIDE * CROP_SIDE),
        ]
    ).astype(jnp.float32)[:, None]
    live_count = jnp.sum(live_mask)
    thresh = pixel_rows(thresholds).astype(jnp.float32)
    cot_live = pixel_rows(cotangent) * live_mask.astype(low)

    first_act = jnp.dot(inputs, reduce_full, preferred_element_type=jnp.float32)
    normed_one, inv_one, counted, counts = batch_norm(
        sizes, first_act, live_mask, live_count, None
    )
    pre_one = normed_one * gain_full[:C_MID] + shift_full[:C_MID]
    hidden_one = jax.nn.silu(pre_one).astype(low)
    shifted = neighbours(hidden_one, image_slots, crop_slots)
    second_act = jnp.dot(
        jnp.concatenate(shifted, axis=1), spatial_full, preferred_element_type=jnp.float32
    )
    normed_two, inv_two, counted, _ = batch_norm(sizes, second_act, live_mask, live_count, counts)
    pre_two = normed_two * gain_full[C_MID : 2 * C_MID] + shift_full[C_MID : 2 * C_MID]
    hidden_two = jax.nn.silu(pre_two).astype(low)
    task_grads = [
        jnp.dot(
            cot_live[:, task * HEAD : (task + 1) * HEAD],
            heads_full[:, task * HEAD : (task + 1) * HEAD].T,
            preferred_element_type=jnp.float32,
        )
        for task in range(TASKS)
    ]
    combined = soft_drop(task_grads, thresh)
    third_act = jnp.dot(hidden_two, expand_full, preferred_element_type=jnp.float32)
    normed_three, inv_three, counted, _ = batch_norm(
        sizes, third_act, live_mask, live_count, counts
    )
    summed = (
        normed_three * gain_full[2 * C_MID :] + shift_full[2 * C_MID :] + inputs.astype(jnp.float32)
    )
    trunk = jax.nn.silu(summed).astype(low)
    predictions = slot_rows(
        (jnp.dot(trunk, heads_full, preferred_element_type=jnp.float32) * live_mask).astype(low)
    )
    grad_heads = jnp.dot(trunk.T, cot_live, preferred_element_type=jnp.float32)
    upstream = combined * silu_slope(summed)
    grad_three, gain_three, shift_three = norm_back(
        sizes, upstream, normed_three, gain_full[2 * C_MID :], inv_three, live_mask, counted
    )
    grad_expand = jnp.dot(hidden_two.T, grad_three, preferred_element_type=jnp.float32)
    back_two = jnp.dot(grad_three, expand_full.T, preferred_element_type=jnp.float32) * silu_slope(
        pre_two
    )
    grad_two, gain_two, shift_two = norm_back(
        sizes, back_two, normed_two, gain_full[C_MID : 2 * C_MID], inv_two, live_mask, counted
    )
    grad_spatial = jnp.concatenate(
        [jnp.dot(piece.T, grad_two, preferred_element_type=jnp.float32) for piece in shifted],
        axis=0,
    )
    spread = neighbours(grad_two, image_slots, crop_slots)
    back_one = lax.dot_general(
        jnp.stack(spread[::-1], axis=1),
        spatial_full.reshape(9, C_MID, C_MID),
        (((1, 2), (0, 2)), ((), ())),
        preferred_element_type=jnp.float32,
    ) * silu_slope(pre_one)
    grad_one, gain_one, shift_one = norm_back(
        sizes, back_one, normed_one, gain_full[:C_MID], inv_one, live_mask, counted
    )
    grad_reduce = jnp.dot(inputs.T, grad_one, preferred_element_type=jnp.float32)

    shard_third = scatter_wide(
        sizes,
        side_by_side(
            grad_expand.reshape(places, -1, C_IN), grad_heads.reshape(places, -1, TASKS * HEAD)
        ),
    )
    shard_spatial = scatter_ring(sizes, grad_spatial.reshape(places, -1, C_MID))
    shard_reduce = scatter_ring(sizes, grad_reduce.reshape(places, -1, C_MID))
    shard_expand, shard_heads = apart_again(shard_third[None], expand_weight.shape[0])
    shard_expand, shard_heads = shard_expand[0], shard_heads[0]

    back = reduce_full.T
    grad_images = (
        (
            jnp.dot(grad_one[:image_rows], back, preferred_element_type=jnp.float32)
            + upstream[:image_rows]
        )
        .astype(low)
        .reshape(SIDE, SIDE, image_slots, C_IN)
        .transpose(2, 0, 1, 3)
    )
    grad_crops = (
        (
            jnp.dot(grad_one[image_rows:], back, preferred_element_type=jnp.float32)
            + upstream[image_rows:]
        )
        .astype(low)
        .reshape(CROP_SIDE, CROP_SIDE, crop_slots, C_IN)
        .transpose(2, 0, 1, 3)
    )

    norm_grads = jnp.stack(
        [
            jnp.concatenate([gain_one, gain_two, gain_three]),
            jnp.concatenate([shift_one, shift_two, shift_three]),
        ]
    )
    norm_shard = lax.dynamic_slice_in_dim(
        norm_grads, lax.axis_index("wide") * norm_width, norm_width, 1
    )
    local_squares = (
        jnp.sum(jnp.square(shard_reduce))
        + jnp.sum(jnp.square(shard_spatial))
        + jnp.sum(jnp.square(shard_third))
    )
    squares = sum_rounds(
        sizes,
        jnp.broadcast_to(local_squares, (8, 128)),
        [(swap_wide, masks) for masks in rounds_of(sizes[1])],
    )[0, 0] + jnp.sum(jnp.square(norm_grads))
    norm_before = jnp.sqrt(squares)
    factor = clip_bound / jnp.maximum(norm_before, clip_bound)
    new_reduce, moment_reduce, square_reduce = adamw_step(
        reduce_weight, shard_reduce * factor, first_reduce, second_reduce, weight_rate, weight_decay
    )
    new_spatial, moment_spatial, square_spatial = adamw_step(
        spatial_weight,
        shard_spatial * factor,
        first_spatial,
        second_spatial,
        weight_rate,
        weight_decay,
    )
    new_expand, moment_expand, square_expand = adamw_step(
        expand_weight, shard_expand * factor, first_expand, second_expand, weight_rate, weight_decay
    )
    new_heads, moment_heads, square_heads = adamw_step(
        heads_weight, shard_heads * factor, first_heads, second_heads, weight_rate, weight_decay
    )
    new_norm, moment_norm, square_norm = adamw_step(
        jnp.stack([norm_gains, norm_shifts]),
        norm_shard * factor,
        first_norm,
        second_norm,
        norm_rate,
        0.0,
    )
    return (
        norm_before,
        predictions,
        grad_images,
        grad_crops,
        new_reduce,
        new_spatial,
        new_expand,
        new_heads,
        new_norm,
        moment_reduce,
        moment_spatial,
        moment_expand,
        moment_heads,
        moment_norm,
        square_reduce,
        square_spatial,
        square_expand,
        square_heads,
        square_norm,
    )


def solution(mesh):
    sizes = (mesh.shape["dp"], mesh.shape["wide"])
    return jax.shard_map(
        functools.partial(local, sizes),
        mesh=mesh,
        in_specs=(
            P(("dp", "wide"), None, None, None),
            P(("dp", "wide"), None, None, None),
            P(("dp", "wide"), None),
            P(("dp", "wide"), None),
            P(("dp", "wide")),
            P(("dp", "wide")),
            P("wide", None),
            P("wide", None),
            P("wide", None),
            P("wide", None),
            P("wide"),
            P("wide"),
            P("wide", None),
            P("wide", None),
            P("wide", None),
            P("wide", None),
            P(None, "wide"),
            P("wide", None),
            P("wide", None),
            P("wide", None),
            P("wide", None),
            P(None, "wide"),
        ),
        out_specs=(
            P(),
            P(("dp", "wide"), None),
            P(("dp", "wide"), None, None, None),
            P(("dp", "wide"), None, None, None),
            P("wide", None),
            P("wide", None),
            P("wide", None),
            P("wide", None),
            P(None, "wide"),
            P("wide", None),
            P("wide", None),
            P("wide", None),
            P("wide", None),
            P(None, "wide"),
            P("wide", None),
            P("wide", None),
            P("wide", None),
            P("wide", None),
            P(None, "wide"),
        ),
        check_vma=False,
    )
```

```python
import functools

import jax
import jax.numpy as jnp
from jax import lax
from jax.experimental import pallas as pl
from jax.experimental.pallas import tpu as pltpu
from jax.sharding import PartitionSpec as P

C_IN = 2048
C_MID = 512
HEAD = 128
TASKS = 3
SIDE = 7
CROP_SIDE = 2
STEP = 10
IMG_CAP = 24
CROP_CAP = 16


norm_eps = 1e-05
soft_scale = 0.05
purity_temper = 0.1
clip_bound = 1.0
first_decay = 0.9
second_decay = 0.999
adam_eps = 1e-08
weight_rate = 0.02
norm_rate = 0.5
weight_decay = 0.1


def silu_slope(values):
    sigma = jax.nn.sigmoid(values)
    return sigma * (1.0 + values * (1.0 - sigma))


def soft_drop(task_grads, thresh):
    together = task_grads[0]
    magnitude = jnp.sqrt(task_grads[0] * task_grads[0] + soft_scale * soft_scale)
    for further in task_grads[1:]:
        together = together + further
        magnitude = magnitude + jnp.sqrt(further * further + soft_scale * soft_scale)
    purity = 0.5 * (1.0 + together / magnitude)
    upward = jax.nn.sigmoid((purity - thresh) / purity_temper)
    combined = jnp.zeros_like(together)
    for grad_part in task_grads:
        keeping = upward * jax.nn.sigmoid(grad_part / soft_scale) + (1.0 - upward) * jax.nn.sigmoid(
            -grad_part / soft_scale
        )
        combined = combined + grad_part * keeping
    return combined


def adamw_step(weights, gradient, moment, square, step_rate, decay_rate):
    moment_new = first_decay * moment + (1.0 - first_decay) * gradient
    square_new = second_decay * square + (1.0 - second_decay) * gradient * gradient
    moment_hat = moment_new / (1.0 - first_decay**STEP)
    square_hat = square_new / (1.0 - second_decay**STEP)
    updated = weights - step_rate * (
        moment_hat / (jnp.sqrt(square_hat) + adam_eps) + decay_rate * weights
    )
    return (updated, moment_new, square_new)


BOTH = ("dp", "wide")
LANES = 128


def bits_of(size):
    return [1 << k for k in range(size.bit_length() - 1)]


def swap_dp(sizes, values, mask):
    return lax.ppermute(values, "dp", [(i, i ^ mask) for i in range(sizes[0])])


def swap_wide(sizes, values, mask):
    return lax.ppermute(values, "wide", [(i, i ^ mask) for i in range(sizes[1])])


def rounds_of(size):
    left = bits_of(size)[::-1]
    rounds = []
    while left:
        pair, left = left[:2], left[2:]
        rounds.append((pair[1], pair[0], pair[0] | pair[1]) if len(pair) == 2 else (pair[0],))
    return rounds


def all_rounds(sizes):
    return [(swap_dp, masks) for masks in rounds_of(sizes[0])] + [
        (swap_wide, masks) for masks in rounds_of(sizes[1])
    ]


def beside(job, token, got):
    if job is None:
        return got
    return lax.optimization_barrier((got, job(token)))[0]


def after(token, values):
    return lax.optimization_barrier((values, token))[0]


def sum_rounds(sizes, values, rounds, jobs=()):
    for level, (swap, masks) in enumerate(rounds):
        got = [swap(sizes, values, mask) for mask in masks]
        got = beside(jobs[level] if level < len(jobs) else None, values, got)
        if len(masks) == 3:
            values = (values + got[0]) + (got[1] + got[2])
        else:
            values = values + got[0]
    return values


def pool(first, second):
    count_a, total_a, spread_a = first
    count_b, total_b, spread_b = second
    count = count_a + count_b
    apart = total_a / count_a - total_b / count_b
    weight = count_a * count_b / count
    return (count, total_a + total_b, (spread_a + spread_b) + (apart * apart) * weight)


def pool_all(sizes, count, total, spread, counts, jobs):
    seen = []
    total, spread = total.reshape(-1, LANES), spread.reshape(-1, LANES)
    for level, (swap, masks) in enumerate(all_rounds(sizes)):
        parts = [total, spread]
        if counts is None:
            parts.append(jnp.broadcast_to(count, total.shape))
        packet = jnp.stack(parts)
        got = [swap(sizes, packet, mask) for mask in masks]
        got = beside(jobs[level] if level < len(jobs) else None, packet, got)
        seen.append((count, [g[2, :1] for g in got]) if counts is None else counts[level])
        sets = [(seen[-1][0], total, spread)] + [
            (c, g[0], g[1]) for c, g in zip(seen[-1][1], got)
        ]
        if len(sets) == 4:
            sets = [pool(sets[0], sets[1]), pool(sets[2], sets[3])]
        count, total, spread = pool(sets[0], sets[1])
    return (count, total, spread, seen)


def batch_norm(sizes, values, live_mask, live_count, counts, jobs=()):
    width = values.shape[1]
    total = jnp.sum(values * live_mask, axis=0)
    own_mean = (total.reshape(-1, LANES) / live_count).reshape(width)
    deviation = (values - own_mean) * live_mask
    spread = jnp.sum(deviation * deviation, axis=0)
    counted, total, spread, counts = pool_all(sizes, live_count, total, spread, counts, jobs)
    inv_std = lax.rsqrt(spread / counted + norm_eps).reshape(width)
    centre = (total / counted).reshape(width)
    return ((values - centre) * inv_std, inv_std, counted, counts)


def norm_back(sizes, upstream, normed, gain_part, inv_std, live_mask, counted, jobs=()):
    width = upstream.shape[1]
    sums = sum_rounds(
        sizes,
        jnp.stack(
            [
                jnp.sum(upstream * normed, axis=0).reshape(-1, LANES),
                jnp.sum(upstream, axis=0).reshape(-1, LANES),
            ]
        ),
        all_rounds(sizes),
        jobs,
    )
    mean_gain = (sums[0] / counted).reshape(width)
    mean_shift = (sums[1] / counted).reshape(width)
    grad_act = live_mask * (gain_part * inv_std) * (upstream - (mean_shift + normed * mean_gain))
    return (grad_act.astype(jnp.bfloat16), sums[0].reshape(width), sums[1].reshape(width))


def orders(size):
    down = bits_of(size)[::-1]
    return (down, down[:-2] + down[:-3:-1])


def crossing(sizes, step):
    pair = orders(sizes[1])
    return [
        (dp * sizes[1] + place, dp * sizes[1] + (place ^ pair[dp & 1][step]))
        for dp in range(sizes[0])
        for place in range(sizes[1])
    ]


def apart_of(sizes, core, slot):
    masks = []
    for order in orders(sizes[1]):
        mask = 0
        for k, bit in enumerate(order):
            if slot >> k & 1:
                mask ^= bit
        masks.append(mask)
    return jnp.where(core == 0, masks[0], masks[1])


def pick(blocks, index):
    return lax.dynamic_index_in_dim(blocks, index, 0, keepdims=True)


def settle_kernel(sizes, starts, *refs):
    outs, pieces = refs[-len(starts) :], refs[: -len(starts)]
    core, place = lax.axis_index("dp") & 1, lax.axis_index("wide")
    per_core = len(pieces) // 2
    for part, piece in enumerate(pieces):
        half = core if part < per_core else 1 - core
        for block in range(piece.shape[0]):
            slot = block + (part % per_core) * piece.shape[0]
            target = (place ^ apart_of(sizes, half, slot)) * 2 + half
            for start, out in zip(starts, outs):
                out[target] = piece[block, start : start + out.shape[1]]


def settle(sizes, pieces, heights):
    width = pieces[0].shape[2]
    count = 2 * sizes[1]
    starts = [sum(heights[:k]) for k in range(len(heights))]
    return pl.pallas_call(
        functools.partial(settle_kernel, sizes, starts),
        in_specs=[pl.BlockSpec(memory_space=pltpu.VMEM)] * len(pieces),
        out_specs=[pl.BlockSpec(memory_space=pltpu.VMEM)] * len(heights),
        out_shape=[
            jax.ShapeDtypeStruct((count, height, width), pieces[0].dtype) for height in heights
        ],
        compiler_params=pltpu.CompilerParams(vmem_limit_bytes=12 * 2**20),
        cost_estimate=pl.CostEstimate(
            flops=0, bytes_accessed=4 * count * sum(heights) * width, transcendentals=0
        ),
    )(*pieces)


def halves_of(shard):
    return shard.reshape(2, shard.shape[0] // 2, shard.shape[1])


def ring_own(shards):
    return pick(jnp.concatenate(shards, axis=1), lax.axis_index("dp") & 1)


def ring_step(sizes, held, step):
    return lax.ppermute(held, BOTH, crossing(sizes, step))


def ring_end(sizes, held, got, heights):
    pieces = [held, got]
    pieces += [swap_dp(sizes, piece, 1) for piece in pieces]
    return settle(sizes, pieces, heights)


def gather_wide(sizes, shard):
    core = lax.axis_index("dp") & 1
    halves = shard.reshape(2, shard.shape[0] // 2, shard.shape[1])
    held = lax.all_gather(pick(halves, core), "wide", axis=0, tiled=True)
    other = swap_dp(sizes, held, 1)
    low = jnp.where(core == 0, held, other)
    high = jnp.where(core == 0, other, held)
    return jnp.stack([low, high], axis=1).reshape((sizes[1],) + shard.shape)


def finish_sum(sizes, held):
    core = lax.axis_index("dp") & 1
    for bit in bits_of(sizes[0])[1:]:
        low = held.astype(jnp.bfloat16)
        held = low.astype(jnp.float32) + swap_dp(sizes, low, bit).astype(jnp.float32)
    other = swap_dp(sizes, held, 1)
    return jnp.where(
        core == 0,
        jnp.concatenate([held, other], axis=0),
        jnp.concatenate([other, held], axis=0),
    )


def scatter_start(sizes, grads):
    core, place = lax.axis_index("dp") & 1, lax.axis_index("wide")
    count, rows, width = grads.shape
    blocks = grads.reshape(count * 2, rows // 2, width)

    def block(half, slot):
        return pick(blocks, (place ^ apart_of(sizes, half, slot)) * 2 + half)

    sent = jnp.concatenate([block(1 - core, slot) for slot in range(count)], axis=0)
    return (functools.partial(block, core), sent.astype(jnp.bfloat16))


def scatter_own(sizes, block, got):
    return [
        block(slot) + got[slot : slot + 1].astype(jnp.float32) for slot in range(sizes[1])
    ]


def scatter_sent(held):
    return jnp.concatenate(held[len(held) // 2 :], axis=0).astype(jnp.bfloat16)


def scatter_kept(held, got):
    return [
        held[slot] + got[slot : slot + 1].astype(jnp.float32) for slot in range(len(held) // 2)
    ]


class Scatter:
    def __init__(self, sizes, grads):
        self.sizes, self.step = sizes, len(bits_of(sizes[1]))
        self.block, self.sent = scatter_start(sizes, grads)
        self.got = swap_dp(sizes, self.sent, 1)
        self.held = None

    def go(self, token=None):
        got = self.got if token is None else after(token, self.got)
        if self.held is None:
            self.held = scatter_own(self.sizes, self.block, got)
        else:
            self.held = scatter_kept(self.held, got)
        self.step -= 1
        self.sent = scatter_sent(self.held)
        self.got = ring_step(self.sizes, self.sent, self.step)
        return self.sent

    def end(self):
        while self.step:
            self.go()
        return finish_sum(self.sizes, scatter_kept(self.held, self.got)[0][0])


def side_by_side(expand, heads):
    count, rows, _ = expand.shape
    four = jnp.concatenate(
        [expand[:, :, part * C_MID : (part + 1) * C_MID] for part in range(4)], axis=1
    )
    return jnp.concatenate([four, heads], axis=2)


def apart_again(both, rows):
    four, heads = both[:, :, :C_MID], both[:, :, C_MID:]
    expand = jnp.concatenate(
        [four[:, part * rows : (part + 1) * rows] for part in range(4)], axis=2
    )
    return (expand, heads)


def neighbours(rows, image_slots, crop_slots):
    width = rows.shape[1]
    cut = image_slots * SIDE * SIDE
    images = jnp.pad(
        rows[:cut].reshape(SIDE, SIDE, image_slots, width), ((1, 1), (1, 1), (0, 0), (0, 0))
    )
    crops = jnp.pad(
        rows[cut:].reshape(CROP_SIDE, CROP_SIDE, crop_slots, width),
        ((1, 1), (1, 1), (0, 0), (0, 0)),
    )
    return [
        jnp.concatenate(
            [
                images[oy : oy + SIDE, ox : ox + SIDE].reshape(-1, width),
                crops[oy : oy + CROP_SIDE, ox : ox + CROP_SIDE].reshape(-1, width),
            ],
            axis=0,
        )
        for oy in range(3)
        for ox in range(3)
    ]


def drop_kernel(cot_ref, heads_ref, thresh_ref, *rest):
    out_ref = rest[-1]
    half_scale, half_temper = 0.5 / soft_scale, 0.5 / purity_temper
    together, magnitude, leaning = 0.0, 0.0, 0.0
    for task in range(TASKS):
        columns = slice(task * HEAD, (task + 1) * HEAD)
        part = lax.dot_general(
            cot_ref[:, columns],
            heads_ref[:, columns],
            (((1,), (1,)), ((), ())),
            preferred_element_type=jnp.float32,
        )
        square = part * part + soft_scale * soft_scale
        together = together + part
        magnitude = magnitude + square * lax.rsqrt(square)
        leaning = leaning + part * jnp.tanh(part * half_scale)
    lean = (
        thresh_ref[...].astype(jnp.float32) * -half_temper
        + 0.5 * half_temper
        + (together * (0.5 * half_temper)) / magnitude
    )
    out_ref[...] = 0.5 * (together + jnp.tanh(lean) * leaning)


DROP_TILE = 256


def soft_drop(cot_live, heads_full, thresh, first, count, into=None):
    rows, width = thresh.shape
    more = [] if into is None else [into]
    return pl.pallas_call(
        drop_kernel,
        grid=(count,),
        in_specs=[
            pl.BlockSpec((rows, TASKS * HEAD), lambda i: (0, 0)),
            pl.BlockSpec((DROP_TILE, TASKS * HEAD), lambda i: (first + i, 0)),
            pl.BlockSpec((rows, DROP_TILE), lambda i: (0, first + i)),
        ]
        + [pl.BlockSpec(memory_space=pl.ANY)] * len(more),
        out_specs=pl.BlockSpec((rows, DROP_TILE), lambda i: (0, first + i)),
        out_shape=jax.ShapeDtypeStruct((rows, width), jnp.float32),
        input_output_aliases={3: 0} if more else {},
        compiler_params=pltpu.CompilerParams(vmem_limit_bytes=18 * 2**20),
        cost_estimate=pl.CostEstimate(
            flops=2 * rows * count * DROP_TILE * TASKS * HEAD,
            bytes_accessed=6 * rows * count * DROP_TILE,
            transcendentals=8 * rows * count * DROP_TILE,
        ),
    )(cot_live, heads_full, thresh, *more)


def slot_source(image_slots, crop_slots):
    def part(slots, pixels, start):
        return (jnp.arange(slots)[None, :] * pixels + jnp.arange(pixels)[:, None]).reshape(-1) + start

    images = image_slots * SIDE * SIDE
    return jnp.concatenate(
        [part(image_slots, SIDE * SIDE, 0), part(crop_slots, CROP_SIDE * CROP_SIDE, images)]
    )


def local(
    sizes,
    images,
    crop_pixels,
    thresholds,
    cotangent,
    image_count,
    crop_count,
    reduce_weight,
    spatial_weight,
    expand_weight,
    heads_weight,
    norm_gains,
    norm_shifts,
    first_reduce,
    first_spatial,
    first_expand,
    first_heads,
    first_norm,
    second_reduce,
    second_spatial,
    second_expand,
    second_heads,
    second_norm,
):
    low = jnp.bfloat16
    image_slots, crop_slots = images.shape[0], crop_pixels.shape[0]
    image_rows = image_slots * SIDE * SIDE
    rows = image_rows + crop_slots * CROP_SIDE * CROP_SIDE
    places = sizes[1]
    reorder = (
        slot_source(image_slots, crop_slots)[:, None] == jnp.arange(rows)[None, :]
    ).astype(low)

    norm_width = norm_gains.shape[0]
    norms = jnp.pad(
        jnp.stack([norm_gains, norm_shifts]).astype(low)[:, None],
        ((0, 0), (0, 15), (0, C_MID - norm_width)),
    )
    third_own = side_by_side(expand_weight.astype(low)[None], heads_weight.astype(low)[None])[0]
    first_shards = [halves_of(reduce_weight.astype(low)), norms]
    first_held = ring_own(first_shards)
    second_held = ring_own([halves_of(spatial_weight.astype(low))])

    live_mask = jnp.concatenate(
        [
            jnp.tile(jnp.arange(image_slots) < image_count[0], SIDE * SIDE),
            jnp.tile(jnp.arange(crop_slots) < crop_count[0], CROP_SIDE * CROP_SIDE),
        ]
    ).astype(jnp.float32)[:, None]
    live_count = jnp.broadcast_to(
        (image_count * (SIDE * SIDE) + crop_count * (CROP_SIDE * CROP_SIDE)).astype(jnp.float32)[
            None, :
        ],
        (1, LANES),
    )
    made = {}

    def make_inputs(token):
        image_part, crop_part = after(token, (images, crop_pixels))
        made["inputs"] = jnp.concatenate(
            [
                image_part.transpose(1, 2, 0, 3).reshape(image_rows, C_IN),
                crop_part.transpose(1, 2, 0, 3).reshape(-1, C_IN),
            ],
            axis=0,
        )
        return made["inputs"]

    def make_cotangent(token):
        made["cot"] = jnp.dot(
            reorder, after(token, cotangent), preferred_element_type=jnp.float32
        ).astype(low) * live_mask.astype(low)
        return made["cot"]

    def make_thresh(token):
        made["thresh"] = jnp.dot(
            reorder, after(token, thresholds), preferred_element_type=jnp.float32
        ).astype(low)
        return made["thresh"]

    steps = len(bits_of(sizes[1]))
    for step in range(steps):
        job = {0: make_inputs, 1: make_cotangent, steps - 1: make_thresh}.get(step)
        first_got = beside(job, first_held, ring_step(sizes, first_held, step))
        if step == 0:
            second_held, third_own = after(first_got, (second_held, third_own))
            second_got = ring_step(sizes, second_held, 0)
            third_blocks = gather_wide(sizes, third_own)
        if step < steps - 1:
            first_held = jnp.concatenate([first_held, first_got], axis=0)
    inputs, cot_live, thresh = made["inputs"], made["cot"], made["thresh"]
    for step in range(1, steps):
        second_got = after(first_got, second_got)
        second_held = jnp.concatenate([second_held, second_got], axis=0)
        second_got = ring_step(sizes, second_held, step)
    reduce_full, norms_full = ring_end(
        sizes, first_held, first_got, [shard.shape[1] for shard in first_shards]
    )
    reduce_full = reduce_full.reshape(C_IN, C_MID)
    norms_full = norms_full[:, 0, :norm_width].reshape(places, 2, norm_width)
    gain_full = norms_full[:, 0].reshape(-1).astype(jnp.float32)
    shift_full = norms_full[:, 1].reshape(-1).astype(jnp.float32)
    expand_full, heads_full = apart_again(third_blocks, expand_weight.shape[0])
    expand_full = expand_full.reshape(C_MID, C_IN)
    heads_full = heads_full.reshape(C_IN, TASKS * HEAD)

    first_act = jnp.dot(inputs, reduce_full, preferred_element_type=jnp.float32)
    def make_spatial(token):
        made["got"] = after(token, second_got)
        return made["got"]

    normed_one, inv_one, counted, counts = batch_norm(
        sizes, first_act, live_mask, live_count, None, [make_spatial]
    )
    (spatial_full,) = ring_end(sizes, second_held, made["got"], [second_held.shape[1]])
    spatial_full = spatial_full.reshape(9 * C_MID, C_MID)
    pre_one = normed_one * gain_full[:C_MID] + shift_full[:C_MID]
    hidden_one = jax.nn.silu(pre_one).astype(low)
    hidden_one, spatial_full = lax.optimization_barrier((hidden_one, spatial_full))
    shifted = neighbours(hidden_one, image_slots, crop_slots)
    second_act = jnp.dot(
        jnp.concatenate(shifted, axis=1), spatial_full, preferred_element_type=jnp.float32
    )
    def make_drop(first, count):
        def job(token):
            cot, into = after(token, (cot_live, made.get("drop")))
            made["drop"] = soft_drop(cot, heads_full, thresh, first, count, into)
            return made["drop"]

        return job

    normed_two, inv_two, counted, _ = batch_norm(
        sizes,
        second_act,
        live_mask,
        live_count,
        counts,
        [make_drop(0, 1), make_drop(1, 1), make_drop(2, 1)],
    )
    pre_two = normed_two * gain_full[C_MID : 2 * C_MID] + shift_full[C_MID : 2 * C_MID]
    hidden_two = jax.nn.silu(pre_two).astype(low)
    third_act = jnp.dot(hidden_two, expand_full, preferred_element_type=jnp.float32)
    normed_three, inv_three, counted, _ = batch_norm(
        sizes,
        third_act,
        live_mask,
        live_count,
        counts,
        [make_drop(3, 2), make_drop(5, 1), make_drop(6, 2)],
    )
    combined = made["drop"]
    summed = (
        normed_three * gain_full[2 * C_MID :] + shift_full[2 * C_MID :] + inputs.astype(jnp.float32)
    )
    trunk = jax.nn.silu(summed).astype(low)
    upstream = combined * silu_slope(summed)

    def make_heads(first, count):
        def job(token):
            part = after(token, trunk[:, first : first + count])
            made[first] = jnp.dot(part.T, cot_live, preferred_element_type=jnp.float32)
            return made[first]

        return job

    def make_predictions(token):
        made["predictions"] = (
            jnp.dot(after(token, trunk), heads_full, preferred_element_type=jnp.float32) * live_mask
        ).astype(low)
        return made["predictions"]

    grad_three, gain_three, shift_three = norm_back(
        sizes,
        upstream,
        normed_three,
        gain_full[2 * C_MID :],
        inv_three,
        live_mask,
        counted,
        [make_heads(0, C_IN // 2), make_heads(C_IN // 2, C_IN // 2), make_predictions],
    )
    grad_heads = jnp.concatenate([made[0], made[C_IN // 2]], axis=0)
    made["heads"] = Scatter(sizes, grad_heads.reshape(places, -1, TASKS * HEAD))
    back_two = jnp.dot(grad_three, expand_full.T, preferred_element_type=jnp.float32) * silu_slope(
        pre_two
    )

    def make_expand(token):
        grad_expand = jnp.dot(
            hidden_two.T, after(token, grad_three), preferred_element_type=jnp.float32
        )
        made["expand"] = Scatter(sizes, grad_expand.reshape(places, -1, C_IN))
        return (made["expand"].sent, made["heads"].go())

    grad_two, gain_two, shift_two = norm_back(
        sizes,
        back_two,
        normed_two,
        gain_full[C_MID : 2 * C_MID],
        inv_two,
        live_mask,
        counted,
        [make_expand, lambda token: made["heads"].go(token), lambda token: made["heads"].go(token)],
    )
    grad_two, _ = lax.optimization_barrier((grad_two, made["expand"].go()))
    grad_spatial = jnp.concatenate(
        [jnp.dot(piece.T, grad_two, preferred_element_type=jnp.float32) for piece in shifted],
        axis=0,
    )
    spatial = Scatter(sizes, grad_spatial.reshape(places, -1, C_MID))
    grad_two, _ = lax.optimization_barrier((grad_two, (spatial.sent, made["expand"].go())))
    grad_two, _ = lax.optimization_barrier((grad_two, spatial.go()))
    spread = neighbours(grad_two, image_slots, crop_slots)
    back_one = lax.dot_general(
        jnp.stack(spread[::-1], axis=1),
        spatial_full.reshape(9, C_MID, C_MID),
        (((1, 2), (0, 2)), ((), ())),
        preferred_element_type=jnp.float32,
    ) * silu_slope(pre_one)
    grad_one, gain_one, shift_one = norm_back(
        sizes,
        back_one,
        normed_one,
        gain_full[:C_MID],
        inv_one,
        live_mask,
        counted,
        [
            lambda token: made["expand"].go(token),
            lambda token: spatial.go(token),
            lambda token: spatial.go(token),
        ],
    )
    grad_reduce = jnp.dot(inputs.T, grad_one, preferred_element_type=jnp.float32)

    reduce = Scatter(sizes, grad_reduce.reshape(places, -1, C_MID))
    shard_heads, shard_expand = made["heads"].end(), made["expand"].end()
    shard_spatial, shard_reduce = spatial.end(), reduce.end()

    predictions = lax.dot_general(
        reorder,
        made["predictions"],
        (((0,), (0,)), ((), ())),
        preferred_element_type=jnp.float32,
    ).astype(low)
    back = reduce_full.T
    grad_images = (
        (
            jnp.dot(grad_one[:image_rows], back, preferred_element_type=jnp.float32)
            + upstream[:image_rows]
        )
        .astype(low)
        .reshape(SIDE, SIDE, image_slots, C_IN)
        .transpose(2, 0, 1, 3)
    )
    grad_crops = (
        (
            jnp.dot(grad_one[image_rows:], back, preferred_element_type=jnp.float32)
            + upstream[image_rows:]
        )
        .astype(low)
        .reshape(CROP_SIDE, CROP_SIDE, crop_slots, C_IN)
        .transpose(2, 0, 1, 3)
    )

    norm_grads = jnp.stack(
        [
            jnp.concatenate([gain_one, gain_two, gain_three]),
            jnp.concatenate([shift_one, shift_two, shift_three]),
        ]
    )
    norm_shard = lax.dynamic_slice_in_dim(
        norm_grads, lax.axis_index("wide") * norm_width, norm_width, 1
    )
    local_squares = (
        jnp.sum(jnp.square(shard_reduce), axis=0)
        + jnp.sum(jnp.square(shard_spatial), axis=0)
        + jnp.sum(jnp.square(shard_expand).reshape(-1, C_MID), axis=0)
        + jnp.pad(jnp.sum(jnp.square(shard_heads), axis=0), (0, C_MID - TASKS * HEAD))
    )
    squares = jnp.sum(
        sum_rounds(
            sizes,
            local_squares.reshape(-1, LANES),
            [(swap_wide, masks) for masks in rounds_of(sizes[1])],
        )
    ) + jnp.sum(jnp.square(norm_grads))
    norm_before = jnp.sqrt(squares)
    factor = clip_bound / jnp.maximum(norm_before, clip_bound)
    new_reduce, moment_reduce, square_reduce = adamw_step(
        reduce_weight, shard_reduce * factor, first_reduce, second_reduce, weight_rate, weight_decay
    )
    new_spatial, moment_spatial, square_spatial = adamw_step(
        spatial_weight,
        shard_spatial * factor,
        first_spatial,
        second_spatial,
        weight_rate,
        weight_decay,
    )
    new_expand, moment_expand, square_expand = adamw_step(
        expand_weight, shard_expand * factor, first_expand, second_expand, weight_rate, weight_decay
    )
    new_heads, moment_heads, square_heads = adamw_step(
        heads_weight, shard_heads * factor, first_heads, second_heads, weight_rate, weight_decay
    )
    new_norm, moment_norm, square_norm = adamw_step(
        jnp.stack([norm_gains, norm_shifts]),
        norm_shard * factor,
        first_norm,
        second_norm,
        norm_rate,
        0.0,
    )
    return (
        norm_before,
        predictions,
        grad_images,
        grad_crops,
        new_reduce,
        new_spatial,
        new_expand,
        new_heads,
        new_norm,
        moment_reduce,
        moment_spatial,
        moment_expand,
        moment_heads,
        moment_norm,
        square_reduce,
        square_spatial,
        square_expand,
        square_heads,
        square_norm,
    )


def solution(mesh):
    sizes = (mesh.shape["dp"], mesh.shape["wide"])
    return jax.shard_map(
        functools.partial(local, sizes),
        mesh=mesh,
        in_specs=(
            P(("dp", "wide"), None, None, None),
            P(("dp", "wide"), None, None, None),
            P(("dp", "wide"), None),
            P(("dp", "wide"), None),
            P(("dp", "wide")),
            P(("dp", "wide")),
            P("wide", None),
            P("wide", None),
            P("wide", None),
            P("wide", None),
            P("wide"),
            P("wide"),
            P("wide", None),
            P("wide", None),
            P("wide", None),
            P("wide", None),
            P(None, "wide"),
            P("wide", None),
            P("wide", None),
            P("wide", None),
            P("wide", None),
            P(None, "wide"),
        ),
        out_specs=(
            P(),
            P(("dp", "wide"), None),
            P(("dp", "wide"), None, None, None),
            P(("dp", "wide"), None, None, None),
            P("wide", None),
            P("wide", None),
            P("wide", None),
            P("wide", None),
            P(None, "wide"),
            P("wide", None),
            P("wide", None),
            P("wide", None),
            P("wide", None),
            P(None, "wide"),
            P("wide", None),
            P("wide", None),
            P("wide", None),
            P("wide", None),
            P(None, "wide"),
        ),
        check_vma=False,
    )
```

```python
import functools

import jax
import jax.numpy as jnp
from jax import lax
from jax.experimental import pallas as pl
from jax.experimental.pallas import tpu as pltpu
from jax.sharding import PartitionSpec as P

C_IN = 2048
C_MID = 512
HEAD = 128
TASKS = 3
SIDE = 7
CROP_SIDE = 2
STEP = 10
IMG_CAP = 24
CROP_CAP = 16


norm_eps = 1e-05
soft_scale = 0.05
purity_temper = 0.1
clip_bound = 1.0
first_decay = 0.9
second_decay = 0.999
adam_eps = 1e-08
weight_rate = 0.02
norm_rate = 0.5
weight_decay = 0.1


def silu_slope(values):
    sigma = jax.nn.sigmoid(values)
    return sigma * (1.0 + values * (1.0 - sigma))


def soft_drop(task_grads, thresh):
    together = task_grads[0]
    magnitude = jnp.sqrt(task_grads[0] * task_grads[0] + soft_scale * soft_scale)
    for further in task_grads[1:]:
        together = together + further
        magnitude = magnitude + jnp.sqrt(further * further + soft_scale * soft_scale)
    purity = 0.5 * (1.0 + together / magnitude)
    upward = jax.nn.sigmoid((purity - thresh) / purity_temper)
    combined = jnp.zeros_like(together)
    for grad_part in task_grads:
        keeping = upward * jax.nn.sigmoid(grad_part / soft_scale) + (1.0 - upward) * jax.nn.sigmoid(
            -grad_part / soft_scale
        )
        combined = combined + grad_part * keeping
    return combined


def adamw_step(weights, gradient, moment, square, step_rate, decay_rate):
    moment_new = first_decay * moment + (1.0 - first_decay) * gradient
    square_new = second_decay * square + (1.0 - second_decay) * gradient * gradient
    moment_hat = moment_new / (1.0 - first_decay**STEP)
    square_hat = square_new / (1.0 - second_decay**STEP)
    updated = weights - step_rate * (
        moment_hat / (jnp.sqrt(square_hat) + adam_eps) + decay_rate * weights
    )
    return (updated, moment_new, square_new)


BOTH = ("dp", "wide")
LANES = 128


def bits_of(size):
    return [1 << k for k in range(size.bit_length() - 1)]


def swap_dp(sizes, values, mask):
    return lax.ppermute(values, "dp", [(i, i ^ mask) for i in range(sizes[0])])


def swap_wide(sizes, values, mask):
    return lax.ppermute(values, "wide", [(i, i ^ mask) for i in range(sizes[1])])


def rounds_of(size):
    left = bits_of(size)[::-1]
    rounds = []
    while left:
        pair, left = left[:2], left[2:]
        rounds.append((pair[1], pair[0], pair[0] | pair[1]) if len(pair) == 2 else (pair[0],))
    return rounds


def all_rounds(sizes):
    return [(swap_dp, masks) for masks in rounds_of(sizes[0])] + [
        (swap_wide, masks) for masks in rounds_of(sizes[1])
    ]


def beside(job, token, got):
    if job is None:
        return got
    return lax.optimization_barrier((got, job(token)))[0]


def after(token, values):
    return lax.optimization_barrier((values, token))[0]


def sum_rounds(sizes, values, rounds, jobs=()):
    for level, (swap, masks) in enumerate(rounds):
        got = [swap(sizes, values, mask) for mask in masks]
        got = beside(jobs[level] if level < len(jobs) else None, values, got)
        if len(masks) == 3:
            values = (values + got[0]) + (got[1] + got[2])
        else:
            values = values + got[0]
    return values


def pool(first, second):
    count_a, total_a, spread_a = first
    count_b, total_b, spread_b = second
    count = count_a + count_b
    apart = total_a / count_a - total_b / count_b
    weight = count_a * count_b / count
    return (count, total_a + total_b, (spread_a + spread_b) + (apart * apart) * weight)


def pool_all(sizes, count, total, spread, counts, jobs):
    seen = []
    total, spread = total.reshape(-1, LANES), spread.reshape(-1, LANES)
    for level, (swap, masks) in enumerate(all_rounds(sizes)):
        parts = [total, spread]
        if counts is None:
            parts.append(jnp.broadcast_to(count, total.shape))
        packet = jnp.stack(parts)
        got = [swap(sizes, packet, mask) for mask in masks]
        got = beside(jobs[level] if level < len(jobs) else None, packet, got)
        seen.append((count, [g[2, :1] for g in got]) if counts is None else counts[level])
        sets = [(seen[-1][0], total, spread)] + [
            (c, g[0], g[1]) for c, g in zip(seen[-1][1], got)
        ]
        if len(sets) == 4:
            sets = [pool(sets[0], sets[1]), pool(sets[2], sets[3])]
        count, total, spread = pool(sets[0], sets[1])
    return (count, total, spread, seen)


def batch_norm(sizes, values, live_mask, live_count, counts, jobs=()):
    width = values.shape[1]
    total = jnp.sum(values * live_mask, axis=0)
    own_mean = (total.reshape(-1, LANES) / live_count).reshape(width)
    deviation = (values - own_mean) * live_mask
    spread = jnp.sum(deviation * deviation, axis=0)
    counted, total, spread, counts = pool_all(sizes, live_count, total, spread, counts, jobs)
    inv_std = lax.rsqrt(spread / counted + norm_eps).reshape(width)
    centre = (total / counted).reshape(width)
    return ((values - centre) * inv_std, inv_std, counted, counts)


def norm_back(sizes, upstream, normed, gain_part, inv_std, live_mask, counted, jobs=()):
    width = upstream.shape[1]
    sums = sum_rounds(
        sizes,
        jnp.stack(
            [
                jnp.sum(upstream * normed, axis=0).reshape(-1, LANES),
                jnp.sum(upstream, axis=0).reshape(-1, LANES),
            ]
        ),
        all_rounds(sizes),
        jobs,
    )
    mean_gain = (sums[0] / counted).reshape(width)
    mean_shift = (sums[1] / counted).reshape(width)
    grad_act = live_mask * (gain_part * inv_std) * (upstream - (mean_shift + normed * mean_gain))
    return (grad_act.astype(jnp.bfloat16), sums[0].reshape(width), sums[1].reshape(width))


def orders(size):
    down = bits_of(size)[::-1]
    return (down, down[:-2] + down[:-3:-1])


def crossing(sizes, step):
    pair = orders(sizes[1])
    return [
        (dp * sizes[1] + place, dp * sizes[1] + (place ^ pair[dp & 1][step]))
        for dp in range(sizes[0])
        for place in range(sizes[1])
    ]


def apart_of(sizes, core, slot):
    masks = []
    for order in orders(sizes[1]):
        mask = 0
        for k, bit in enumerate(order):
            if slot >> k & 1:
                mask ^= bit
        masks.append(mask)
    return jnp.where(core == 0, masks[0], masks[1])


def pick(blocks, index):
    return lax.dynamic_index_in_dim(blocks, index, 0, keepdims=True)


def settle_kernel(sizes, starts, *refs):
    outs, pieces = refs[-len(starts) :], refs[: -len(starts)]
    core, place = lax.axis_index("dp") & 1, lax.axis_index("wide")
    per_core = len(pieces) // 2
    for part, piece in enumerate(pieces):
        half = core if part < per_core else 1 - core
        for block in range(piece.shape[0]):
            slot = block + (part % per_core) * piece.shape[0]
            target = (place ^ apart_of(sizes, half, slot)) * 2 + half
            for start, out in zip(starts, outs):
                out[target] = piece[block, start : start + out.shape[1]]


def settle(sizes, pieces, heights):
    width = pieces[0].shape[2]
    count = 2 * sizes[1]
    starts = [sum(heights[:k]) for k in range(len(heights))]
    return pl.pallas_call(
        functools.partial(settle_kernel, sizes, starts),
        in_specs=[pl.BlockSpec(memory_space=pltpu.VMEM)] * len(pieces),
        out_specs=[pl.BlockSpec(memory_space=pltpu.VMEM)] * len(heights),
        out_shape=[
            jax.ShapeDtypeStruct((count, height, width), pieces[0].dtype) for height in heights
        ],
        compiler_params=pltpu.CompilerParams(vmem_limit_bytes=12 * 2**20),
        cost_estimate=pl.CostEstimate(
            flops=0, bytes_accessed=4 * count * sum(heights) * width, transcendentals=0
        ),
    )(*pieces)


def halves_of(shard):
    return shard.reshape(2, shard.shape[0] // 2, shard.shape[1])


def ring_own(shards):
    return pick(jnp.concatenate(shards, axis=1), lax.axis_index("dp") & 1)


def ring_step(sizes, held, step):
    return lax.ppermute(held, BOTH, crossing(sizes, step))


def ring_end(sizes, held, got, heights):
    pieces = [held, got]
    pieces += [swap_dp(sizes, piece, 1) for piece in pieces]
    return settle(sizes, pieces, heights)


def gather_wide(sizes, shard):
    core = lax.axis_index("dp") & 1
    return lax.all_gather(pick(halves_of(shard), core), "wide", axis=0, tiled=True)


def gather_end(sizes, held):
    core = lax.axis_index("dp") & 1
    other = swap_dp(sizes, held, 1)
    low = jnp.where(core == 0, held, other)
    high = jnp.where(core == 0, other, held)
    count, rows, width = held.shape
    return jnp.stack([low, high], axis=1).reshape(count, 2 * rows, width)


def finish_sum(sizes, held):
    core = lax.axis_index("dp") & 1
    for bit in bits_of(sizes[0])[1:]:
        low = held.astype(jnp.bfloat16)
        held = low.astype(jnp.float32) + swap_dp(sizes, low, bit).astype(jnp.float32)
    other = swap_dp(sizes, held, 1)
    return jnp.where(
        core == 0,
        jnp.concatenate([held, other], axis=0),
        jnp.concatenate([other, held], axis=0),
    )


def scatter_halves(grads):
    core = lax.axis_index("dp") & 1
    count, rows, width = grads.shape
    halves = grads.reshape(count, 2, rows // 2, width)
    sent = lax.dynamic_index_in_dim(halves, 1 - core, 1, keepdims=False).astype(jnp.bfloat16)
    return (sent, lax.dynamic_index_in_dim(halves, core, 1, keepdims=False))


def part_kernel(sizes, blocks_ref, sent_ref):
    core, place = lax.axis_index("dp") & 1, lax.axis_index("wide")
    for slot in range(sent_ref.shape[0]):
        source = (place ^ apart_of(sizes, 1 - core, slot)) * 2 + 1 - core
        sent_ref[slot] = blocks_ref[source].astype(sent_ref.dtype)


def part(sizes, blocks):
    _, rows, width = blocks.shape
    return pl.pallas_call(
        functools.partial(part_kernel, sizes),
        in_specs=[pl.BlockSpec(memory_space=pltpu.VMEM)],
        out_specs=pl.BlockSpec(memory_space=pltpu.VMEM),
        out_shape=jax.ShapeDtypeStruct((sizes[1], rows, width), jnp.bfloat16),
        compiler_params=pltpu.CompilerParams(vmem_limit_bytes=16 * 2**20),
        cost_estimate=pl.CostEstimate(
            flops=0, bytes_accessed=6 * sizes[1] * rows * width, transcendentals=0
        ),
    )(blocks)


def join_kernel(sizes, first, held_ref, got_ref, sent_ref, kept_ref):
    core, place = lax.axis_index("dp") & 1, lax.axis_index("wide")
    half = sent_ref.shape[0]
    for slot in range(2 * half):
        source = (place ^ apart_of(sizes, core, slot)) * 2 + core if first else slot
        value = held_ref[source] + got_ref[slot].astype(jnp.float32)
        if slot < half:
            kept_ref[slot] = value
        else:
            sent_ref[slot - half] = value.astype(sent_ref.dtype)


def join(sizes, first, held, got):
    count, rows, width = got.shape
    shape = (count // 2, rows, width)
    return pl.pallas_call(
        functools.partial(join_kernel, sizes, first),
        in_specs=[pl.BlockSpec(memory_space=pltpu.VMEM)] * 2,
        out_specs=[pl.BlockSpec(memory_space=pltpu.VMEM)] * 2,
        out_shape=[
            jax.ShapeDtypeStruct(shape, jnp.bfloat16),
            jax.ShapeDtypeStruct(shape, jnp.float32),
        ],
        compiler_params=pltpu.CompilerParams(vmem_limit_bytes=20 * 2**20),
        cost_estimate=pl.CostEstimate(
            flops=count * rows * width, bytes_accessed=9 * count * rows * width, transcendentals=0
        ),
    )(held, got)


class Scatter:
    def __init__(self, sizes, grads):
        self.sizes, self.step = sizes, len(bits_of(sizes[1]))
        count, rows, width = grads.shape
        self.held, self.first = grads.reshape(count * 2, rows // 2, width), True
        self.sent = part(sizes, self.held)
        self.got = swap_dp(sizes, self.sent, 1)

    def go(self, token=None):
        got = self.got if token is None else after(token, self.got)
        self.sent, self.held = join(self.sizes, self.first, self.held, got)
        self.step, self.first = self.step - 1, False
        self.got = ring_step(self.sizes, self.sent, self.step)
        return self.sent

    def end(self):
        while self.step:
            self.go()
        return finish_sum(self.sizes, self.held[0] + self.got[0].astype(jnp.float32))


def side_by_side(expand, heads):
    count, rows, _ = expand.shape
    four = jnp.concatenate(
        [expand[:, :, part * C_MID : (part + 1) * C_MID] for part in range(4)], axis=1
    )
    return jnp.concatenate([four, heads], axis=2)


def apart_again(both, rows):
    four, heads = both[:, :, :C_MID], both[:, :, C_MID:]
    expand = jnp.concatenate(
        [four[:, part * rows : (part + 1) * rows] for part in range(4)], axis=2
    )
    return (expand, heads)


def neighbours(rows, image_slots, crop_slots):
    width = rows.shape[1]
    cut = image_slots * SIDE * SIDE
    images = jnp.pad(
        rows[:cut].reshape(SIDE, SIDE, image_slots, width), ((1, 1), (1, 1), (0, 0), (0, 0))
    )
    crops = jnp.pad(
        rows[cut:].reshape(CROP_SIDE, CROP_SIDE, crop_slots, width),
        ((1, 1), (1, 1), (0, 0), (0, 0)),
    )
    return [
        jnp.concatenate(
            [
                images[oy : oy + SIDE, ox : ox + SIDE].reshape(-1, width),
                crops[oy : oy + CROP_SIDE, ox : ox + CROP_SIDE].reshape(-1, width),
            ],
            axis=0,
        )
        for oy in range(3)
        for ox in range(3)
    ]


def drop_kernel(cot_ref, heads_ref, thresh_ref, *rest):
    out_ref = rest[-1]
    half_scale, half_temper = 0.5 / soft_scale, 0.5 / purity_temper
    together, magnitude, leaning = 0.0, 0.0, 0.0
    for task in range(TASKS):
        columns = slice(task * HEAD, (task + 1) * HEAD)
        part = lax.dot_general(
            cot_ref[:, columns],
            heads_ref[:, columns],
            (((1,), (1,)), ((), ())),
            preferred_element_type=jnp.float32,
        )
        square = part * part + soft_scale * soft_scale
        together = together + part
        magnitude = magnitude + square * lax.rsqrt(square)
        leaning = leaning + part * jnp.tanh(part * half_scale)
    lean = (
        thresh_ref[...].astype(jnp.float32) * -half_temper
        + 0.5 * half_temper
        + (together * (0.5 * half_temper)) / magnitude
    )
    out_ref[...] = 0.5 * (together + jnp.tanh(lean) * leaning)


DROP_TILE = 256


def soft_drop(cot_live, heads_full, thresh, first, count, into=None):
    rows, width = thresh.shape
    more = [] if into is None else [into]
    return pl.pallas_call(
        drop_kernel,
        grid=(count,),
        in_specs=[
            pl.BlockSpec((rows, TASKS * HEAD), lambda i: (0, 0)),
            pl.BlockSpec((DROP_TILE, TASKS * HEAD), lambda i: (first + i, 0)),
            pl.BlockSpec((rows, DROP_TILE), lambda i: (0, first + i)),
        ]
        + [pl.BlockSpec(memory_space=pl.ANY)] * len(more),
        out_specs=pl.BlockSpec((rows, DROP_TILE), lambda i: (0, first + i)),
        out_shape=jax.ShapeDtypeStruct((rows, width), jnp.float32),
        input_output_aliases={3: 0} if more else {},
        compiler_params=pltpu.CompilerParams(vmem_limit_bytes=18 * 2**20),
        cost_estimate=pl.CostEstimate(
            flops=2 * rows * count * DROP_TILE * TASKS * HEAD,
            bytes_accessed=6 * rows * count * DROP_TILE,
            transcendentals=8 * rows * count * DROP_TILE,
        ),
    )(cot_live, heads_full, thresh, *more)


def slot_source(image_slots, crop_slots):
    def part(slots, pixels, start):
        return (jnp.arange(slots)[None, :] * pixels + jnp.arange(pixels)[:, None]).reshape(-1) + start

    images = image_slots * SIDE * SIDE
    return jnp.concatenate(
        [part(image_slots, SIDE * SIDE, 0), part(crop_slots, CROP_SIDE * CROP_SIDE, images)]
    )


def local(
    sizes,
    images,
    crop_pixels,
    thresholds,
    cotangent,
    image_count,
    crop_count,
    reduce_weight,
    spatial_weight,
    expand_weight,
    heads_weight,
    norm_gains,
    norm_shifts,
    first_reduce,
    first_spatial,
    first_expand,
    first_heads,
    first_norm,
    second_reduce,
    second_spatial,
    second_expand,
    second_heads,
    second_norm,
):
    low = jnp.bfloat16
    image_slots, crop_slots = images.shape[0], crop_pixels.shape[0]
    image_rows = image_slots * SIDE * SIDE
    rows = image_rows + crop_slots * CROP_SIDE * CROP_SIDE
    places = sizes[1]
    reorder = (
        slot_source(image_slots, crop_slots)[:, None] == jnp.arange(rows)[None, :]
    ).astype(low)

    norm_width = norm_gains.shape[0]
    norms = jnp.pad(
        jnp.stack([norm_gains, norm_shifts]).astype(low)[:, None],
        ((0, 0), (0, 15), (0, C_MID - norm_width)),
    )
    third_own = side_by_side(expand_weight.astype(low)[None], heads_weight.astype(low)[None])[0]
    first_shards = [halves_of(reduce_weight.astype(low)), norms]
    first_held = ring_own(first_shards)
    second_held = ring_own([halves_of(spatial_weight.astype(low))])

    live_mask = jnp.concatenate(
        [
            jnp.tile(jnp.arange(image_slots) < image_count[0], SIDE * SIDE),
            jnp.tile(jnp.arange(crop_slots) < crop_count[0], CROP_SIDE * CROP_SIDE),
        ]
    ).astype(jnp.float32)[:, None]
    live_count = jnp.broadcast_to(
        (image_count * (SIDE * SIDE) + crop_count * (CROP_SIDE * CROP_SIDE)).astype(jnp.float32)[
            None, :
        ],
        (1, LANES),
    )
    made = {}

    def make_inputs(token):
        image_part, crop_part = after(token, (images, crop_pixels))
        made["inputs"] = jnp.concatenate(
            [
                image_part.transpose(1, 2, 0, 3).reshape(image_rows, C_IN),
                crop_part.transpose(1, 2, 0, 3).reshape(-1, C_IN),
            ],
            axis=0,
        )
        return made["inputs"]

    def make_cotangent(token):
        made["cot"] = jnp.dot(
            reorder, after(token, cotangent), preferred_element_type=jnp.float32
        ).astype(low) * live_mask.astype(low)
        return made["cot"]

    def make_thresh(token):
        made["thresh"] = jnp.dot(
            reorder, after(token, thresholds), preferred_element_type=jnp.float32
        ).astype(low)
        return made["thresh"]

    steps = len(bits_of(sizes[1]))
    for step in range(steps):
        job = {0: make_inputs, 1: make_cotangent}.get(step)
        first_got = beside(job, first_held, ring_step(sizes, first_held, step))
        if step == 0:
            second_held, third_own = after(first_got, (second_held, third_own))
            second_got = ring_step(sizes, second_held, 0)
            third_blocks = gather_wide(sizes, third_own)
        if step < steps - 1:
            first_held = jnp.concatenate([first_held, first_got], axis=0)
    inputs, cot_live = made["inputs"], made["cot"]
    second_held = jnp.concatenate([second_held, after(first_got, second_got)], axis=0)
    second_got = ring_step(sizes, second_held, 1)
    reduce_full, norms_full = ring_end(
        sizes, first_held, first_got, [shard.shape[1] for shard in first_shards]
    )
    reduce_full = reduce_full.reshape(C_IN, C_MID)
    norms_full = norms_full[:, 0, :norm_width].reshape(places, 2, norm_width)
    gain_full = norms_full[:, 0].reshape(-1).astype(jnp.float32)
    shift_full = norms_full[:, 1].reshape(-1).astype(jnp.float32)
    inputs, second_got = lax.optimization_barrier((inputs, second_got))
    first_act = jnp.dot(inputs, reduce_full, preferred_element_type=jnp.float32)
    for step in range(2, steps):
        second_held = jnp.concatenate([second_held, second_got], axis=0)
        second_got = ring_step(sizes, second_held, step)

    def make_spatial(token):
        made["got"] = after(token, second_got)
        return made["got"]

    normed_one, inv_one, counted, counts = batch_norm(
        sizes, first_act, live_mask, live_count, None, [make_thresh, make_spatial]
    )
    (spatial_full,) = ring_end(sizes, second_held, made["got"], [second_held.shape[1]])
    spatial_full = spatial_full.reshape(9 * C_MID, C_MID)
    pre_one = normed_one * gain_full[:C_MID] + shift_full[:C_MID]
    hidden_one = jax.nn.silu(pre_one).astype(low)
    hidden_one, spatial_full = lax.optimization_barrier((hidden_one, spatial_full))
    shifted = neighbours(hidden_one, image_slots, crop_slots)
    second_act = jnp.dot(
        jnp.concatenate(shifted, axis=1), spatial_full, preferred_element_type=jnp.float32
    )
    expand_full, heads_full = apart_again(
        gather_end(sizes, after(second_act, third_blocks)), expand_weight.shape[0]
    )
    expand_full = expand_full.reshape(C_MID, C_IN)
    heads_full = heads_full.reshape(C_IN, TASKS * HEAD)

    def make_drop(first, count):
        def job(token):
            cot, into = after(token, (cot_live, made.get("drop")))
            made["drop"] = soft_drop(cot, heads_full, made["thresh"], first, count, into)
            return made["drop"]

        return job

    normed_two, inv_two, counted, _ = batch_norm(
        sizes,
        second_act,
        live_mask,
        live_count,
        counts,
        [make_drop(0, 1), make_drop(1, 1), make_drop(2, 1)],
    )
    pre_two = normed_two * gain_full[C_MID : 2 * C_MID] + shift_full[C_MID : 2 * C_MID]
    hidden_two = jax.nn.silu(pre_two).astype(low)
    third_act = jnp.dot(hidden_two, expand_full, preferred_element_type=jnp.float32)
    normed_three, inv_three, counted, _ = batch_norm(
        sizes,
        third_act,
        live_mask,
        live_count,
        counts,
        [make_drop(3, 2), make_drop(5, 1), make_drop(6, 2)],
    )
    combined = made["drop"]
    summed = (
        normed_three * gain_full[2 * C_MID :] + shift_full[2 * C_MID :] + inputs.astype(jnp.float32)
    )
    trunk = jax.nn.silu(summed).astype(low)
    upstream = combined * silu_slope(summed)

    def make_heads(first, count):
        def job(token):
            part = after(token, trunk[:, first : first + count])
            made[first] = jnp.dot(part.T, cot_live, preferred_element_type=jnp.float32)
            return made[first]

        return job

    def make_predictions(token):
        made["predictions"] = (
            jnp.dot(after(token, trunk), heads_full, preferred_element_type=jnp.float32) * live_mask
        ).astype(low)
        return made["predictions"]

    grad_three, gain_three, shift_three = norm_back(
        sizes,
        upstream,
        normed_three,
        gain_full[2 * C_MID :],
        inv_three,
        live_mask,
        counted,
        [make_heads(0, C_IN // 2), make_heads(C_IN // 2, C_IN // 2), make_predictions],
    )
    heads = Scatter(
        sizes,
        jnp.concatenate([made[0], made[C_IN // 2]], axis=0).reshape(places, -1, TASKS * HEAD),
    )
    grad_three, _ = lax.optimization_barrier((grad_three, heads.go()))
    back_two = jnp.dot(grad_three, expand_full.T, preferred_element_type=jnp.float32) * silu_slope(
        pre_two
    )

    def make_expand(token):
        grad_expand = jnp.dot(
            hidden_two.T, after(token, grad_three), preferred_element_type=jnp.float32
        )
        made["expand"] = Scatter(sizes, grad_expand.reshape(places, -1, C_IN))
        return made["expand"].sent

    grad_two, gain_two, shift_two = norm_back(
        sizes,
        back_two,
        normed_two,
        gain_full[C_MID : 2 * C_MID],
        inv_two,
        live_mask,
        counted,
        [make_expand, heads.go, heads.go],
    )
    expand = made["expand"]
    grad_two, _ = lax.optimization_barrier((grad_two, expand.go()))
    spread = neighbours(grad_two, image_slots, crop_slots)
    back_one = lax.dot_general(
        jnp.stack(spread[::-1], axis=1),
        spatial_full.reshape(9, C_MID, C_MID),
        (((1, 2), (0, 2)), ((), ())),
        preferred_element_type=jnp.float32,
    ) * silu_slope(pre_one)
    def make_spatial_grad(first, count):
        def job(token):
            upstream_two = after(token, grad_two)
            made[first, "spatial"] = [
                jnp.dot(piece.T, upstream_two, preferred_element_type=jnp.float32)
                for piece in shifted[first : first + count]
            ]
            return made[first, "spatial"]

        return job

    def start_spatial(token):
        pieces = after(token, made[0, "spatial"] + made[4, "spatial"])
        made["spatial"] = Scatter(
            sizes, jnp.concatenate(pieces, axis=0).reshape(places, -1, C_MID)
        )
        return (made["spatial"].sent, expand.go())

    grad_one, gain_one, shift_one = norm_back(
        sizes,
        back_one,
        normed_one,
        gain_full[:C_MID],
        inv_one,
        live_mask,
        counted,
        [make_spatial_grad(0, 4), make_spatial_grad(4, 5), start_spatial],
    )
    spatial = made["spatial"]
    grad_one, _ = lax.optimization_barrier((grad_one, (spatial.go(), expand.go())))
    grad_reduce = jnp.dot(inputs.T, grad_one, preferred_element_type=jnp.float32)

    reduce = Scatter(sizes, grad_reduce.reshape(places, -1, C_MID))
    reduce.go()
    spatial.go()

    predictions = lax.dot_general(
        reorder,
        made["predictions"],
        (((0,), (0,)), ((), ())),
        preferred_element_type=jnp.float32,
    ).astype(low)
    back = reduce_full.T
    grad_images = (
        jnp.dot(grad_one[:image_rows], back, preferred_element_type=jnp.float32)
        + upstream[:image_rows]
    ).astype(low)
    grad_crops = (
        jnp.dot(grad_one[image_rows:], back, preferred_element_type=jnp.float32)
        + upstream[image_rows:]
    ).astype(low)
    reduce.got, predictions, grad_images, grad_crops = lax.optimization_barrier(
        (reduce.got, predictions, grad_images, grad_crops)
    )
    grad_images = grad_images.reshape(SIDE, SIDE, image_slots, C_IN).transpose(2, 0, 1, 3)
    grad_crops = grad_crops.reshape(CROP_SIDE, CROP_SIDE, crop_slots, C_IN).transpose(2, 0, 1, 3)
    shard_heads, shard_expand = heads.end(), expand.end()
    shard_spatial, shard_reduce = spatial.end(), reduce.end()

    norm_grads = jnp.stack(
        [
            jnp.concatenate([gain_one, gain_two, gain_three]),
            jnp.concatenate([shift_one, shift_two, shift_three]),
        ]
    )
    norm_shard = lax.dynamic_slice_in_dim(
        norm_grads, lax.axis_index("wide") * norm_width, norm_width, 1
    )
    local_squares = (
        jnp.sum(jnp.square(shard_reduce), axis=0)
        + jnp.sum(jnp.square(shard_spatial), axis=0)
        + jnp.sum(jnp.square(shard_expand).reshape(-1, C_MID), axis=0)
        + jnp.pad(jnp.sum(jnp.square(shard_heads), axis=0), (0, C_MID - TASKS * HEAD))
    )
    squares = jnp.sum(
        sum_rounds(
            sizes,
            local_squares.reshape(-1, LANES),
            [(swap_wide, masks) for masks in rounds_of(sizes[1])],
        )
    ) + jnp.sum(jnp.square(norm_grads))
    norm_before = jnp.sqrt(squares)
    factor = clip_bound / jnp.maximum(norm_before, clip_bound)
    new_reduce, moment_reduce, square_reduce = adamw_step(
        reduce_weight, shard_reduce * factor, first_reduce, second_reduce, weight_rate, weight_decay
    )
    new_spatial, moment_spatial, square_spatial = adamw_step(
        spatial_weight,
        shard_spatial * factor,
        first_spatial,
        second_spatial,
        weight_rate,
        weight_decay,
    )
    new_expand, moment_expand, square_expand = adamw_step(
        expand_weight, shard_expand * factor, first_expand, second_expand, weight_rate, weight_decay
    )
    new_heads, moment_heads, square_heads = adamw_step(
        heads_weight, shard_heads * factor, first_heads, second_heads, weight_rate, weight_decay
    )
    new_norm, moment_norm, square_norm = adamw_step(
        jnp.stack([norm_gains, norm_shifts]),
        norm_shard * factor,
        first_norm,
        second_norm,
        norm_rate,
        0.0,
    )
    return (
        norm_before,
        predictions,
        grad_images,
        grad_crops,
        new_reduce,
        new_spatial,
        new_expand,
        new_heads,
        new_norm,
        moment_reduce,
        moment_spatial,
        moment_expand,
        moment_heads,
        moment_norm,
        square_reduce,
        square_spatial,
        square_expand,
        square_heads,
        square_norm,
    )


def solution(mesh):
    sizes = (mesh.shape["dp"], mesh.shape["wide"])
    return jax.shard_map(
        functools.partial(local, sizes),
        mesh=mesh,
        in_specs=(
            P(("dp", "wide"), None, None, None),
            P(("dp", "wide"), None, None, None),
            P(("dp", "wide"), None),
            P(("dp", "wide"), None),
            P(("dp", "wide")),
            P(("dp", "wide")),
            P("wide", None),
            P("wide", None),
            P("wide", None),
            P("wide", None),
            P("wide"),
            P("wide"),
            P("wide", None),
            P("wide", None),
            P("wide", None),
            P("wide", None),
            P(None, "wide"),
            P("wide", None),
            P("wide", None),
            P("wide", None),
            P("wide", None),
            P(None, "wide"),
        ),
        out_specs=(
            P(),
            P(("dp", "wide"), None),
            P(("dp", "wide"), None, None, None),
            P(("dp", "wide"), None, None, None),
            P("wide", None),
            P("wide", None),
            P("wide", None),
            P("wide", None),
            P(None, "wide"),
            P("wide", None),
            P("wide", None),
            P("wide", None),
            P("wide", None),
            P(None, "wide"),
            P("wide", None),
            P("wide", None),
            P("wide", None),
            P("wide", None),
            P(None, "wide"),
        ),
        check_vma=False,
    )
```

```python
import functools

import jax
import jax.numpy as jnp
from jax import lax
from jax.experimental import pallas as pl
from jax.experimental.pallas import tpu as pltpu
from jax.sharding import PartitionSpec as P

C_IN = 2048
C_MID = 512
HEAD = 128
TASKS = 3
SIDE = 7
CROP_SIDE = 2
STEP = 10
IMG_CAP = 24
CROP_CAP = 16


norm_eps = 1e-05
soft_scale = 0.05
purity_temper = 0.1
clip_bound = 1.0
first_decay = 0.9
second_decay = 0.999
adam_eps = 1e-08
weight_rate = 0.02
norm_rate = 0.5
weight_decay = 0.1


def silu_slope(values):
    sigma = jax.nn.sigmoid(values)
    return sigma * (1.0 + values * (1.0 - sigma))


def soft_drop(task_grads, thresh):
    together = task_grads[0]
    magnitude = jnp.sqrt(task_grads[0] * task_grads[0] + soft_scale * soft_scale)
    for further in task_grads[1:]:
        together = together + further
        magnitude = magnitude + jnp.sqrt(further * further + soft_scale * soft_scale)
    purity = 0.5 * (1.0 + together / magnitude)
    upward = jax.nn.sigmoid((purity - thresh) / purity_temper)
    combined = jnp.zeros_like(together)
    for grad_part in task_grads:
        keeping = upward * jax.nn.sigmoid(grad_part / soft_scale) + (1.0 - upward) * jax.nn.sigmoid(
            -grad_part / soft_scale
        )
        combined = combined + grad_part * keeping
    return combined


def adamw_step(weights, gradient, moment, square, step_rate, decay_rate):
    moment_new = first_decay * moment + (1.0 - first_decay) * gradient
    square_new = second_decay * square + (1.0 - second_decay) * gradient * gradient
    moment_hat = moment_new / (1.0 - first_decay**STEP)
    square_hat = square_new / (1.0 - second_decay**STEP)
    updated = weights - step_rate * (
        moment_hat / (jnp.sqrt(square_hat) + adam_eps) + decay_rate * weights
    )
    return (updated, moment_new, square_new)


BOTH = ("dp", "wide")
LANES = 128


def bits_of(size):
    return [1 << k for k in range(size.bit_length() - 1)]


def swap_dp(sizes, values, mask):
    return lax.ppermute(values, "dp", [(i, i ^ mask) for i in range(sizes[0])])


def swap_wide(sizes, values, mask):
    return lax.ppermute(values, "wide", [(i, i ^ mask) for i in range(sizes[1])])


def rounds_of(size):
    left = bits_of(size)[::-1]
    rounds = []
    while left:
        pair, left = left[:2], left[2:]
        rounds.append((pair[1], pair[0], pair[0] | pair[1]) if len(pair) == 2 else (pair[0],))
    return rounds


def all_rounds(sizes):
    return [(swap_dp, masks) for masks in rounds_of(sizes[0])] + [
        (swap_wide, masks) for masks in rounds_of(sizes[1])
    ]


def beside(job, token, got):
    if job is None:
        return got
    return lax.optimization_barrier((got, job(token)))[0]


def after(token, values):
    return lax.optimization_barrier((values, token))[0]


def both_jobs(one, other):
    return lambda token: (one(token), other(token))


def sum_rounds(sizes, values, rounds, jobs=()):
    for level, (swap, masks) in enumerate(rounds):
        got = [swap(sizes, values, mask) for mask in masks]
        got = beside(jobs[level] if level < len(jobs) else None, values, got)
        if len(masks) == 3:
            values = (values + got[0]) + (got[1] + got[2])
        else:
            values = values + got[0]
    return values


def pool(first, second):
    count_a, total_a, spread_a = first
    count_b, total_b, spread_b = second
    count = count_a + count_b
    apart = total_a / count_a - total_b / count_b
    weight = count_a * count_b / count
    return (count, total_a + total_b, (spread_a + spread_b) + (apart * apart) * weight)


def pool_all(sizes, count, total, spread, counts, jobs):
    seen = []
    total, spread = total.reshape(-1, LANES), spread.reshape(-1, LANES)
    for level, (swap, masks) in enumerate(all_rounds(sizes)):
        parts = [total, spread]
        if counts is None:
            parts.append(jnp.broadcast_to(count, total.shape))
        packet = jnp.stack(parts)
        got = [swap(sizes, packet, mask) for mask in masks]
        got = beside(jobs[level] if level < len(jobs) else None, packet, got)
        seen.append((count, [g[2, :1] for g in got]) if counts is None else counts[level])
        sets = [(seen[-1][0], total, spread)] + [
            (c, g[0], g[1]) for c, g in zip(seen[-1][1], got)
        ]
        if len(sets) == 4:
            sets = [pool(sets[0], sets[1]), pool(sets[2], sets[3])]
        count, total, spread = pool(sets[0], sets[1])
    return (count, total, spread, seen)


def batch_norm(sizes, values, live_mask, live_count, counts, jobs=()):
    width = values.shape[1]
    total = jnp.sum(values * live_mask, axis=0)
    own_mean = (total.reshape(-1, LANES) / live_count).reshape(width)
    deviation = (values - own_mean) * live_mask
    spread = jnp.sum(deviation * deviation, axis=0)
    counted, total, spread, counts = pool_all(sizes, live_count, total, spread, counts, jobs)
    inv_std = lax.rsqrt(spread / counted + norm_eps).reshape(width)
    centre = (total / counted).reshape(width)
    return ((values - centre) * inv_std, inv_std, counted, counts)


def norm_back(sizes, upstream, normed, gain_part, inv_std, live_mask, counted, jobs=()):
    width = upstream.shape[1]
    sums = sum_rounds(
        sizes,
        jnp.stack(
            [
                jnp.sum(upstream * normed, axis=0).reshape(-1, LANES),
                jnp.sum(upstream, axis=0).reshape(-1, LANES),
            ]
        ),
        all_rounds(sizes),
        jobs,
    )
    mean_gain = (sums[0] / counted).reshape(width)
    mean_shift = (sums[1] / counted).reshape(width)
    grad_act = live_mask * (gain_part * inv_std) * (upstream - (mean_shift + normed * mean_gain))
    return (grad_act.astype(jnp.bfloat16), sums[0].reshape(width), sums[1].reshape(width))


def orders(size):
    down = bits_of(size)[::-1]
    return (down, down[:-2] + down[:-3:-1])


def crossing(sizes, step):
    pair = orders(sizes[1])
    return [
        (dp * sizes[1] + place, dp * sizes[1] + (place ^ pair[dp & 1][step]))
        for dp in range(sizes[0])
        for place in range(sizes[1])
    ]


def apart_of(sizes, core, slot):
    masks = []
    for order in orders(sizes[1]):
        mask = 0
        for k, bit in enumerate(order):
            if slot >> k & 1:
                mask ^= bit
        masks.append(mask)
    return jnp.where(core == 0, masks[0], masks[1])


def pick(blocks, index):
    return lax.dynamic_index_in_dim(blocks, index, 0, keepdims=True)


def settle_kernel(sizes, starts, *refs):
    outs, pieces = refs[-len(starts) :], refs[: -len(starts)]
    core, place = lax.axis_index("dp") & 1, lax.axis_index("wide")
    per_core = len(pieces) // 2
    for part, piece in enumerate(pieces):
        half = core if part < per_core else 1 - core
        for block in range(piece.shape[0]):
            slot = block + (part % per_core) * piece.shape[0]
            target = (place ^ apart_of(sizes, half, slot)) * 2 + half
            for start, out in zip(starts, outs):
                out[target] = piece[block, start : start + out.shape[1]]


def settle(sizes, pieces, heights):
    width = pieces[0].shape[2]
    count = 2 * sizes[1]
    starts = [sum(heights[:k]) for k in range(len(heights))]
    return pl.pallas_call(
        functools.partial(settle_kernel, sizes, starts),
        in_specs=[pl.BlockSpec(memory_space=pltpu.VMEM)] * len(pieces),
        out_specs=[pl.BlockSpec(memory_space=pltpu.VMEM)] * len(heights),
        out_shape=[
            jax.ShapeDtypeStruct((count, height, width), pieces[0].dtype) for height in heights
        ],
        compiler_params=pltpu.CompilerParams(vmem_limit_bytes=12 * 2**20),
        cost_estimate=pl.CostEstimate(
            flops=0, bytes_accessed=4 * count * sum(heights) * width, transcendentals=0
        ),
    )(*pieces)


def halves_of(shard):
    return shard.reshape(2, shard.shape[0] // 2, shard.shape[1])


def ring_own(shards):
    return pick(jnp.concatenate(shards, axis=1), lax.axis_index("dp") & 1)


def ring_step(sizes, held, step):
    return lax.ppermute(held, BOTH, crossing(sizes, step))


def ring_pieces(sizes, held, got):
    pieces = [held, got]
    return pieces + [swap_dp(sizes, piece, 1) for piece in pieces]


def ring_end(sizes, held, got, heights):
    return settle(sizes, ring_pieces(sizes, held, got), heights)


def third_halves(expand, heads):
    parts = halves_of(expand)
    four = jnp.concatenate(
        [parts[:, :, part * C_MID : (part + 1) * C_MID] for part in range(4)], axis=1
    )
    return jnp.concatenate([four, halves_of(heads)], axis=2)


def third_kernel(sizes, own_ref, other_ref, expand_ref, heads_ref):
    core, place = lax.axis_index("dp") & 1, lax.axis_index("wide")
    side = lax.axis_index("dp") >> 1 & 1
    rows, count = expand_ref.shape[1], own_ref.shape[0] // 2
    for half, piece in ((core, own_ref), (1 - core, other_ref)):
        for turn in range(2):
            quarter = side if turn == 0 else 1 - side
            for slot in range(count):
                block = turn * count + slot
                target = (place ^ apart_of(sizes, half, slot)) * 2 + half
                for part in range(2):
                    start = pl.multiple_of((2 * quarter + part) * C_MID, C_MID)
                    expand_ref[target, :, pl.ds(start, C_MID)] = piece[
                        block, part * rows : (part + 1) * rows, :C_MID
                    ]
                start = pl.multiple_of(quarter * 2 * rows, 2 * rows)
                heads_ref[target, pl.ds(start, 2 * rows)] = piece[block, :, C_MID:]


def settle_third(sizes, own, other):
    _, rows, width = own.shape
    count = 2 * sizes[1]
    return pl.pallas_call(
        functools.partial(third_kernel, sizes),
        in_specs=[pl.BlockSpec(memory_space=pltpu.VMEM)] * 2,
        out_specs=[pl.BlockSpec(memory_space=pltpu.VMEM)] * 2,
        out_shape=[
            jax.ShapeDtypeStruct((count, rows // 2, 4 * C_MID), own.dtype),
            jax.ShapeDtypeStruct((count, 2 * rows, width - C_MID), own.dtype),
        ],
        compiler_params=pltpu.CompilerParams(vmem_limit_bytes=12 * 2**20),
        cost_estimate=pl.CostEstimate(
            flops=0, bytes_accessed=8 * count * rows * width, transcendentals=0
        ),
    )(own, other)


def part_kernel(sizes, blocks_ref, sent_ref, kept_ref):
    core, place = lax.axis_index("dp") & 1, lax.axis_index("wide")
    for slot in range(sent_ref.shape[0]):
        source = (place ^ apart_of(sizes, 1 - core, slot)) * 2 + 1 - core
        sent_ref[slot] = blocks_ref[source].astype(sent_ref.dtype)
        kept_ref[slot] = blocks_ref[(place ^ apart_of(sizes, core, slot)) * 2 + core]


def part(sizes, blocks):
    _, rows, width = blocks.shape
    shape = (sizes[1], rows, width)
    return pl.pallas_call(
        functools.partial(part_kernel, sizes),
        in_specs=[pl.BlockSpec(memory_space=pltpu.VMEM)],
        out_specs=[pl.BlockSpec(memory_space=pltpu.VMEM)] * 2,
        out_shape=[
            jax.ShapeDtypeStruct(shape, jnp.bfloat16),
            jax.ShapeDtypeStruct(shape, jnp.float32),
        ],
        compiler_params=pltpu.CompilerParams(
            vmem_limit_bytes=14 * sizes[1] * rows * width + 2**21
        ),
        cost_estimate=pl.CostEstimate(
            flops=0, bytes_accessed=14 * sizes[1] * rows * width, transcendentals=0
        ),
    )(blocks)


def join_kernel(held_ref, got_ref, sent_ref, kept_ref):
    half = sent_ref.shape[0]
    for slot in range(half):
        kept_ref[slot] = held_ref[slot] + got_ref[slot].astype(jnp.float32)
        sent_ref[slot] = (
            held_ref[half + slot] + got_ref[half + slot].astype(jnp.float32)
        ).astype(sent_ref.dtype)


def join(held, got):
    count, rows, width = got.shape
    shape = (count // 2, rows, width)
    return pl.pallas_call(
        join_kernel,
        in_specs=[pl.BlockSpec(memory_space=pltpu.VMEM)] * 2,
        out_specs=[pl.BlockSpec(memory_space=pltpu.VMEM)] * 2,
        out_shape=[
            jax.ShapeDtypeStruct(shape, jnp.bfloat16),
            jax.ShapeDtypeStruct(shape, jnp.float32),
        ],
        compiler_params=pltpu.CompilerParams(vmem_limit_bytes=9 * count * rows * width + 2**21),
        cost_estimate=pl.CostEstimate(
            flops=count * rows * width, bytes_accessed=9 * count * rows * width, transcendentals=0
        ),
    )(held, got)


class Scatter:
    def __init__(self, sizes, grads):
        self.sizes, self.step = sizes, len(bits_of(sizes[1]))
        count, rows, width = grads.shape
        self.sent, self.held = part(sizes, grads.reshape(count * 2, rows // 2, width))
        self.got = swap_dp(sizes, self.sent, 1)

    def go(self, token=None):
        got = self.got if token is None else after(token, self.got)
        self.sent, self.held = join(self.held, got)
        self.step -= 1
        self.got = ring_step(self.sizes, self.sent, self.step)
        return self.sent

    def cross(self, token):
        while self.step:
            self.go()
        got = after(token, self.got)
        self.held = (self.held[0] + got[0].astype(jnp.float32)).astype(jnp.bfloat16)
        self.others = bits_of(self.sizes[0])[1:]
        self.got = swap_dp(self.sizes, self.held, self.others[0])

    def close(self):
        held, got = self.held, self.got
        for bit in self.others[1:]:
            held = (held.astype(jnp.float32) + got.astype(jnp.float32)).astype(jnp.bfloat16)
            got = swap_dp(self.sizes, held, bit)
        held = held.astype(jnp.float32) + got.astype(jnp.float32)
        other = swap_dp(self.sizes, held, 1)
        return jnp.where(
            lax.axis_index("dp") & 1 == 0,
            jnp.concatenate([held, other], axis=0),
            jnp.concatenate([other, held], axis=0),
        )


def neighbours(rows, image_slots, crop_slots):
    width = rows.shape[1]
    cut = image_slots * SIDE * SIDE
    images = jnp.pad(
        rows[:cut].reshape(SIDE, SIDE, image_slots, width), ((1, 1), (1, 1), (0, 0), (0, 0))
    )
    crops = jnp.pad(
        rows[cut:].reshape(CROP_SIDE, CROP_SIDE, crop_slots, width),
        ((1, 1), (1, 1), (0, 0), (0, 0)),
    )
    return [
        jnp.concatenate(
            [
                images[oy : oy + SIDE, ox : ox + SIDE].reshape(-1, width),
                crops[oy : oy + CROP_SIDE, ox : ox + CROP_SIDE].reshape(-1, width),
            ],
            axis=0,
        )
        for oy in range(3)
        for ox in range(3)
    ]


def conv_back(rows, weights, image_slots, crop_slots):
    cut, width = image_slots * SIDE * SIDE, rows.shape[1]
    kernel = weights.reshape(3, 3, width, width)[::-1, ::-1]
    parts = []
    for part, side, slots in ((rows[:cut], SIDE, image_slots), (rows[cut:], CROP_SIDE, crop_slots)):
        got = lax.conv_general_dilated(
            part.reshape(side, side, slots, width),
            kernel,
            (1, 1),
            "SAME",
            dimension_numbers=("HWNC", "HWOI", "HWNC"),
            preferred_element_type=jnp.float32,
        )
        parts.append(got.reshape(side * side * slots, width))
    return jnp.concatenate(parts, axis=0)


def drop_kernel(cot_ref, heads_ref, thresh_ref, *rest):
    out_ref = rest[-1]
    half_scale, half_temper = 0.5 / soft_scale, 0.5 / purity_temper
    together, magnitude, leaning = 0.0, 0.0, 0.0
    for task in range(TASKS):
        columns = slice(task * HEAD, (task + 1) * HEAD)
        part = lax.dot_general(
            cot_ref[:, columns],
            heads_ref[:, columns],
            (((1,), (1,)), ((), ())),
            preferred_element_type=jnp.float32,
        )
        square = part * part + soft_scale * soft_scale
        together = together + part
        magnitude = magnitude + square * lax.rsqrt(square)
        leaning = leaning + part * jnp.tanh(part * half_scale)
    lean = (
        thresh_ref[...].astype(jnp.float32) * -half_temper
        + 0.5 * half_temper
        + (together * (0.5 * half_temper)) / magnitude
    )
    out_ref[...] = 0.5 * (together + jnp.tanh(lean) * leaning)


DROP_TILE = 256


def soft_drop(cot_live, heads_full, thresh, skip, first, count, into=None):
    rows, width = thresh.shape[0], heads_full.shape[0]
    more = [] if into is None else [into]
    return pl.pallas_call(
        drop_kernel,
        grid=(count,),
        in_specs=[
            pl.BlockSpec((rows, TASKS * HEAD), lambda i: (0, 0)),
            pl.BlockSpec((DROP_TILE, TASKS * HEAD), lambda i: (first + i, 0)),
            pl.BlockSpec((rows, DROP_TILE), lambda i: (0, skip + i)),
        ]
        + [pl.BlockSpec(memory_space=pl.ANY)] * len(more),
        out_specs=pl.BlockSpec((rows, DROP_TILE), lambda i: (0, first + i)),
        out_shape=jax.ShapeDtypeStruct((rows, width), jnp.float32),
        input_output_aliases={3: 0} if more else {},
        compiler_params=pltpu.CompilerParams(vmem_limit_bytes=16 * 2**20),
        cost_estimate=pl.CostEstimate(
            flops=2 * rows * count * DROP_TILE * TASKS * HEAD,
            bytes_accessed=6 * rows * count * DROP_TILE,
            transcendentals=8 * rows * count * DROP_TILE,
        ),
    )(cot_live, heads_full, thresh, *more)


def slot_source(image_slots, crop_slots):
    def part(slots, pixels, start):
        return (jnp.arange(slots)[None, :] * pixels + jnp.arange(pixels)[:, None]).reshape(-1) + start

    images = image_slots * SIDE * SIDE
    return jnp.concatenate(
        [part(image_slots, SIDE * SIDE, 0), part(crop_slots, CROP_SIDE * CROP_SIDE, images)]
    )


def local(
    sizes,
    images,
    crop_pixels,
    thresholds,
    cotangent,
    image_count,
    crop_count,
    reduce_weight,
    spatial_weight,
    expand_weight,
    heads_weight,
    norm_gains,
    norm_shifts,
    first_reduce,
    first_spatial,
    first_expand,
    first_heads,
    first_norm,
    second_reduce,
    second_spatial,
    second_expand,
    second_heads,
    second_norm,
):
    low = jnp.bfloat16
    image_slots, crop_slots = images.shape[0], crop_pixels.shape[0]
    image_rows = image_slots * SIDE * SIDE
    rows = image_rows + crop_slots * CROP_SIDE * CROP_SIDE
    places = sizes[1]
    reorder = (
        slot_source(image_slots, crop_slots)[:, None] == jnp.arange(rows)[None, :]
    ).astype(low)

    norm_width = norm_gains.shape[0]
    norms = jnp.pad(
        jnp.stack([norm_gains, norm_shifts]).astype(low)[:, None],
        ((0, 0), (0, 15), (0, C_MID - norm_width)),
    )
    device = lax.axis_index("dp")
    third_own = third_halves(expand_weight.astype(low), heads_weight.astype(low))
    third_held = pick(
        third_own.reshape(4, third_own.shape[1] // 2, third_own.shape[2]),
        (device & 1) * 2 + (device >> 1 & 1),
    )
    first_shards = [halves_of(reduce_weight.astype(low)), norms]
    first_held = ring_own(first_shards)
    second_held = ring_own([halves_of(spatial_weight.astype(low))])

    live_mask = jnp.concatenate(
        [
            jnp.tile(jnp.arange(image_slots) < image_count[0], SIDE * SIDE),
            jnp.tile(jnp.arange(crop_slots) < crop_count[0], CROP_SIDE * CROP_SIDE),
        ]
    ).astype(jnp.float32)[:, None]
    live_count = jnp.broadcast_to(
        (image_count * (SIDE * SIDE) + crop_count * (CROP_SIDE * CROP_SIDE)).astype(jnp.float32)[
            None, :
        ],
        (1, LANES),
    )
    made = {}

    def make_inputs(token):
        image_part, crop_part = after(token, (images, crop_pixels))
        made["inputs"] = jnp.concatenate(
            [
                image_part.transpose(1, 2, 0, 3).reshape(image_rows, C_IN),
                crop_part.transpose(1, 2, 0, 3).reshape(-1, C_IN),
            ],
            axis=0,
        )
        return made["inputs"]

    def make_cotangent(token):
        made["cot"] = jnp.dot(
            reorder, after(token, cotangent), preferred_element_type=jnp.float32
        ).astype(low) * live_mask.astype(low)
        return made["cot"]

    def make_thresh(first, count):
        def job(token):
            columns = slice(first * DROP_TILE, (first + count) * DROP_TILE)
            made["thresh", first] = jnp.dot(
                reorder, after(token, thresholds[:, columns]), preferred_element_type=jnp.float32
            ).astype(low)
            return made["thresh", first]

        return job

    steps = len(bits_of(sizes[1]))
    for step in range(steps):
        job = {0: make_inputs, 1: make_cotangent}.get(step)
        first_got = beside(job, first_held, ring_step(sizes, first_held, step))
        if step == 0:
            second_held = after(first_got, second_held)
            second_got = ring_step(sizes, second_held, 0)
        if step < steps - 1:
            first_held = jnp.concatenate([first_held, first_got], axis=0)
    inputs, cot_live = made["inputs"], made["cot"]
    second_held = jnp.concatenate([second_held, after(first_got, second_got)], axis=0)
    inputs, second_held = lax.optimization_barrier((inputs, second_held))
    second_got = ring_step(sizes, second_held, 1)
    reduce_full, norms_full = ring_end(
        sizes, first_held, first_got, [shard.shape[1] for shard in first_shards]
    )
    reduce_full = reduce_full.reshape(C_IN, C_MID)
    norms_full = norms_full[:, 0, :norm_width].reshape(places, 2, norm_width)
    gain_full = norms_full[:, 0].reshape(-1).astype(jnp.float32)
    shift_full = norms_full[:, 1].reshape(-1).astype(jnp.float32)
    first_act = jnp.dot(inputs, reduce_full, preferred_element_type=jnp.float32)
    second_got = after(first_act, second_got)
    for step in range(2, steps):
        second_held = jnp.concatenate([second_held, second_got], axis=0)
        second_got = ring_step(sizes, second_held, step)

    def make_spatial(token):
        made["got"] = after(token, second_got)
        return made["got"]

    normed_one, inv_one, counted, counts = batch_norm(
        sizes, first_act, live_mask, live_count, None, [None, None, make_spatial]
    )
    (spatial_full,) = ring_end(sizes, second_held, made["got"], [second_held.shape[1]])
    spatial_full = spatial_full.reshape(9 * C_MID, C_MID)
    pre_one = normed_one * gain_full[:C_MID] + shift_full[:C_MID]
    hidden_one = jax.nn.silu(pre_one).astype(low)
    third_held = after(made["got"], third_held)
    third_got = ring_step(sizes, third_held, 0)
    hidden_one, spatial_full, third_got = lax.optimization_barrier(
        (hidden_one, spatial_full, third_got)
    )
    third_held = jnp.concatenate([third_held, third_got], axis=0)
    third_got = ring_step(sizes, third_held, 1)
    shifted = neighbours(hidden_one, image_slots, crop_slots)
    shifted, third_got = lax.optimization_barrier((shifted, third_got))
    for step in range(2, steps):
        third_held = jnp.concatenate([third_held, third_got], axis=0)
        third_got = ring_step(sizes, third_held, step)
    second_act = jnp.dot(
        jnp.concatenate(shifted, axis=1), spatial_full, preferred_element_type=jnp.float32
    )
    second_act, third_got = lax.optimization_barrier((second_act, third_got))
    third_near = swap_dp(sizes, third_held, 2)

    def cross_third(token):
        made["far"] = swap_dp(sizes, after(token, third_got), 2)
        return third_near

    def swap_third(token):
        near, far = after(token, (third_near, made["far"]))
        made["own"] = jnp.concatenate([third_held, third_got, near, far], axis=0)
        made["other"] = swap_dp(sizes, made["own"], 1)
        return made["own"]

    def make_drop(first, count):
        def job(token):
            cot, into = after(token, (cot_live, made.get("drop")))
            start = max(part for part in (0, 3, 6) if part <= first)
            made["drop"] = soft_drop(
                cot, heads_full, made["thresh", start], first - start, first, count, into
            )
            return made["drop"]

        return job

    normed_two, inv_two, counted, _ = batch_norm(
        sizes,
        second_act,
        live_mask,
        live_count,
        counts,
        [
            both_jobs(cross_third, make_thresh(0, 3)),
            make_thresh(3, 3),
            both_jobs(swap_third, make_thresh(6, 2)),
        ],
    )
    pre_two = normed_two * gain_full[C_MID : 2 * C_MID] + shift_full[C_MID : 2 * C_MID]
    hidden_two = jax.nn.silu(pre_two).astype(low)
    expand_full, heads_full = settle_third(sizes, made["own"], made["other"])
    expand_full = expand_full.reshape(C_MID, C_IN)
    heads_full = heads_full.reshape(C_IN, TASKS * HEAD)
    third_act = jnp.dot(hidden_two, expand_full, preferred_element_type=jnp.float32)
    normed_three, inv_three, counted, _ = batch_norm(
        sizes,
        third_act,
        live_mask,
        live_count,
        counts,
        [make_drop(0, 3), make_drop(3, 3), make_drop(6, 2)],
    )
    combined = made["drop"]
    summed = (
        normed_three * gain_full[2 * C_MID :] + shift_full[2 * C_MID :] + inputs.astype(jnp.float32)
    )
    trunk = jax.nn.silu(summed).astype(low)
    upstream = combined * silu_slope(summed)

    def make_heads(token):
        made["heads"] = jnp.dot(
            after(token, trunk).T, cot_live, preferred_element_type=jnp.float32
        )
        return made["heads"]

    def make_predictions(token):
        made["predictions"] = (
            jnp.dot(after(token, trunk), heads_full, preferred_element_type=jnp.float32) * live_mask
        ).astype(low)
        return made["predictions"]

    grad_three, gain_three, shift_three = norm_back(
        sizes,
        upstream,
        normed_three,
        gain_full[2 * C_MID :],
        inv_three,
        live_mask,
        counted,
        [None, make_heads, make_predictions],
    )
    heads = Scatter(sizes, made["heads"].reshape(places, -1, TASKS * HEAD))
    grad_three, _ = lax.optimization_barrier((grad_three, heads.go()))
    back_two = jnp.dot(grad_three, expand_full.T, preferred_element_type=jnp.float32) * silu_slope(
        pre_two
    )

    def make_expand(token):
        grad_expand = jnp.dot(
            hidden_two.T, after(token, grad_three), preferred_element_type=jnp.float32
        )
        made["expand"] = Scatter(sizes, grad_expand.reshape(places, -1, C_IN))
        return made["expand"].sent

    grad_two, gain_two, shift_two = norm_back(
        sizes,
        back_two,
        normed_two,
        gain_full[C_MID : 2 * C_MID],
        inv_two,
        live_mask,
        counted,
        [make_expand, heads.go, heads.go],
    )
    expand = made["expand"]
    grad_two, _ = lax.optimization_barrier((grad_two, expand.go()))
    grad_spatial = [
        jnp.dot(piece.T, grad_two, preferred_element_type=jnp.float32) for piece in shifted[:5]
    ]
    grad_spatial, heads.got = lax.optimization_barrier((grad_spatial, heads.got))
    grad_late = after(heads.got, grad_two)
    grad_spatial += [
        jnp.dot(piece.T, grad_late, preferred_element_type=jnp.float32) for piece in shifted[5:]
    ]
    grad_spatial = jnp.concatenate(grad_spatial, axis=0)
    spatial = Scatter(sizes, grad_spatial.reshape(places, -1, C_MID))
    grad_two, _ = lax.optimization_barrier((grad_two, (spatial.sent, expand.go())))
    back_one = conv_back(grad_two, spatial_full, image_slots, crop_slots) * silu_slope(pre_one)
    back_one, _ = lax.optimization_barrier((back_one, (spatial.go(), expand.go())))
    grad_one, gain_one, shift_one = norm_back(
        sizes,
        back_one,
        normed_one,
        gain_full[:C_MID],
        inv_one,
        live_mask,
        counted,
    )
    grad_one, _ = lax.optimization_barrier((grad_one, (spatial.go(), expand.got)))
    grad_reduce = jnp.dot(inputs.T, grad_one, preferred_element_type=jnp.float32)

    grad_reduce, spatial.got = lax.optimization_barrier((grad_reduce, spatial.got))
    spatial.go()
    grad_reduce = after(spatial.sent, grad_reduce)
    reduce = Scatter(sizes, grad_reduce.reshape(places, -1, C_MID))
    reduce.go()

    heads.cross(reduce.sent)
    expand.cross(reduce.sent)
    back = reduce_full.T
    grad_late, upstream_late = after(reduce.sent, (grad_one, upstream))
    grad_images = (
        jnp.dot(grad_late[:image_rows], back, preferred_element_type=jnp.float32)
        + upstream_late[:image_rows]
    ).astype(low)
    reduce.got, heads.got, expand.got, grad_images = lax.optimization_barrier(
        (reduce.got, heads.got, expand.got, grad_images)
    )
    grad_images = grad_images.reshape(SIDE, SIDE, image_slots, C_IN).transpose(2, 0, 1, 3)
    reduce.go()

    spatial.cross(reduce.sent)
    predictions = lax.dot_general(
        reorder,
        after(reduce.sent, made["predictions"]),
        (((0,), (0,)), ((), ())),
        preferred_element_type=jnp.float32,
    ).astype(low)
    reduce.got, predictions = lax.optimization_barrier((reduce.got, predictions))
    reduce.go()

    grad_late, upstream_late = after(reduce.sent, (grad_one, upstream))
    grad_crops = (
        jnp.dot(grad_late[image_rows:], back, preferred_element_type=jnp.float32)
        + upstream_late[image_rows:]
    ).astype(low)
    shard_heads, shard_expand = heads.close(), expand.close()
    reduce.got, spatial.got, shard_heads, shard_expand, grad_crops = lax.optimization_barrier(
        (reduce.got, spatial.got, shard_heads, shard_expand, grad_crops)
    )
    grad_crops = grad_crops.reshape(CROP_SIDE, CROP_SIDE, crop_slots, C_IN).transpose(2, 0, 1, 3)
    shard_spatial = spatial.close()
    reduce.cross(reduce.sent)
    shard_reduce = reduce.close()

    gain_one, gain_two, gain_three, shift_one, shift_two, shift_three = after(
        reduce.sent, (gain_one, gain_two, gain_three, shift_one, shift_two, shift_three)
    )
    norm_grads = jnp.stack(
        [
            jnp.concatenate([gain_one, gain_two, gain_three]),
            jnp.concatenate([shift_one, shift_two, shift_three]),
        ]
    )
    norm_shard = lax.dynamic_slice_in_dim(
        norm_grads, lax.axis_index("wide") * norm_width, norm_width, 1
    )
    local_squares = (
        jnp.sum(jnp.square(shard_reduce), axis=0)
        + jnp.sum(jnp.square(shard_spatial), axis=0)
        + jnp.sum(jnp.square(shard_expand).reshape(-1, C_MID), axis=0)
        + jnp.pad(jnp.sum(jnp.square(shard_heads), axis=0), (0, C_MID - TASKS * HEAD))
    )
    squares = jnp.sum(
        sum_rounds(
            sizes,
            local_squares.reshape(-1, LANES),
            [(swap_wide, masks) for masks in rounds_of(sizes[1])],
        )
    ) + jnp.sum(jnp.square(norm_grads))
    norm_before = jnp.sqrt(squares)
    factor = clip_bound / jnp.maximum(norm_before, clip_bound)
    new_reduce, moment_reduce, square_reduce = adamw_step(
        reduce_weight, shard_reduce * factor, first_reduce, second_reduce, weight_rate, weight_decay
    )
    new_spatial, moment_spatial, square_spatial = adamw_step(
        spatial_weight,
        shard_spatial * factor,
        first_spatial,
        second_spatial,
        weight_rate,
        weight_decay,
    )
    new_expand, moment_expand, square_expand = adamw_step(
        expand_weight, shard_expand * factor, first_expand, second_expand, weight_rate, weight_decay
    )
    new_heads, moment_heads, square_heads = adamw_step(
        heads_weight, shard_heads * factor, first_heads, second_heads, weight_rate, weight_decay
    )
    new_norm, moment_norm, square_norm = adamw_step(
        jnp.stack([norm_gains, norm_shifts]),
        norm_shard * factor,
        first_norm,
        second_norm,
        norm_rate,
        0.0,
    )
    return (
        norm_before,
        predictions,
        grad_images,
        grad_crops,
        new_reduce,
        new_spatial,
        new_expand,
        new_heads,
        new_norm,
        moment_reduce,
        moment_spatial,
        moment_expand,
        moment_heads,
        moment_norm,
        square_reduce,
        square_spatial,
        square_expand,
        square_heads,
        square_norm,
    )


def solution(mesh):
    sizes = (mesh.shape["dp"], mesh.shape["wide"])
    return jax.shard_map(
        functools.partial(local, sizes),
        mesh=mesh,
        in_specs=(
            P(("dp", "wide"), None, None, None),
            P(("dp", "wide"), None, None, None),
            P(("dp", "wide"), None),
            P(("dp", "wide"), None),
            P(("dp", "wide")),
            P(("dp", "wide")),
            P("wide", None),
            P("wide", None),
            P("wide", None),
            P("wide", None),
            P("wide"),
            P("wide"),
            P("wide", None),
            P("wide", None),
            P("wide", None),
            P("wide", None),
            P(None, "wide"),
            P("wide", None),
            P("wide", None),
            P("wide", None),
            P("wide", None),
            P(None, "wide"),
        ),
        out_specs=(
            P(),
            P(("dp", "wide"), None),
            P(("dp", "wide"), None, None, None),
            P(("dp", "wide"), None, None, None),
            P("wide", None),
            P("wide", None),
            P("wide", None),
            P("wide", None),
            P(None, "wide"),
            P("wide", None),
            P("wide", None),
            P("wide", None),
            P("wide", None),
            P(None, "wide"),
            P("wide", None),
            P("wide", None),
            P("wide", None),
            P("wide", None),
            P(None, "wide"),
        ),
        check_vma=False,
    )
```

```python
import functools

import jax
import jax.numpy as jnp
from jax import lax
from jax.experimental import pallas as pl
from jax.experimental.pallas import tpu as pltpu
from jax.sharding import PartitionSpec as P

C_IN = 2048
C_MID = 512
HEAD = 128
TASKS = 3
SIDE = 7
CROP_SIDE = 2
STEP = 10
IMG_CAP = 24
CROP_CAP = 16


norm_eps = 1e-05
soft_scale = 0.05
purity_temper = 0.1
clip_bound = 1.0
first_decay = 0.9
second_decay = 0.999
adam_eps = 1e-08
weight_rate = 0.02
norm_rate = 0.5
weight_decay = 0.1


def silu_slope(values):
    sigma = jax.nn.sigmoid(values)
    return sigma * (1.0 + values * (1.0 - sigma))


def soft_drop(task_grads, thresh):
    together = task_grads[0]
    magnitude = jnp.sqrt(task_grads[0] * task_grads[0] + soft_scale * soft_scale)
    for further in task_grads[1:]:
        together = together + further
        magnitude = magnitude + jnp.sqrt(further * further + soft_scale * soft_scale)
    purity = 0.5 * (1.0 + together / magnitude)
    upward = jax.nn.sigmoid((purity - thresh) / purity_temper)
    combined = jnp.zeros_like(together)
    for grad_part in task_grads:
        keeping = upward * jax.nn.sigmoid(grad_part / soft_scale) + (1.0 - upward) * jax.nn.sigmoid(
            -grad_part / soft_scale
        )
        combined = combined + grad_part * keeping
    return combined


def adamw_step(weights, gradient, moment, square, step_rate, decay_rate):
    moment_new = first_decay * moment + (1.0 - first_decay) * gradient
    square_new = second_decay * square + (1.0 - second_decay) * gradient * gradient
    moment_hat = moment_new / (1.0 - first_decay**STEP)
    square_hat = square_new / (1.0 - second_decay**STEP)
    updated = weights - step_rate * (
        moment_hat / (jnp.sqrt(square_hat) + adam_eps) + decay_rate * weights
    )
    return (updated, moment_new, square_new)


BOTH = ("dp", "wide")
LANES = 128


def bits_of(size):
    return [1 << k for k in range(size.bit_length() - 1)]


def swap_dp(sizes, values, mask):
    return lax.ppermute(values, "dp", [(i, i ^ mask) for i in range(sizes[0])])


def swap_wide(sizes, values, mask):
    return lax.ppermute(values, "wide", [(i, i ^ mask) for i in range(sizes[1])])


def rounds_of(size):
    left = bits_of(size)[::-1]
    rounds = []
    while left:
        pair, left = left[:2], left[2:]
        rounds.append((pair[1], pair[0], pair[0] | pair[1]) if len(pair) == 2 else (pair[0],))
    return rounds


def all_rounds(sizes):
    return [(swap_dp, masks) for masks in rounds_of(sizes[0])] + [
        (swap_wide, masks) for masks in rounds_of(sizes[1])
    ]


def beside(job, token, got):
    if job is None:
        return got
    return lax.optimization_barrier((got, job(token)))[0]


def after(token, values):
    return lax.optimization_barrier((values, token))[0]


def both_jobs(one, other):
    return lambda token: (one(token), other(token))


def sum_rounds(sizes, values, rounds, jobs=()):
    for level, (swap, masks) in enumerate(rounds):
        got = [swap(sizes, values, mask) for mask in masks]
        got = beside(jobs[level] if level < len(jobs) else None, values, got)
        if len(masks) == 3:
            values = (values + got[0]) + (got[1] + got[2])
        else:
            values = values + got[0]
    return values


def pool(first, second):
    count_a, total_a, spread_a = first
    count_b, total_b, spread_b = second
    count = count_a + count_b
    apart = total_a / count_a - total_b / count_b
    weight = count_a * count_b / count
    return (count, total_a + total_b, (spread_a + spread_b) + (apart * apart) * weight)


def pool_all(sizes, count, total, spread, counts, jobs):
    seen = []
    total, spread = total.reshape(-1, LANES), spread.reshape(-1, LANES)
    for level, (swap, masks) in enumerate(all_rounds(sizes)):
        parts = [total, spread]
        if counts is None:
            parts.append(jnp.broadcast_to(count, total.shape))
        packet = jnp.stack(parts)
        got = [swap(sizes, packet, mask) for mask in masks]
        got = beside(jobs[level] if level < len(jobs) else None, packet, got)
        seen.append((count, [g[2, :1] for g in got]) if counts is None else counts[level])
        sets = [(seen[-1][0], total, spread)] + [
            (c, g[0], g[1]) for c, g in zip(seen[-1][1], got)
        ]
        if len(sets) == 4:
            sets = [pool(sets[0], sets[1]), pool(sets[2], sets[3])]
        count, total, spread = pool(sets[0], sets[1])
    return (count, total, spread, seen)


def own_moments(values, live_mask, live_count):
    total = jnp.sum(values * live_mask, axis=0)
    own_mean = (total.reshape(-1, LANES) / live_count).reshape(values.shape[1])
    deviation = (values - own_mean) * live_mask
    return (total, jnp.sum(deviation * deviation, axis=0))


def batch_norm(sizes, moments, live_count, counts, jobs=()):
    total, spread = moments
    width = total.shape[0]
    counted, total, spread, counts = pool_all(sizes, live_count, total, spread, counts, jobs)
    inv_std = lax.rsqrt(spread / counted + norm_eps).reshape(width)
    return ((total / counted).reshape(width), inv_std, counted, counts)


def norm_back(
    sizes, upstream, normed, gain_part, inv_std, live_mask, counted, jobs=(), again=None
):
    width = upstream.shape[1]
    sums = sum_rounds(
        sizes,
        jnp.stack(
            [
                jnp.sum(upstream * normed, axis=0).reshape(-1, LANES),
                jnp.sum(upstream, axis=0).reshape(-1, LANES),
            ]
        ),
        all_rounds(sizes),
        jobs,
    )
    mean_gain = (sums[0] / counted).reshape(width)
    mean_shift = (sums[1] / counted).reshape(width)
    if again is not None:
        normed = again(mean_gain)
    grad_act = live_mask * (gain_part * inv_std) * (upstream - (mean_shift + normed * mean_gain))
    return (grad_act.astype(jnp.bfloat16), sums[0].reshape(width), sums[1].reshape(width))


def orders(size):
    down = bits_of(size)[::-1]
    return (down, down[:-2] + down[:-3:-1])


def crossing(sizes, step):
    pair = orders(sizes[1])
    return [
        (dp * sizes[1] + place, dp * sizes[1] + (place ^ pair[dp & 1][step]))
        for dp in range(sizes[0])
        for place in range(sizes[1])
    ]


def apart_of(sizes, core, slot):
    masks = []
    for order in orders(sizes[1]):
        mask = 0
        for k, bit in enumerate(order):
            if slot >> k & 1:
                mask ^= bit
        masks.append(mask)
    return jnp.where(core == 0, masks[0], masks[1])


def pick(blocks, index):
    return lax.dynamic_index_in_dim(blocks, index, 0, keepdims=True)


def settle_kernel(sizes, starts, *refs):
    outs, pieces = refs[-len(starts) :], refs[: -len(starts)]
    core, place = lax.axis_index("dp") & 1, lax.axis_index("wide")
    per_core = len(pieces) // 2
    for part, piece in enumerate(pieces):
        half = core if part < per_core else 1 - core
        for block in range(piece.shape[0]):
            slot = block + (part % per_core) * piece.shape[0]
            target = (place ^ apart_of(sizes, half, slot)) * 2 + half
            for start, out in zip(starts, outs):
                out[target] = piece[block, start : start + out.shape[1]]


def settle(sizes, pieces, heights):
    width = pieces[0].shape[2]
    count = 2 * sizes[1]
    starts = [sum(heights[:k]) for k in range(len(heights))]
    return pl.pallas_call(
        functools.partial(settle_kernel, sizes, starts),
        in_specs=[pl.BlockSpec(memory_space=pltpu.VMEM)] * len(pieces),
        out_specs=[pl.BlockSpec(memory_space=pltpu.VMEM)] * len(heights),
        out_shape=[
            jax.ShapeDtypeStruct((count, height, width), pieces[0].dtype) for height in heights
        ],
        compiler_params=pltpu.CompilerParams(vmem_limit_bytes=12 * 2**20),
        cost_estimate=pl.CostEstimate(
            flops=0, bytes_accessed=4 * count * sum(heights) * width, transcendentals=0
        ),
    )(*pieces)


def halves_of(shard):
    return shard.reshape(2, shard.shape[0] // 2, shard.shape[1])


def ring_own(shards):
    return pick(jnp.concatenate(shards, axis=1), lax.axis_index("dp") & 1)


def ring_step(sizes, held, step):
    return lax.ppermute(held, BOTH, crossing(sizes, step))


def ring_pieces(sizes, held, got):
    pieces = [held, got]
    return pieces + [swap_dp(sizes, piece, 1) for piece in pieces]


def ring_end(sizes, held, got, heights):
    return settle(sizes, ring_pieces(sizes, held, got), heights)


def third_halves(expand, heads):
    parts = halves_of(expand)
    four = jnp.concatenate(
        [parts[:, :, part * C_MID : (part + 1) * C_MID] for part in range(4)], axis=1
    )
    return jnp.concatenate([four, halves_of(heads)], axis=2)


def third_kernel(sizes, own_ref, other_ref, expand_ref, heads_ref):
    core, place = lax.axis_index("dp") & 1, lax.axis_index("wide")
    side = lax.axis_index("dp") >> 1 & 1
    rows, count = expand_ref.shape[1], own_ref.shape[0] // 2
    for half, piece in ((core, own_ref), (1 - core, other_ref)):
        for turn in range(2):
            quarter = side if turn == 0 else 1 - side
            for slot in range(count):
                block = turn * count + slot
                target = (place ^ apart_of(sizes, half, slot)) * 2 + half
                for part in range(2):
                    start = pl.multiple_of((2 * quarter + part) * C_MID, C_MID)
                    expand_ref[target, :, pl.ds(start, C_MID)] = piece[
                        block, part * rows : (part + 1) * rows, :C_MID
                    ]
                start = pl.multiple_of(quarter * 2 * rows, 2 * rows)
                heads_ref[target, pl.ds(start, 2 * rows)] = piece[block, :, C_MID:]


def settle_third(sizes, own, other):
    _, rows, width = own.shape
    count = 2 * sizes[1]
    return pl.pallas_call(
        functools.partial(third_kernel, sizes),
        in_specs=[pl.BlockSpec(memory_space=pltpu.VMEM)] * 2,
        out_specs=[pl.BlockSpec(memory_space=pltpu.VMEM)] * 2,
        out_shape=[
            jax.ShapeDtypeStruct((count, rows // 2, 4 * C_MID), own.dtype),
            jax.ShapeDtypeStruct((count, 2 * rows, width - C_MID), own.dtype),
        ],
        compiler_params=pltpu.CompilerParams(vmem_limit_bytes=12 * 2**20),
        cost_estimate=pl.CostEstimate(
            flops=0, bytes_accessed=8 * count * rows * width, transcendentals=0
        ),
    )(own, other)


def part_kernel(sizes, blocks_ref, sent_ref, kept_ref):
    core, place = lax.axis_index("dp") & 1, lax.axis_index("wide")
    for slot in range(sent_ref.shape[0]):
        source = (place ^ apart_of(sizes, 1 - core, slot)) * 2 + 1 - core
        sent_ref[slot] = blocks_ref[source].astype(sent_ref.dtype)
        kept_ref[slot] = blocks_ref[(place ^ apart_of(sizes, core, slot)) * 2 + core]


def part(sizes, blocks):
    _, rows, width = blocks.shape
    shape = (sizes[1], rows, width)
    return pl.pallas_call(
        functools.partial(part_kernel, sizes),
        in_specs=[pl.BlockSpec(memory_space=pltpu.VMEM)],
        out_specs=[pl.BlockSpec(memory_space=pltpu.VMEM)] * 2,
        out_shape=[
            jax.ShapeDtypeStruct(shape, jnp.bfloat16),
            jax.ShapeDtypeStruct(shape, jnp.float32),
        ],
        compiler_params=pltpu.CompilerParams(
            vmem_limit_bytes=14 * sizes[1] * rows * width + 2**21
        ),
        cost_estimate=pl.CostEstimate(
            flops=0, bytes_accessed=14 * sizes[1] * rows * width, transcendentals=0
        ),
    )(blocks)


def join_kernel(held_ref, got_ref, sent_ref, kept_ref):
    half = sent_ref.shape[0]
    for slot in range(half):
        kept_ref[slot] = held_ref[slot] + got_ref[slot].astype(jnp.float32)
        sent_ref[slot] = (
            held_ref[half + slot] + got_ref[half + slot].astype(jnp.float32)
        ).astype(sent_ref.dtype)


def join(held, got):
    count, rows, width = got.shape
    shape = (count // 2, rows, width)
    return pl.pallas_call(
        join_kernel,
        in_specs=[pl.BlockSpec(memory_space=pltpu.VMEM)] * 2,
        out_specs=[pl.BlockSpec(memory_space=pltpu.VMEM)] * 2,
        out_shape=[
            jax.ShapeDtypeStruct(shape, jnp.bfloat16),
            jax.ShapeDtypeStruct(shape, jnp.float32),
        ],
        compiler_params=pltpu.CompilerParams(vmem_limit_bytes=9 * count * rows * width + 2**21),
        cost_estimate=pl.CostEstimate(
            flops=count * rows * width, bytes_accessed=9 * count * rows * width, transcendentals=0
        ),
    )(held, got)


class Scatter:
    def __init__(self, sizes, grads):
        self.sizes, self.step = sizes, len(bits_of(sizes[1]))
        count, rows, width = grads.shape
        self.sent, self.held = part(sizes, grads.reshape(count * 2, rows // 2, width))
        self.got = swap_dp(sizes, self.sent, 1)

    def go(self, token=None):
        got = self.got if token is None else after(token, self.got)
        self.sent, self.held = join(self.held, got)
        self.step -= 1
        self.got = ring_step(self.sizes, self.sent, self.step)
        return self.sent

    def cross(self, token):
        while self.step:
            self.go()
        got = after(token, self.got)
        self.held = (self.held[0] + got[0].astype(jnp.float32)).astype(jnp.bfloat16)
        self.others = bits_of(self.sizes[0])[1:]
        self.got = swap_dp(self.sizes, self.held, self.others[0])

    def close(self):
        held, got = self.held, self.got
        for bit in self.others[1:]:
            held = (held.astype(jnp.float32) + got.astype(jnp.float32)).astype(jnp.bfloat16)
            got = swap_dp(self.sizes, held, bit)
        held = held.astype(jnp.float32) + got.astype(jnp.float32)
        other = swap_dp(self.sizes, held, 1)
        return jnp.where(
            lax.axis_index("dp") & 1 == 0,
            jnp.concatenate([held, other], axis=0),
            jnp.concatenate([other, held], axis=0),
        )


def neighbours(rows, image_slots, crop_slots):
    width = rows.shape[1]
    cut = image_slots * SIDE * SIDE
    images = jnp.pad(
        rows[:cut].reshape(SIDE, SIDE, image_slots, width), ((1, 1), (1, 1), (0, 0), (0, 0))
    )
    crops = jnp.pad(
        rows[cut:].reshape(CROP_SIDE, CROP_SIDE, crop_slots, width),
        ((1, 1), (1, 1), (0, 0), (0, 0)),
    )
    return [
        jnp.concatenate(
            [
                images[oy : oy + SIDE, ox : ox + SIDE].reshape(-1, width),
                crops[oy : oy + CROP_SIDE, ox : ox + CROP_SIDE].reshape(-1, width),
            ],
            axis=0,
        )
        for oy in range(3)
        for ox in range(3)
    ]


def conv_back(rows, weights, side, slots):
    width = rows.shape[1]
    got = lax.conv_general_dilated(
        rows.reshape(side, side, slots, width),
        weights.reshape(3, 3, width, width)[::-1, ::-1],
        (1, 1),
        "SAME",
        dimension_numbers=("HWNC", "HWOI", "HWNC"),
        preferred_element_type=jnp.float32,
    )
    return got.reshape(side * side * slots, width)


def drop_kernel(cot_ref, heads_ref, thresh_ref, *rest):
    out_ref = rest[-1]
    half_scale, half_temper = 0.5 / soft_scale, 0.5 / purity_temper
    together, magnitude, leaning = 0.0, 0.0, 0.0
    for task in range(TASKS):
        columns = slice(task * HEAD, (task + 1) * HEAD)
        part = lax.dot_general(
            cot_ref[:, columns],
            heads_ref[:, columns],
            (((1,), (1,)), ((), ())),
            preferred_element_type=jnp.float32,
        )
        square = part * part + soft_scale * soft_scale
        together = together + part
        magnitude = magnitude + square * lax.rsqrt(square)
        leaning = leaning + part * jnp.tanh(part * half_scale)
    lean = (
        thresh_ref[...].astype(jnp.float32) * -half_temper
        + 0.5 * half_temper
        + (together * (0.5 * half_temper)) / magnitude
    )
    out_ref[...] = 0.5 * (together + jnp.tanh(lean) * leaning)


DROP_TILE = 256


def soft_drop(cot_live, heads_full, thresh, skip, first, count, into=None):
    rows, width = thresh.shape[0], heads_full.shape[0]
    more = [] if into is None else [into]
    return pl.pallas_call(
        drop_kernel,
        grid=(count,),
        in_specs=[
            pl.BlockSpec((rows, TASKS * HEAD), lambda i: (0, 0)),
            pl.BlockSpec((DROP_TILE, TASKS * HEAD), lambda i: (first + i, 0)),
            pl.BlockSpec((rows, DROP_TILE), lambda i: (0, skip + i)),
        ]
        + [pl.BlockSpec(memory_space=pl.ANY)] * len(more),
        out_specs=pl.BlockSpec((rows, DROP_TILE), lambda i: (0, first + i)),
        out_shape=jax.ShapeDtypeStruct((rows, width), jnp.float32),
        input_output_aliases={3: 0} if more else {},
        compiler_params=pltpu.CompilerParams(vmem_limit_bytes=16 * 2**20),
        cost_estimate=pl.CostEstimate(
            flops=2 * rows * count * DROP_TILE * TASKS * HEAD,
            bytes_accessed=6 * rows * count * DROP_TILE,
            transcendentals=8 * rows * count * DROP_TILE,
        ),
    )(cot_live, heads_full, thresh, *more)


def slot_source(image_slots, crop_slots):
    def part(slots, pixels, start):
        return (jnp.arange(slots)[None, :] * pixels + jnp.arange(pixels)[:, None]).reshape(-1) + start

    images = image_slots * SIDE * SIDE
    return jnp.concatenate(
        [part(image_slots, SIDE * SIDE, 0), part(crop_slots, CROP_SIDE * CROP_SIDE, images)]
    )


def local(
    sizes,
    images,
    crop_pixels,
    thresholds,
    cotangent,
    image_count,
    crop_count,
    reduce_weight,
    spatial_weight,
    expand_weight,
    heads_weight,
    norm_gains,
    norm_shifts,
    first_reduce,
    first_spatial,
    first_expand,
    first_heads,
    first_norm,
    second_reduce,
    second_spatial,
    second_expand,
    second_heads,
    second_norm,
):
    low = jnp.bfloat16
    image_slots, crop_slots = images.shape[0], crop_pixels.shape[0]
    image_rows = image_slots * SIDE * SIDE
    rows = image_rows + crop_slots * CROP_SIDE * CROP_SIDE
    places = sizes[1]
    reorder = (
        slot_source(image_slots, crop_slots)[:, None] == jnp.arange(rows)[None, :]
    ).astype(low)

    norm_width = norm_gains.shape[0]
    norms = jnp.pad(
        jnp.stack([norm_gains, norm_shifts]).astype(low)[:, None],
        ((0, 0), (0, 15), (0, C_MID - norm_width)),
    )
    device = lax.axis_index("dp")
    third_own = third_halves(expand_weight.astype(low), heads_weight.astype(low))
    third_held = pick(
        third_own.reshape(4, third_own.shape[1] // 2, third_own.shape[2]),
        (device & 1) * 2 + (device >> 1 & 1),
    )
    first_shards = [halves_of(reduce_weight.astype(low)), norms]
    first_held = ring_own(first_shards)
    second_held = ring_own([halves_of(spatial_weight.astype(low))])

    live_mask = jnp.concatenate(
        [
            jnp.tile(jnp.arange(image_slots) < image_count[0], SIDE * SIDE),
            jnp.tile(jnp.arange(crop_slots) < crop_count[0], CROP_SIDE * CROP_SIDE),
        ]
    ).astype(jnp.float32)[:, None]
    live_count = jnp.broadcast_to(
        (image_count * (SIDE * SIDE) + crop_count * (CROP_SIDE * CROP_SIDE)).astype(jnp.float32)[
            None, :
        ],
        (1, LANES),
    )
    made = {}

    def make_inputs(token):
        image_part, crop_part = after(token, (images, crop_pixels))
        made["inputs"] = jnp.concatenate(
            [
                image_part.transpose(1, 2, 0, 3).reshape(image_rows, C_IN),
                crop_part.transpose(1, 2, 0, 3).reshape(-1, C_IN),
            ],
            axis=0,
        )
        return made["inputs"]

    def make_cotangent(token):
        made["cot"] = jnp.dot(
            reorder, after(token, cotangent), preferred_element_type=jnp.float32
        ).astype(low) * live_mask.astype(low)
        return made["cot"]

    def make_thresh(first, count):
        def job(token):
            columns = slice(first * DROP_TILE, (first + count) * DROP_TILE)
            made["thresh", first] = jnp.dot(
                reorder, after(token, thresholds[:, columns]), preferred_element_type=jnp.float32
            ).astype(low)
            return made["thresh", first]

        return job

    steps = len(bits_of(sizes[1]))
    for step in range(steps):
        job = {0: make_inputs, 1: make_cotangent}.get(step)
        first_got = beside(job, first_held, ring_step(sizes, first_held, step))
        if step == 0:
            second_held = after(first_got, second_held)
            second_got = ring_step(sizes, second_held, 0)
        if step < steps - 1:
            first_held = jnp.concatenate([first_held, first_got], axis=0)
    inputs, cot_live = made["inputs"], made["cot"]
    second_held = jnp.concatenate([second_held, after(first_got, second_got)], axis=0)
    inputs, second_held = lax.optimization_barrier((inputs, second_held))
    second_got = ring_step(sizes, second_held, 1)
    reduce_full, norms_full = ring_end(
        sizes, first_held, first_got, [shard.shape[1] for shard in first_shards]
    )
    reduce_full = reduce_full.reshape(C_IN, C_MID)
    norms_full = norms_full[:, 0, :norm_width].reshape(places, 2, norm_width)
    gain_full = norms_full[:, 0].reshape(-1).astype(jnp.float32)
    shift_full = norms_full[:, 1].reshape(-1).astype(jnp.float32)
    first_act = jnp.dot(inputs, reduce_full, preferred_element_type=jnp.float32)
    second_got = after(first_act, second_got)
    for step in range(2, steps):
        second_held = jnp.concatenate([second_held, second_got], axis=0)
        second_got = ring_step(sizes, second_held, step)

    def make_spatial(token):
        made["got"] = after(token, second_got)
        return made["got"]

    centre_one, inv_one, counted, counts = batch_norm(
        sizes,
        own_moments(first_act, live_mask, live_count),
        live_count,
        None,
        [None, None, make_spatial],
    )
    normed_one = (first_act - centre_one) * inv_one
    (spatial_full,) = ring_end(sizes, second_held, made["got"], [second_held.shape[1]])
    spatial_full = spatial_full.reshape(9 * C_MID, C_MID)
    pre_one = normed_one * gain_full[:C_MID] + shift_full[:C_MID]
    hidden_one = jax.nn.silu(pre_one).astype(low)
    third_held = after(made["got"], third_held)
    third_got = ring_step(sizes, third_held, 0)
    hidden_one, spatial_full, third_got = lax.optimization_barrier(
        (hidden_one, spatial_full, third_got)
    )
    third_held = jnp.concatenate([third_held, third_got], axis=0)
    third_got = ring_step(sizes, third_held, 1)
    shifted = neighbours(hidden_one, image_slots, crop_slots)
    shifted, third_got = lax.optimization_barrier((shifted, third_got))
    for step in range(2, steps):
        third_held = jnp.concatenate([third_held, third_got], axis=0)
        third_got = ring_step(sizes, third_held, step)
    second_act = jnp.dot(
        jnp.concatenate(shifted, axis=1), spatial_full, preferred_element_type=jnp.float32
    )
    second_act, third_got = lax.optimization_barrier((second_act, third_got))
    third_near = swap_dp(sizes, third_held, 2)

    def cross_third(token):
        made["far"] = swap_dp(sizes, after(token, third_got), 2)
        return third_near

    def swap_third(token):
        near, far = after(token, (third_near, made["far"]))
        made["own"] = jnp.concatenate([third_held, third_got, near, far], axis=0)
        made["other"] = swap_dp(sizes, made["own"], 1)
        return made["own"]

    def make_drop(first, count):
        def job(token):
            cot, into = after(token, (cot_live, made.get("drop")))
            start = max(part for part in (0, 3, 6) if part <= first)
            made["drop"] = soft_drop(
                cot, heads_full, made["thresh", start], first - start, first, count, into
            )
            return made["drop"]

        return job

    centre_two, inv_two, counted, _ = batch_norm(
        sizes,
        own_moments(second_act, live_mask, live_count),
        live_count,
        counts,
        [
            both_jobs(cross_third, make_thresh(0, 3)),
            make_thresh(3, 3),
            both_jobs(swap_third, make_thresh(6, 2)),
        ],
    )
    normed_two = (second_act - centre_two) * inv_two
    pre_two = normed_two * gain_full[C_MID : 2 * C_MID] + shift_full[C_MID : 2 * C_MID]
    hidden_two = jax.nn.silu(pre_two).astype(low)
    expand_full, heads_full = settle_third(sizes, made["own"], made["other"])
    expand_full = expand_full.reshape(C_MID, C_IN)
    heads_full = heads_full.reshape(C_IN, TASKS * HEAD)
    def third_product(token):
        return jnp.dot(after(token, hidden_two), expand_full, preferred_element_type=jnp.float32)

    moments = []
    for part in range(4):
        act = jnp.dot(
            hidden_two,
            expand_full[:, part * C_MID : (part + 1) * C_MID],
            preferred_element_type=jnp.float32,
        )
        moments.append(own_moments(act, live_mask, live_count))
    centre_three, inv_three, counted, _ = batch_norm(
        sizes,
        [jnp.concatenate(sums) for sums in zip(*moments)],
        live_count,
        counts,
        [make_drop(0, 3), make_drop(3, 3), make_drop(6, 2)],
    )
    normed_three = (third_product(inv_three) - centre_three) * inv_three
    combined = made["drop"]
    summed = (
        normed_three * gain_full[2 * C_MID :] + shift_full[2 * C_MID :] + inputs.astype(jnp.float32)
    )
    trunk = jax.nn.silu(summed).astype(low)
    upstream = combined * silu_slope(summed)

    def make_heads(token):
        made["heads"] = jnp.dot(
            after(token, trunk).T, cot_live, preferred_element_type=jnp.float32
        )
        return made["heads"]

    def make_predictions(token):
        made["predictions"] = (
            jnp.dot(after(token, trunk), heads_full, preferred_element_type=jnp.float32) * live_mask
        ).astype(low)
        return made["predictions"]

    grad_three, gain_three, shift_three = norm_back(
        sizes,
        upstream,
        normed_three,
        gain_full[2 * C_MID :],
        inv_three,
        live_mask,
        counted,
        [None, make_heads, make_predictions],
        lambda token: (third_product(token) - centre_three) * inv_three,
    )
    heads = Scatter(sizes, made["heads"].reshape(places, -1, TASKS * HEAD))
    grad_three, _ = lax.optimization_barrier((grad_three, heads.go()))
    back_two = jnp.dot(grad_three, expand_full.T, preferred_element_type=jnp.float32) * silu_slope(
        pre_two
    )

    def make_expand(token):
        grad_expand = jnp.dot(
            hidden_two.T, after(token, grad_three), preferred_element_type=jnp.float32
        )
        made["expand"] = Scatter(sizes, grad_expand.reshape(places, -1, C_IN))
        return made["expand"].sent

    grad_two, gain_two, shift_two = norm_back(
        sizes,
        back_two,
        normed_two,
        gain_full[C_MID : 2 * C_MID],
        inv_two,
        live_mask,
        counted,
        [make_expand, heads.go, heads.go],
    )
    expand = made["expand"]
    grad_two, _ = lax.optimization_barrier((grad_two, expand.go()))
    grad_spatial = [
        jnp.dot(piece.T, grad_two, preferred_element_type=jnp.float32) for piece in shifted[:5]
    ]
    grad_spatial, heads.got = lax.optimization_barrier((grad_spatial, heads.got))
    grad_late = after(heads.got, grad_two)
    grad_spatial += [
        jnp.dot(piece.T, grad_late, preferred_element_type=jnp.float32) for piece in shifted[5:]
    ]
    grad_spatial = jnp.concatenate(grad_spatial, axis=0)
    spatial = Scatter(sizes, grad_spatial.reshape(places, -1, C_MID))
    grad_two, _ = lax.optimization_barrier((grad_two, spatial.sent))
    crop_back = conv_back(grad_two[image_rows:], spatial_full, CROP_SIDE, crop_slots)
    crop_back, image_grad, _ = lax.optimization_barrier(
        (crop_back, grad_two[:image_rows], spatial.go(crop_back))
    )
    image_back = conv_back(image_grad, spatial_full, SIDE, image_slots)
    back_one = jnp.concatenate([image_back, crop_back], axis=0) * silu_slope(pre_one)
    back_one, _ = lax.optimization_barrier((back_one, expand.go(image_back)))
    grad_one, gain_one, shift_one = norm_back(
        sizes,
        back_one,
        normed_one,
        gain_full[:C_MID],
        inv_one,
        live_mask,
        counted,
        [None, None, spatial.go],
    )
    grad_reduce = jnp.dot(inputs.T, grad_one, preferred_element_type=jnp.float32)

    grad_reduce, spatial.got, expand.got = lax.optimization_barrier(
        (grad_reduce, spatial.got, expand.got)
    )
    spatial.go()
    expand.go()
    grad_reduce = after(spatial.sent, grad_reduce)
    reduce = Scatter(sizes, grad_reduce.reshape(places, -1, C_MID))
    reduce.go()

    heads.cross(reduce.sent)
    back = reduce_full.T
    grad_late, upstream_late = after(reduce.sent, (grad_one, upstream))
    grad_images = (
        jnp.dot(grad_late[:image_rows], back, preferred_element_type=jnp.float32)
        + upstream_late[:image_rows]
    ).astype(low)
    reduce.got, heads.got, grad_images = lax.optimization_barrier(
        (reduce.got, heads.got, grad_images)
    )
    grad_images = grad_images.reshape(SIDE, SIDE, image_slots, C_IN).transpose(2, 0, 1, 3)
    reduce.go()

    predictions = lax.dot_general(
        reorder,
        after(reduce.sent, made["predictions"]),
        (((0,), (0,)), ((), ())),
        preferred_element_type=jnp.float32,
    ).astype(low)
    reduce.got, predictions = lax.optimization_barrier((reduce.got, predictions))
    reduce.go()
    expand.cross(reduce.sent)
    spatial.cross(reduce.sent)

    grad_late, upstream_late = after(reduce.sent, (grad_one, upstream))
    grad_crops = (
        jnp.dot(grad_late[image_rows:], back, preferred_element_type=jnp.float32)
        + upstream_late[image_rows:]
    ).astype(low)
    grad_crops = grad_crops.reshape(CROP_SIDE, CROP_SIDE, crop_slots, C_IN).transpose(2, 0, 1, 3)
    reduce.got, expand.got, spatial.got, grad_crops = lax.optimization_barrier(
        (reduce.got, expand.got, spatial.got, grad_crops)
    )
    reduce.cross(reduce.sent)
    heads.got, expand.got, spatial.got = after(
        reduce.held, (heads.got, expand.got, spatial.got)
    )
    shard_heads, shard_expand = heads.close(), expand.close()
    shard_spatial, shard_reduce = spatial.close(), reduce.close()

    norm_gains, norm_shifts = after(reduce.held, (norm_gains, norm_shifts))
    gain_one, gain_two, gain_three, shift_one, shift_two, shift_three = after(
        reduce.held, (gain_one, gain_two, gain_three, shift_one, shift_two, shift_three)
    )
    norm_grads = jnp.stack(
        [
            jnp.concatenate([gain_one, gain_two, gain_three]),
            jnp.concatenate([shift_one, shift_two, shift_three]),
        ]
    )
    norm_shard = lax.dynamic_slice_in_dim(
        norm_grads, lax.axis_index("wide") * norm_width, norm_width, 1
    )
    local_squares = (
        jnp.sum(jnp.square(shard_reduce), axis=0)
        + jnp.sum(jnp.square(shard_spatial), axis=0)
        + jnp.sum(jnp.square(shard_expand).reshape(-1, C_MID), axis=0)
        + jnp.pad(jnp.sum(jnp.square(shard_heads), axis=0), (0, C_MID - TASKS * HEAD))
    )
    squares = jnp.sum(
        sum_rounds(
            sizes,
            local_squares.reshape(-1, LANES),
            [(swap_wide, masks) for masks in rounds_of(sizes[1])],
        )
    ) + jnp.sum(jnp.square(norm_grads))
    norm_before = jnp.sqrt(squares)
    factor = clip_bound / jnp.maximum(norm_before, clip_bound)
    new_reduce, moment_reduce, square_reduce = adamw_step(
        reduce_weight, shard_reduce * factor, first_reduce, second_reduce, weight_rate, weight_decay
    )
    new_spatial, moment_spatial, square_spatial = adamw_step(
        spatial_weight,
        shard_spatial * factor,
        first_spatial,
        second_spatial,
        weight_rate,
        weight_decay,
    )
    new_expand, moment_expand, square_expand = adamw_step(
        expand_weight, shard_expand * factor, first_expand, second_expand, weight_rate, weight_decay
    )
    new_heads, moment_heads, square_heads = adamw_step(
        heads_weight, shard_heads * factor, first_heads, second_heads, weight_rate, weight_decay
    )
    new_norm, moment_norm, square_norm = adamw_step(
        jnp.stack([norm_gains, norm_shifts]),
        norm_shard * factor,
        first_norm,
        second_norm,
        norm_rate,
        0.0,
    )
    return (
        norm_before,
        predictions,
        grad_images,
        grad_crops,
        new_reduce,
        new_spatial,
        new_expand,
        new_heads,
        new_norm,
        moment_reduce,
        moment_spatial,
        moment_expand,
        moment_heads,
        moment_norm,
        square_reduce,
        square_spatial,
        square_expand,
        square_heads,
        square_norm,
    )


def solution(mesh):
    sizes = (mesh.shape["dp"], mesh.shape["wide"])
    return jax.shard_map(
        functools.partial(local, sizes),
        mesh=mesh,
        in_specs=(
            P(("dp", "wide"), None, None, None),
            P(("dp", "wide"), None, None, None),
            P(("dp", "wide"), None),
            P(("dp", "wide"), None),
            P(("dp", "wide")),
            P(("dp", "wide")),
            P("wide", None),
            P("wide", None),
            P("wide", None),
            P("wide", None),
            P("wide"),
            P("wide"),
            P("wide", None),
            P("wide", None),
            P("wide", None),
            P("wide", None),
            P(None, "wide"),
            P("wide", None),
            P("wide", None),
            P("wide", None),
            P("wide", None),
            P(None, "wide"),
        ),
        out_specs=(
            P(),
            P(("dp", "wide"), None),
            P(("dp", "wide"), None, None, None),
            P(("dp", "wide"), None, None, None),
            P("wide", None),
            P("wide", None),
            P("wide", None),
            P("wide", None),
            P(None, "wide"),
            P("wide", None),
            P("wide", None),
            P("wide", None),
            P("wide", None),
            P(None, "wide"),
            P("wide", None),
            P("wide", None),
            P("wide", None),
            P("wide", None),
            P(None, "wide"),
        ),
        check_vma=False,
    )
```

```python
import functools

import jax
import jax.numpy as jnp
from jax import lax
from jax.experimental import pallas as pl
from jax.experimental.pallas import tpu as pltpu
from jax.sharding import PartitionSpec as P

C_IN = 2048
C_MID = 512
HEAD = 128
TASKS = 3
SIDE = 7
CROP_SIDE = 2
STEP = 10
IMG_CAP = 24
CROP_CAP = 16


norm_eps = 1e-05
soft_scale = 0.05
purity_temper = 0.1
clip_bound = 1.0
first_decay = 0.9
second_decay = 0.999
adam_eps = 1e-08
weight_rate = 0.02
norm_rate = 0.5
weight_decay = 0.1


def silu_slope(values):
    sigma = jax.nn.sigmoid(values)
    return sigma * (1.0 + values * (1.0 - sigma))


def soft_drop(task_grads, thresh):
    together = task_grads[0]
    magnitude = jnp.sqrt(task_grads[0] * task_grads[0] + soft_scale * soft_scale)
    for further in task_grads[1:]:
        together = together + further
        magnitude = magnitude + jnp.sqrt(further * further + soft_scale * soft_scale)
    purity = 0.5 * (1.0 + together / magnitude)
    upward = jax.nn.sigmoid((purity - thresh) / purity_temper)
    combined = jnp.zeros_like(together)
    for grad_part in task_grads:
        keeping = upward * jax.nn.sigmoid(grad_part / soft_scale) + (1.0 - upward) * jax.nn.sigmoid(
            -grad_part / soft_scale
        )
        combined = combined + grad_part * keeping
    return combined


def adamw_step(weights, gradient, moment, square, step_rate, decay_rate):
    moment_new = first_decay * moment + (1.0 - first_decay) * gradient
    square_new = second_decay * square + (1.0 - second_decay) * gradient * gradient
    moment_hat = moment_new / (1.0 - first_decay**STEP)
    square_hat = square_new / (1.0 - second_decay**STEP)
    updated = weights - step_rate * (
        moment_hat / (jnp.sqrt(square_hat) + adam_eps) + decay_rate * weights
    )
    return (updated, moment_new, square_new)


BOTH = ("dp", "wide")
LANES = 128


def bits_of(size):
    return [1 << k for k in range(size.bit_length() - 1)]


def swap_dp(sizes, values, mask):
    return lax.ppermute(values, "dp", [(i, i ^ mask) for i in range(sizes[0])])


def swap_wide(sizes, values, mask):
    return lax.ppermute(values, "wide", [(i, i ^ mask) for i in range(sizes[1])])


def rounds_of(size):
    left = bits_of(size)[::-1]
    rounds = []
    while left:
        pair, left = left[:2], left[2:]
        rounds.append((pair[1], pair[0], pair[0] | pair[1]) if len(pair) == 2 else (pair[0],))
    return rounds


def all_rounds(sizes):
    return [(swap_dp, masks) for masks in rounds_of(sizes[0])] + [
        (swap_wide, masks) for masks in rounds_of(sizes[1])
    ]


def beside(job, token, got):
    if job is None:
        return got
    return lax.optimization_barrier((got, job(token)))[0]


def after(token, values):
    return lax.optimization_barrier((values, token))[0]


def both_jobs(one, other):
    return lambda token: (one(token), other(token))


def sum_rounds(sizes, values, rounds, jobs=()):
    for level, (swap, masks) in enumerate(rounds):
        got = [swap(sizes, values, mask) for mask in masks]
        got = beside(jobs[level] if level < len(jobs) else None, values, got)
        if len(masks) == 3:
            values = (values + got[0]) + (got[1] + got[2])
        else:
            values = values + got[0]
    return values


def pool(first, second):
    count_a, total_a, spread_a = first
    count_b, total_b, spread_b = second
    count = count_a + count_b
    apart = total_a / count_a - total_b / count_b
    weight = count_a * count_b / count
    return (count, total_a + total_b, (spread_a + spread_b) + (apart * apart) * weight)


def pool_all(sizes, count, total, spread, counts, jobs):
    seen = []
    total, spread = total.reshape(-1, LANES), spread.reshape(-1, LANES)
    for level, (swap, masks) in enumerate(all_rounds(sizes)):
        parts = [total, spread]
        if counts is None:
            parts.append(jnp.broadcast_to(count, total.shape))
        packet = jnp.stack(parts)
        got = [swap(sizes, packet, mask) for mask in masks]
        got = beside(jobs[level] if level < len(jobs) else None, packet, got)
        seen.append((count, [g[2, :1] for g in got]) if counts is None else counts[level])
        sets = [(seen[-1][0], total, spread)] + [
            (c, g[0], g[1]) for c, g in zip(seen[-1][1], got)
        ]
        if len(sets) == 4:
            sets = [pool(sets[0], sets[1]), pool(sets[2], sets[3])]
        count, total, spread = pool(sets[0], sets[1])
    return (count, total, spread, seen)


def own_moments(values, live_mask, live_count):
    total = jnp.sum(values * live_mask, axis=0)
    own_mean = (total.reshape(-1, LANES) / live_count).reshape(values.shape[1])
    deviation = (values - own_mean) * live_mask
    return (total, jnp.sum(deviation * deviation, axis=0))


def batch_norm(sizes, moments, live_count, counts, jobs=()):
    total, spread = moments
    width = total.shape[0]
    counted, total, spread, counts = pool_all(sizes, live_count, total, spread, counts, jobs)
    inv_std = lax.rsqrt(spread / counted + norm_eps).reshape(width)
    return ((total / counted).reshape(width), inv_std, counted, counts)


def norm_back(
    sizes, upstream, normed, gain_part, inv_std, live_mask, counted, jobs=(), again=None
):
    width = upstream.shape[1]
    sums = sum_rounds(
        sizes,
        jnp.stack(
            [
                jnp.sum(upstream * normed, axis=0).reshape(-1, LANES),
                jnp.sum(upstream, axis=0).reshape(-1, LANES),
            ]
        ),
        all_rounds(sizes),
        jobs,
    )
    mean_gain = (sums[0] / counted).reshape(width)
    mean_shift = (sums[1] / counted).reshape(width)
    if again is not None:
        normed = again(mean_gain)
    grad_act = live_mask * (gain_part * inv_std) * (upstream - (mean_shift + normed * mean_gain))
    return (grad_act.astype(jnp.bfloat16), sums[0].reshape(width), sums[1].reshape(width))


def orders(size):
    down = bits_of(size)[::-1]
    return (down, down[:-2] + down[:-3:-1])


def crossing(sizes, step):
    pair = orders(sizes[1])
    return [
        (dp * sizes[1] + place, dp * sizes[1] + (place ^ pair[dp & 1][step]))
        for dp in range(sizes[0])
        for place in range(sizes[1])
    ]


def apart_of(sizes, core, slot):
    masks = []
    for order in orders(sizes[1]):
        mask = 0
        for k, bit in enumerate(order):
            if slot >> k & 1:
                mask ^= bit
        masks.append(mask)
    return jnp.where(core == 0, masks[0], masks[1])


def pick(blocks, index):
    return lax.dynamic_index_in_dim(blocks, index, 0, keepdims=True)


def settle_kernel(sizes, starts, *refs):
    outs, pieces = refs[-len(starts) :], refs[: -len(starts)]
    core, place = lax.axis_index("dp") & 1, lax.axis_index("wide")
    per_core = len(pieces) // 2
    for part, piece in enumerate(pieces):
        half = core if part < per_core else 1 - core
        for block in range(piece.shape[0]):
            slot = block + (part % per_core) * piece.shape[0]
            target = (place ^ apart_of(sizes, half, slot)) * 2 + half
            for start, out in zip(starts, outs):
                out[target] = piece[block, start : start + out.shape[1]]


def settle(sizes, pieces, heights):
    width = pieces[0].shape[2]
    count = 2 * sizes[1]
    starts = [sum(heights[:k]) for k in range(len(heights))]
    return pl.pallas_call(
        functools.partial(settle_kernel, sizes, starts),
        in_specs=[pl.BlockSpec(memory_space=pltpu.VMEM)] * len(pieces),
        out_specs=[pl.BlockSpec(memory_space=pltpu.VMEM)] * len(heights),
        out_shape=[
            jax.ShapeDtypeStruct((count, height, width), pieces[0].dtype) for height in heights
        ],
        compiler_params=pltpu.CompilerParams(vmem_limit_bytes=12 * 2**20),
        cost_estimate=pl.CostEstimate(
            flops=0, bytes_accessed=4 * count * sum(heights) * width, transcendentals=0
        ),
    )(*pieces)


def halves_of(shard):
    return shard.reshape(2, shard.shape[0] // 2, shard.shape[1])


def ring_own(shards):
    return pick(jnp.concatenate(shards, axis=1), lax.axis_index("dp") & 1)


def ring_step(sizes, held, step):
    return lax.ppermute(held, BOTH, crossing(sizes, step))


def ring_pieces(sizes, held, got):
    pieces = [held, got]
    return pieces + [swap_dp(sizes, piece, 1) for piece in pieces]


def ring_end(sizes, held, got, heights):
    return settle(sizes, ring_pieces(sizes, held, got), heights)


def third_halves(expand, heads):
    parts = halves_of(expand)
    four = jnp.concatenate(
        [parts[:, :, part * C_MID : (part + 1) * C_MID] for part in range(4)], axis=1
    )
    return jnp.concatenate([four, halves_of(heads)], axis=2)


def third_kernel(sizes, own_ref, other_ref, expand_ref, heads_ref):
    core, place = lax.axis_index("dp") & 1, lax.axis_index("wide")
    side = lax.axis_index("dp") >> 1 & 1
    rows, count = expand_ref.shape[1], own_ref.shape[0] // 2
    for half, piece in ((core, own_ref), (1 - core, other_ref)):
        for turn in range(2):
            quarter = side if turn == 0 else 1 - side
            for slot in range(count):
                block = turn * count + slot
                target = (place ^ apart_of(sizes, half, slot)) * 2 + half
                for part in range(2):
                    start = pl.multiple_of((2 * quarter + part) * C_MID, C_MID)
                    expand_ref[target, :, pl.ds(start, C_MID)] = piece[
                        block, part * rows : (part + 1) * rows, :C_MID
                    ]
                start = pl.multiple_of(quarter * 2 * rows, 2 * rows)
                heads_ref[target, pl.ds(start, 2 * rows)] = piece[block, :, C_MID:]


def settle_third(sizes, own, other):
    _, rows, width = own.shape
    count = 2 * sizes[1]
    return pl.pallas_call(
        functools.partial(third_kernel, sizes),
        in_specs=[pl.BlockSpec(memory_space=pltpu.VMEM)] * 2,
        out_specs=[pl.BlockSpec(memory_space=pltpu.VMEM)] * 2,
        out_shape=[
            jax.ShapeDtypeStruct((count, rows // 2, 4 * C_MID), own.dtype),
            jax.ShapeDtypeStruct((count, 2 * rows, width - C_MID), own.dtype),
        ],
        compiler_params=pltpu.CompilerParams(vmem_limit_bytes=12 * 2**20),
        cost_estimate=pl.CostEstimate(
            flops=0, bytes_accessed=8 * count * rows * width, transcendentals=0
        ),
    )(own, other)


def part_kernel(sizes, blocks_ref, sent_ref, kept_ref):
    core, place = lax.axis_index("dp") & 1, lax.axis_index("wide")
    for slot in range(sent_ref.shape[0]):
        source = (place ^ apart_of(sizes, 1 - core, slot)) * 2 + 1 - core
        sent_ref[slot] = blocks_ref[source].astype(sent_ref.dtype)
        kept_ref[slot] = blocks_ref[(place ^ apart_of(sizes, core, slot)) * 2 + core]


def part(sizes, blocks):
    _, rows, width = blocks.shape
    shape = (sizes[1], rows, width)
    return pl.pallas_call(
        functools.partial(part_kernel, sizes),
        in_specs=[pl.BlockSpec(memory_space=pltpu.VMEM)],
        out_specs=[pl.BlockSpec(memory_space=pltpu.VMEM)] * 2,
        out_shape=[
            jax.ShapeDtypeStruct(shape, jnp.bfloat16),
            jax.ShapeDtypeStruct(shape, jnp.float32),
        ],
        compiler_params=pltpu.CompilerParams(
            vmem_limit_bytes=14 * sizes[1] * rows * width + 2**21
        ),
        cost_estimate=pl.CostEstimate(
            flops=0, bytes_accessed=14 * sizes[1] * rows * width, transcendentals=0
        ),
    )(blocks)


def join_kernel(held_ref, got_ref, sent_ref, kept_ref):
    half = sent_ref.shape[0]
    for slot in range(half):
        kept_ref[slot] = held_ref[slot] + got_ref[slot].astype(jnp.float32)
        sent_ref[slot] = (
            held_ref[half + slot] + got_ref[half + slot].astype(jnp.float32)
        ).astype(sent_ref.dtype)


def join(held, got):
    count, rows, width = got.shape
    shape = (count // 2, rows, width)
    return pl.pallas_call(
        join_kernel,
        in_specs=[pl.BlockSpec(memory_space=pltpu.VMEM)] * 2,
        out_specs=[pl.BlockSpec(memory_space=pltpu.VMEM)] * 2,
        out_shape=[
            jax.ShapeDtypeStruct(shape, jnp.bfloat16),
            jax.ShapeDtypeStruct(shape, jnp.float32),
        ],
        compiler_params=pltpu.CompilerParams(vmem_limit_bytes=9 * count * rows * width + 2**21),
        cost_estimate=pl.CostEstimate(
            flops=count * rows * width, bytes_accessed=9 * count * rows * width, transcendentals=0
        ),
    )(held, got)


class Scatter:
    def __init__(self, sizes, grads):
        self.sizes, self.step = sizes, len(bits_of(sizes[1]))
        count, rows, width = grads.shape
        self.sent, self.held = part(sizes, grads.reshape(count * 2, rows // 2, width))
        self.got = swap_dp(sizes, self.sent, 1)

    def go(self, token=None):
        got = self.got if token is None else after(token, self.got)
        self.sent, self.held = join(self.held, got)
        self.step -= 1
        self.got = ring_step(self.sizes, self.sent, self.step)
        return self.sent

    def cross(self, token):
        while self.step:
            self.go()
        got = after(token, self.got)
        self.held = (self.held[0] + got[0].astype(jnp.float32)).astype(jnp.bfloat16)
        self.others = bits_of(self.sizes[0])[1:]
        self.got = swap_dp(self.sizes, self.held, self.others[0])

    def close(self):
        held, got = self.held, self.got
        for bit in self.others[1:]:
            held = (held.astype(jnp.float32) + got.astype(jnp.float32)).astype(jnp.bfloat16)
            got = swap_dp(self.sizes, held, bit)
        held = held.astype(jnp.float32) + got.astype(jnp.float32)
        other = swap_dp(self.sizes, held, 1)
        return jnp.where(
            lax.axis_index("dp") & 1 == 0,
            jnp.concatenate([held, other], axis=0),
            jnp.concatenate([other, held], axis=0),
        )


def neighbours(rows, image_slots, crop_slots):
    width = rows.shape[1]
    cut = image_slots * SIDE * SIDE
    images = jnp.pad(
        rows[:cut].reshape(SIDE, SIDE, image_slots, width), ((1, 1), (1, 1), (0, 0), (0, 0))
    )
    crops = jnp.pad(
        rows[cut:].reshape(CROP_SIDE, CROP_SIDE, crop_slots, width),
        ((1, 1), (1, 1), (0, 0), (0, 0)),
    )
    return [
        jnp.concatenate(
            [
                images[oy : oy + SIDE, ox : ox + SIDE].reshape(-1, width),
                crops[oy : oy + CROP_SIDE, ox : ox + CROP_SIDE].reshape(-1, width),
            ],
            axis=0,
        )
        for oy in range(3)
        for ox in range(3)
    ]


def conv_back(rows, weights, side, slots):
    width = rows.shape[1]
    got = lax.conv_general_dilated(
        rows.reshape(side, side, slots, width),
        weights.reshape(3, 3, width, width)[::-1, ::-1],
        (1, 1),
        "SAME",
        dimension_numbers=("HWNC", "HWOI", "HWNC"),
        preferred_element_type=jnp.float32,
    )
    return got.reshape(side * side * slots, width)


def drop_kernel(cot_ref, heads_ref, thresh_ref, *rest):
    out_ref = rest[-1]
    half_scale, half_temper = 0.5 / soft_scale, 0.5 / purity_temper
    together, magnitude, leaning = 0.0, 0.0, 0.0
    for task in range(TASKS):
        columns = slice(task * HEAD, (task + 1) * HEAD)
        part = lax.dot_general(
            cot_ref[:, columns],
            heads_ref[:, columns],
            (((1,), (1,)), ((), ())),
            preferred_element_type=jnp.float32,
        )
        square = part * part + soft_scale * soft_scale
        together = together + part
        magnitude = magnitude + square * lax.rsqrt(square)
        leaning = leaning + part * jnp.tanh(part * half_scale)
    lean = (
        thresh_ref[...].astype(jnp.float32) * -half_temper
        + 0.5 * half_temper
        + (together * (0.5 * half_temper)) / magnitude
    )
    out_ref[...] = 0.5 * (together + jnp.tanh(lean) * leaning)


DROP_TILE = 256


def soft_drop(cot_live, heads_full, thresh, skip, first, count, into=None):
    rows, width = thresh.shape[0], heads_full.shape[0]
    more = [] if into is None else [into]
    return pl.pallas_call(
        drop_kernel,
        grid=(count,),
        in_specs=[
            pl.BlockSpec((rows, TASKS * HEAD), lambda i: (0, 0)),
            pl.BlockSpec((DROP_TILE, TASKS * HEAD), lambda i: (first + i, 0)),
            pl.BlockSpec((rows, DROP_TILE), lambda i: (0, skip + i)),
        ]
        + [pl.BlockSpec(memory_space=pl.ANY)] * len(more),
        out_specs=pl.BlockSpec((rows, DROP_TILE), lambda i: (0, first + i)),
        out_shape=jax.ShapeDtypeStruct((rows, width), jnp.float32),
        input_output_aliases={3: 0} if more else {},
        compiler_params=pltpu.CompilerParams(vmem_limit_bytes=16 * 2**20),
        cost_estimate=pl.CostEstimate(
            flops=2 * rows * count * DROP_TILE * TASKS * HEAD,
            bytes_accessed=6 * rows * count * DROP_TILE,
            transcendentals=8 * rows * count * DROP_TILE,
        ),
    )(cot_live, heads_full, thresh, *more)


def slot_source(image_slots, crop_slots):
    def part(slots, pixels, start):
        return (jnp.arange(slots)[None, :] * pixels + jnp.arange(pixels)[:, None]).reshape(-1) + start

    images = image_slots * SIDE * SIDE
    return jnp.concatenate(
        [part(image_slots, SIDE * SIDE, 0), part(crop_slots, CROP_SIDE * CROP_SIDE, images)]
    )


def local(
    sizes,
    images,
    crop_pixels,
    thresholds,
    cotangent,
    image_count,
    crop_count,
    reduce_weight,
    spatial_weight,
    expand_weight,
    heads_weight,
    norm_gains,
    norm_shifts,
    first_reduce,
    first_spatial,
    first_expand,
    first_heads,
    first_norm,
    second_reduce,
    second_spatial,
    second_expand,
    second_heads,
    second_norm,
):
    low = jnp.bfloat16
    image_slots, crop_slots = images.shape[0], crop_pixels.shape[0]
    image_rows = image_slots * SIDE * SIDE
    rows = image_rows + crop_slots * CROP_SIDE * CROP_SIDE
    places = sizes[1]
    reorder = (
        slot_source(image_slots, crop_slots)[:, None] == jnp.arange(rows)[None, :]
    ).astype(low)

    norm_width = norm_gains.shape[0]
    norms = jnp.pad(
        jnp.stack([norm_gains, norm_shifts]).astype(low)[:, None],
        ((0, 0), (0, 15), (0, C_MID - norm_width)),
    )
    device = lax.axis_index("dp")
    third_own = third_halves(expand_weight.astype(low), heads_weight.astype(low))
    third_held = pick(
        third_own.reshape(4, third_own.shape[1] // 2, third_own.shape[2]),
        (device & 1) * 2 + (device >> 1 & 1),
    )
    first_shards = [halves_of(reduce_weight.astype(low)), norms]
    first_held = ring_own(first_shards)
    second_held = ring_own([halves_of(spatial_weight.astype(low))])

    live_mask = jnp.concatenate(
        [
            jnp.tile(jnp.arange(image_slots) < image_count[0], SIDE * SIDE),
            jnp.tile(jnp.arange(crop_slots) < crop_count[0], CROP_SIDE * CROP_SIDE),
        ]
    ).astype(jnp.float32)[:, None]
    live_count = jnp.broadcast_to(
        (image_count * (SIDE * SIDE) + crop_count * (CROP_SIDE * CROP_SIDE)).astype(jnp.float32)[
            None, :
        ],
        (1, LANES),
    )
    made = {}

    def make_inputs(token):
        image_part, crop_part = after(token, (images, crop_pixels))
        made["inputs"] = jnp.concatenate(
            [
                image_part.transpose(1, 2, 0, 3).reshape(image_rows, C_IN),
                crop_part.transpose(1, 2, 0, 3).reshape(-1, C_IN),
            ],
            axis=0,
        )
        return made["inputs"]

    def make_cotangent(token):
        made["cot"] = jnp.dot(
            reorder, after(token, cotangent), preferred_element_type=jnp.float32
        ).astype(low) * live_mask.astype(low)
        return made["cot"]

    def make_thresh(first, count):
        def job(token):
            columns = slice(first * DROP_TILE, (first + count) * DROP_TILE)
            made["thresh", first] = jnp.dot(
                reorder, after(token, thresholds[:, columns]), preferred_element_type=jnp.float32
            ).astype(low)
            return made["thresh", first]

        return job

    steps = len(bits_of(sizes[1]))
    for step in range(steps):
        job = {0: make_inputs, 1: make_cotangent}.get(step)
        first_got = beside(job, first_held, ring_step(sizes, first_held, step))
        if step == 0:
            second_held = after(first_got, second_held)
            second_got = ring_step(sizes, second_held, 0)
        if step < steps - 1:
            first_held = jnp.concatenate([first_held, first_got], axis=0)
    inputs, cot_live = made["inputs"], made["cot"]
    second_held = jnp.concatenate([second_held, after(first_got, second_got)], axis=0)
    inputs, second_held = lax.optimization_barrier((inputs, second_held))
    second_got = ring_step(sizes, second_held, 1)
    reduce_full, norms_full = ring_end(
        sizes, first_held, first_got, [shard.shape[1] for shard in first_shards]
    )
    reduce_full = reduce_full.reshape(C_IN, C_MID)
    norms_full = norms_full[:, 0, :norm_width].reshape(places, 2, norm_width)
    gain_full = norms_full[:, 0].reshape(-1).astype(jnp.float32)
    shift_full = norms_full[:, 1].reshape(-1).astype(jnp.float32)
    first_act = jnp.dot(inputs, reduce_full, preferred_element_type=jnp.float32)
    second_got = after(first_act, second_got)
    third_held = after(second_got, third_held)
    third_got = ring_step(sizes, third_held, 0)
    for step in range(2, steps):
        second_held = jnp.concatenate([second_held, second_got], axis=0)
        second_got = ring_step(sizes, second_held, step)

    def make_spatial(token):
        made["got"], made["third"] = after(token, (second_got, third_got))
        return (made["got"], made["third"])

    centre_one, inv_one, counted, counts = batch_norm(
        sizes,
        own_moments(first_act, live_mask, live_count),
        live_count,
        None,
        [None, None, make_spatial],
    )
    normed_one = (first_act - centre_one) * inv_one
    (spatial_full,) = ring_end(sizes, second_held, made["got"], [second_held.shape[1]])
    spatial_full = spatial_full.reshape(9 * C_MID, C_MID)
    pre_one = normed_one * gain_full[:C_MID] + shift_full[:C_MID]
    hidden_one = jax.nn.silu(pre_one).astype(low)
    third_held = jnp.concatenate([third_held, made["third"]], axis=0)
    third_got = ring_step(sizes, third_held, 1)
    hidden_one, spatial_full, third_got = lax.optimization_barrier(
        (hidden_one, spatial_full, third_got)
    )
    shifted = neighbours(hidden_one, image_slots, crop_slots)
    shifted = lax.optimization_barrier(shifted)
    for step in range(2, steps):
        third_held = jnp.concatenate([third_held, third_got], axis=0)
        third_got = ring_step(sizes, third_held, step)
    second_act = jnp.dot(
        jnp.concatenate(shifted, axis=1), spatial_full, preferred_element_type=jnp.float32
    )
    third_near = swap_dp(sizes, third_held, 2)
    second_act, third_got, third_near = lax.optimization_barrier(
        (second_act, third_got, third_near)
    )

    def cross_third(token):
        made["far"] = swap_dp(sizes, after(token, third_got), 2)
        return third_near

    def swap_third(token):
        near, far = after(token, (third_near, made["far"]))
        made["own"] = jnp.concatenate([third_held, third_got, near, far], axis=0)
        made["other"] = swap_dp(sizes, made["own"], 1)
        return made["own"]

    def make_drop(first, count):
        def job(token):
            cot, into = after(token, (cot_live, made.get("drop")))
            start = max(part for part in (0, 3, 6) if part <= first)
            made["drop"] = soft_drop(
                cot, heads_full, made["thresh", start], first - start, first, count, into
            )
            return made["drop"]

        return job

    centre_two, inv_two, counted, _ = batch_norm(
        sizes,
        own_moments(second_act, live_mask, live_count),
        live_count,
        counts,
        [
            both_jobs(cross_third, make_thresh(0, 3)),
            make_thresh(3, 3),
            both_jobs(swap_third, make_thresh(6, 2)),
        ],
    )
    normed_two = (second_act - centre_two) * inv_two
    pre_two = normed_two * gain_full[C_MID : 2 * C_MID] + shift_full[C_MID : 2 * C_MID]
    hidden_two = jax.nn.silu(pre_two).astype(low)
    expand_full, heads_full = settle_third(sizes, made["own"], made["other"])
    expand_full = expand_full.reshape(C_MID, C_IN)
    heads_full = heads_full.reshape(C_IN, TASKS * HEAD)
    def third_product(token):
        return jnp.dot(after(token, hidden_two), expand_full, preferred_element_type=jnp.float32)

    moments = []
    for part in range(4):
        act = jnp.dot(
            hidden_two,
            expand_full[:, part * C_MID : (part + 1) * C_MID],
            preferred_element_type=jnp.float32,
        )
        moments.append(own_moments(act, live_mask, live_count))
    centre_three, inv_three, counted, _ = batch_norm(
        sizes,
        [jnp.concatenate(sums) for sums in zip(*moments)],
        live_count,
        counts,
        [make_drop(0, 3), make_drop(3, 3), make_drop(6, 2)],
    )
    normed_three = (third_product(inv_three) - centre_three) * inv_three
    combined = made["drop"]
    summed = (
        normed_three * gain_full[2 * C_MID :] + shift_full[2 * C_MID :] + inputs.astype(jnp.float32)
    )
    trunk = jax.nn.silu(summed).astype(low)
    upstream = combined * silu_slope(summed)

    def make_heads(token):
        made["heads"] = jnp.dot(
            after(token, trunk).T, cot_live, preferred_element_type=jnp.float32
        )
        return made["heads"]

    def make_predictions(token):
        made["predictions"] = (
            jnp.dot(after(token, trunk), heads_full, preferred_element_type=jnp.float32) * live_mask
        ).astype(low)
        return made["predictions"]

    grad_three, gain_three, shift_three = norm_back(
        sizes,
        upstream,
        normed_three,
        gain_full[2 * C_MID :],
        inv_three,
        live_mask,
        counted,
        [None, make_heads, make_predictions],
        lambda token: (third_product(token) - centre_three) * inv_three,
    )
    heads = Scatter(sizes, made["heads"].reshape(places, -1, TASKS * HEAD))
    grad_three, _ = lax.optimization_barrier((grad_three, heads.go()))
    back_two = jnp.dot(grad_three, expand_full.T, preferred_element_type=jnp.float32) * silu_slope(
        pre_two
    )

    def make_expand(token):
        grad_expand = jnp.dot(
            hidden_two.T, after(token, grad_three), preferred_element_type=jnp.float32
        )
        made["expand"] = Scatter(sizes, grad_expand.reshape(places, -1, C_IN))
        return made["expand"].sent

    grad_two, gain_two, shift_two = norm_back(
        sizes,
        back_two,
        normed_two,
        gain_full[C_MID : 2 * C_MID],
        inv_two,
        live_mask,
        counted,
        [make_expand, heads.go, heads.go],
    )
    expand = made["expand"]
    grad_two, _ = lax.optimization_barrier((grad_two, expand.go()))
    grad_spatial = [
        jnp.dot(piece.T, grad_two, preferred_element_type=jnp.float32) for piece in shifted[:5]
    ]
    grad_spatial, heads.got = lax.optimization_barrier((grad_spatial, heads.got))
    grad_late = after(heads.got, grad_two)
    grad_spatial += [
        jnp.dot(piece.T, grad_late, preferred_element_type=jnp.float32) for piece in shifted[5:]
    ]
    grad_spatial = jnp.concatenate(grad_spatial, axis=0)
    spatial = Scatter(sizes, grad_spatial.reshape(places, -1, C_MID))
    grad_two, _ = lax.optimization_barrier((grad_two, spatial.sent))
    crop_back = conv_back(grad_two[image_rows:], spatial_full, CROP_SIDE, crop_slots)
    crop_back, image_grad, _ = lax.optimization_barrier(
        (crop_back, grad_two[:image_rows], spatial.go(crop_back))
    )
    image_back = conv_back(image_grad, spatial_full, SIDE, image_slots)
    back_one = jnp.concatenate([image_back, crop_back], axis=0) * silu_slope(pre_one)
    back_one, _ = lax.optimization_barrier((back_one, expand.go(image_back)))
    grad_one, gain_one, shift_one = norm_back(
        sizes,
        back_one,
        normed_one,
        gain_full[:C_MID],
        inv_one,
        live_mask,
        counted,
        [None, None, spatial.go],
    )
    grad_reduce = jnp.dot(inputs.T, grad_one, preferred_element_type=jnp.float32)

    grad_reduce, spatial.got, expand.got = lax.optimization_barrier(
        (grad_reduce, spatial.got, expand.got)
    )
    spatial.go()
    expand.go()
    grad_reduce = after(spatial.sent, grad_reduce)
    reduce = Scatter(sizes, grad_reduce.reshape(places, -1, C_MID))
    reduce.go()

    heads.cross(reduce.sent)
    back = reduce_full.T
    grad_late, upstream_late = after(reduce.sent, (grad_one, upstream))
    grad_images = (
        jnp.dot(grad_late[:image_rows], back, preferred_element_type=jnp.float32)
        + upstream_late[:image_rows]
    ).astype(low)
    reduce.got, heads.got, grad_images = lax.optimization_barrier(
        (reduce.got, heads.got, grad_images)
    )
    grad_images = grad_images.reshape(SIDE, SIDE, image_slots, C_IN).transpose(2, 0, 1, 3)
    reduce.go()

    predictions = lax.dot_general(
        reorder,
        after(reduce.sent, made["predictions"]),
        (((0,), (0,)), ((), ())),
        preferred_element_type=jnp.float32,
    ).astype(low)
    reduce.got, predictions = lax.optimization_barrier((reduce.got, predictions))
    reduce.go()
    expand.cross(reduce.sent)
    spatial.cross(reduce.sent)

    grad_late, upstream_late = after(reduce.sent, (grad_one, upstream))
    grad_crops = (
        jnp.dot(grad_late[image_rows:], back, preferred_element_type=jnp.float32)
        + upstream_late[image_rows:]
    ).astype(low)
    grad_crops = grad_crops.reshape(CROP_SIDE, CROP_SIDE, crop_slots, C_IN).transpose(2, 0, 1, 3)
    reduce.got, expand.got, spatial.got, grad_crops = lax.optimization_barrier(
        (reduce.got, expand.got, spatial.got, grad_crops)
    )
    reduce.cross(reduce.sent)
    heads.got, expand.got, spatial.got = after(
        reduce.held, (heads.got, expand.got, spatial.got)
    )
    shard_heads, shard_expand = heads.close(), expand.close()
    shard_spatial, shard_reduce = spatial.close(), reduce.close()

    norm_gains, norm_shifts = after(reduce.held, (norm_gains, norm_shifts))
    gain_one, gain_two, gain_three, shift_one, shift_two, shift_three = after(
        reduce.held, (gain_one, gain_two, gain_three, shift_one, shift_two, shift_three)
    )
    norm_grads = jnp.stack(
        [
            jnp.concatenate([gain_one, gain_two, gain_three]),
            jnp.concatenate([shift_one, shift_two, shift_three]),
        ]
    )
    norm_shard = lax.dynamic_slice_in_dim(
        norm_grads, lax.axis_index("wide") * norm_width, norm_width, 1
    )
    local_squares = (
        jnp.sum(jnp.square(shard_reduce), axis=0)
        + jnp.sum(jnp.square(shard_spatial), axis=0)
        + jnp.sum(jnp.square(shard_expand).reshape(-1, C_MID), axis=0)
        + jnp.pad(jnp.sum(jnp.square(shard_heads), axis=0), (0, C_MID - TASKS * HEAD))
    )
    squares = jnp.sum(
        sum_rounds(
            sizes,
            local_squares.reshape(-1, LANES),
            [(swap_wide, masks) for masks in rounds_of(sizes[1])],
        )
    ) + jnp.sum(jnp.square(norm_grads))
    norm_before = jnp.sqrt(squares)
    factor = clip_bound / jnp.maximum(norm_before, clip_bound)
    new_reduce, moment_reduce, square_reduce = adamw_step(
        reduce_weight, shard_reduce * factor, first_reduce, second_reduce, weight_rate, weight_decay
    )
    new_spatial, moment_spatial, square_spatial = adamw_step(
        spatial_weight,
        shard_spatial * factor,
        first_spatial,
        second_spatial,
        weight_rate,
        weight_decay,
    )
    new_expand, moment_expand, square_expand = adamw_step(
        expand_weight, shard_expand * factor, first_expand, second_expand, weight_rate, weight_decay
    )
    new_heads, moment_heads, square_heads = adamw_step(
        heads_weight, shard_heads * factor, first_heads, second_heads, weight_rate, weight_decay
    )
    new_norm, moment_norm, square_norm = adamw_step(
        jnp.stack([norm_gains, norm_shifts]),
        norm_shard * factor,
        first_norm,
        second_norm,
        norm_rate,
        0.0,
    )
    return (
        norm_before,
        predictions,
        grad_images,
        grad_crops,
        new_reduce,
        new_spatial,
        new_expand,
        new_heads,
        new_norm,
        moment_reduce,
        moment_spatial,
        moment_expand,
        moment_heads,
        moment_norm,
        square_reduce,
        square_spatial,
        square_expand,
        square_heads,
        square_norm,
    )


def solution(mesh):
    sizes = (mesh.shape["dp"], mesh.shape["wide"])
    return jax.shard_map(
        functools.partial(local, sizes),
        mesh=mesh,
        in_specs=(
            P(("dp", "wide"), None, None, None),
            P(("dp", "wide"), None, None, None),
            P(("dp", "wide"), None),
            P(("dp", "wide"), None),
            P(("dp", "wide")),
            P(("dp", "wide")),
            P("wide", None),
            P("wide", None),
            P("wide", None),
            P("wide", None),
            P("wide"),
            P("wide"),
            P("wide", None),
            P("wide", None),
            P("wide", None),
            P("wide", None),
            P(None, "wide"),
            P("wide", None),
            P("wide", None),
            P("wide", None),
            P("wide", None),
            P(None, "wide"),
        ),
        out_specs=(
            P(),
            P(("dp", "wide"), None),
            P(("dp", "wide"), None, None, None),
            P(("dp", "wide"), None, None, None),
            P("wide", None),
            P("wide", None),
            P("wide", None),
            P("wide", None),
            P(None, "wide"),
            P("wide", None),
            P("wide", None),
            P("wide", None),
            P("wide", None),
            P(None, "wide"),
            P("wide", None),
            P("wide", None),
            P("wide", None),
            P("wide", None),
            P(None, "wide"),
        ),
        check_vma=False,
    )
```

```python
import functools

import jax
import jax.numpy as jnp
from jax import lax
from jax.experimental import pallas as pl
from jax.experimental.pallas import tpu as pltpu
from jax.sharding import PartitionSpec as P

C_IN = 2048
C_MID = 512
HEAD = 128
TASKS = 3
SIDE = 7
CROP_SIDE = 2
STEP = 10
IMG_CAP = 24
CROP_CAP = 16


norm_eps = 1e-05
soft_scale = 0.05
purity_temper = 0.1
clip_bound = 1.0
first_decay = 0.9
second_decay = 0.999
adam_eps = 1e-08
weight_rate = 0.02
norm_rate = 0.5
weight_decay = 0.1


def silu_slope(values):
    sigma = jax.nn.sigmoid(values)
    return sigma * (1.0 + values * (1.0 - sigma))


def soft_drop(task_grads, thresh):
    together = task_grads[0]
    magnitude = jnp.sqrt(task_grads[0] * task_grads[0] + soft_scale * soft_scale)
    for further in task_grads[1:]:
        together = together + further
        magnitude = magnitude + jnp.sqrt(further * further + soft_scale * soft_scale)
    purity = 0.5 * (1.0 + together / magnitude)
    upward = jax.nn.sigmoid((purity - thresh) / purity_temper)
    combined = jnp.zeros_like(together)
    for grad_part in task_grads:
        keeping = upward * jax.nn.sigmoid(grad_part / soft_scale) + (1.0 - upward) * jax.nn.sigmoid(
            -grad_part / soft_scale
        )
        combined = combined + grad_part * keeping
    return combined


def adamw_step(weights, gradient, moment, square, step_rate, decay_rate):
    moment_new = first_decay * moment + (1.0 - first_decay) * gradient
    square_new = second_decay * square + (1.0 - second_decay) * gradient * gradient
    moment_hat = moment_new / (1.0 - first_decay**STEP)
    square_hat = square_new / (1.0 - second_decay**STEP)
    updated = weights - step_rate * (
        moment_hat / (jnp.sqrt(square_hat) + adam_eps) + decay_rate * weights
    )
    return (updated, moment_new, square_new)


BOTH = ("dp", "wide")
LANES = 128


def bits_of(size):
    return [1 << k for k in range(size.bit_length() - 1)]


def swap_dp(sizes, values, mask):
    return lax.ppermute(values, "dp", [(i, i ^ mask) for i in range(sizes[0])])


def swap_wide(sizes, values, mask):
    return lax.ppermute(values, "wide", [(i, i ^ mask) for i in range(sizes[1])])


def rounds_of(size):
    left = bits_of(size)[::-1]
    rounds = []
    while left:
        pair, left = left[:2], left[2:]
        rounds.append((pair[1], pair[0], pair[0] | pair[1]) if len(pair) == 2 else (pair[0],))
    return rounds


def all_rounds(sizes):
    return [(swap_dp, masks) for masks in rounds_of(sizes[0])] + [
        (swap_wide, masks) for masks in rounds_of(sizes[1])
    ]


def beside(job, token, got):
    if job is None:
        return got
    return lax.optimization_barrier((got, job(token)))[0]


def after(token, values):
    return lax.optimization_barrier((values, token))[0]


def both_jobs(one, other):
    return lambda token: (one(token), other(token))


def sum_rounds(sizes, values, rounds, jobs=()):
    for level, (swap, masks) in enumerate(rounds):
        got = [swap(sizes, values, mask) for mask in masks]
        got = beside(jobs[level] if level < len(jobs) else None, values, got)
        if len(masks) == 3:
            values = (values + got[0]) + (got[1] + got[2])
        else:
            values = values + got[0]
    return values


def pool(first, second):
    count_a, total_a, spread_a = first
    count_b, total_b, spread_b = second
    count = count_a + count_b
    apart = total_a / count_a - total_b / count_b
    weight = count_a * count_b / count
    return (count, total_a + total_b, (spread_a + spread_b) + (apart * apart) * weight)


def pool_all(sizes, count, total, spread, counts, jobs):
    seen = []
    total, spread = total.reshape(-1, LANES), spread.reshape(-1, LANES)
    for level, (swap, masks) in enumerate(all_rounds(sizes)):
        parts = [total, spread]
        if counts is None:
            parts.append(jnp.broadcast_to(count, total.shape))
        packet = jnp.stack(parts)
        got = [swap(sizes, packet, mask) for mask in masks]
        got = beside(jobs[level] if level < len(jobs) else None, packet, got)
        seen.append((count, [g[2, :1] for g in got]) if counts is None else counts[level])
        sets = [(seen[-1][0], total, spread)] + [
            (c, g[0], g[1]) for c, g in zip(seen[-1][1], got)
        ]
        if len(sets) == 4:
            sets = [pool(sets[0], sets[1]), pool(sets[2], sets[3])]
        count, total, spread = pool(sets[0], sets[1])
    return (count, total, spread, seen)


def own_moments(values, live_mask, live_count):
    total = jnp.sum(values * live_mask, axis=0)
    own_mean = (total.reshape(-1, LANES) / live_count).reshape(values.shape[1])
    deviation = (values - own_mean) * live_mask
    return (total, jnp.sum(deviation * deviation, axis=0))


def batch_norm(sizes, moments, live_count, counts, jobs=()):
    total, spread = moments
    width = total.shape[0]
    counted, total, spread, counts = pool_all(sizes, live_count, total, spread, counts, jobs)
    inv_std = lax.rsqrt(spread / counted + norm_eps).reshape(width)
    return ((total / counted).reshape(width), inv_std, counted, counts)


def norm_back(
    sizes, upstream, normed, gain_part, inv_std, live_mask, counted, jobs=(), again=None
):
    width = upstream.shape[1]
    sums = sum_rounds(
        sizes,
        jnp.stack(
            [
                jnp.sum(upstream * normed, axis=0).reshape(-1, LANES),
                jnp.sum(upstream, axis=0).reshape(-1, LANES),
            ]
        ),
        all_rounds(sizes),
        jobs,
    )
    mean_gain = (sums[0] / counted).reshape(width)
    mean_shift = (sums[1] / counted).reshape(width)
    if again is not None:
        normed = again(mean_gain)
    grad_act = live_mask * (gain_part * inv_std) * (upstream - (mean_shift + normed * mean_gain))
    return (grad_act.astype(jnp.bfloat16), sums[0].reshape(width), sums[1].reshape(width))


def orders(size):
    down = bits_of(size)[::-1]
    return (down, down[:-2] + down[:-3:-1])


def crossing(sizes, step):
    pair = orders(sizes[1])
    return [
        (dp * sizes[1] + place, dp * sizes[1] + (place ^ pair[dp & 1][step]))
        for dp in range(sizes[0])
        for place in range(sizes[1])
    ]


def apart_of(sizes, core, slot):
    masks = []
    for order in orders(sizes[1]):
        mask = 0
        for k, bit in enumerate(order):
            if slot >> k & 1:
                mask ^= bit
        masks.append(mask)
    return jnp.where(core == 0, masks[0], masks[1])


def pick(blocks, index):
    return lax.dynamic_index_in_dim(blocks, index, 0, keepdims=True)


def settle_kernel(sizes, starts, *refs):
    outs, pieces = refs[-len(starts) :], refs[: -len(starts)]
    core, place = lax.axis_index("dp") & 1, lax.axis_index("wide")
    per_core = len(pieces) // 2
    for part, piece in enumerate(pieces):
        half = core if part < per_core else 1 - core
        for block in range(piece.shape[0]):
            slot = block + (part % per_core) * piece.shape[0]
            target = (place ^ apart_of(sizes, half, slot)) * 2 + half
            for start, out in zip(starts, outs):
                out[target] = piece[block, start : start + out.shape[1]]


def settle(sizes, pieces, heights):
    width = pieces[0].shape[2]
    count = 2 * sizes[1]
    starts = [sum(heights[:k]) for k in range(len(heights))]
    return pl.pallas_call(
        functools.partial(settle_kernel, sizes, starts),
        in_specs=[pl.BlockSpec(memory_space=pltpu.VMEM)] * len(pieces),
        out_specs=[pl.BlockSpec(memory_space=pltpu.VMEM)] * len(heights),
        out_shape=[
            jax.ShapeDtypeStruct((count, height, width), pieces[0].dtype) for height in heights
        ],
        compiler_params=pltpu.CompilerParams(vmem_limit_bytes=12 * 2**20),
        cost_estimate=pl.CostEstimate(
            flops=0, bytes_accessed=4 * count * sum(heights) * width, transcendentals=0
        ),
    )(*pieces)


def halves_of(shard):
    return shard.reshape(2, shard.shape[0] // 2, shard.shape[1])


def ring_own(shards):
    return pick(jnp.concatenate(shards, axis=1), lax.axis_index("dp") & 1)


def ring_step(sizes, held, step):
    return lax.ppermute(held, BOTH, crossing(sizes, step))


def ring_pieces(sizes, held, got):
    pieces = [held, got]
    return pieces + [swap_dp(sizes, piece, 1) for piece in pieces]


def ring_end(sizes, held, got, heights):
    return settle(sizes, ring_pieces(sizes, held, got), heights)


def third_halves(expand, heads):
    parts = halves_of(expand)
    four = jnp.concatenate(
        [parts[:, :, part * C_MID : (part + 1) * C_MID] for part in range(4)], axis=1
    )
    return jnp.concatenate([four, halves_of(heads)], axis=2)


def third_kernel(sizes, own_ref, other_ref, expand_ref, heads_ref):
    core, place = lax.axis_index("dp") & 1, lax.axis_index("wide")
    side = lax.axis_index("dp") >> 1 & 1
    rows, count = expand_ref.shape[1], own_ref.shape[0] // 2
    for half, piece in ((core, own_ref), (1 - core, other_ref)):
        for turn in range(2):
            quarter = side if turn == 0 else 1 - side
            for slot in range(count):
                block = turn * count + slot
                target = (place ^ apart_of(sizes, half, slot)) * 2 + half
                for part in range(2):
                    start = pl.multiple_of((2 * quarter + part) * C_MID, C_MID)
                    expand_ref[target, :, pl.ds(start, C_MID)] = piece[
                        block, part * rows : (part + 1) * rows, :C_MID
                    ]
                start = pl.multiple_of(quarter * 2 * rows, 2 * rows)
                heads_ref[target, pl.ds(start, 2 * rows)] = piece[block, :, C_MID:]


def settle_third(sizes, own, other):
    _, rows, width = own.shape
    count = 2 * sizes[1]
    return pl.pallas_call(
        functools.partial(third_kernel, sizes),
        in_specs=[pl.BlockSpec(memory_space=pltpu.VMEM)] * 2,
        out_specs=[pl.BlockSpec(memory_space=pltpu.VMEM)] * 2,
        out_shape=[
            jax.ShapeDtypeStruct((count, rows // 2, 4 * C_MID), own.dtype),
            jax.ShapeDtypeStruct((count, 2 * rows, width - C_MID), own.dtype),
        ],
        compiler_params=pltpu.CompilerParams(vmem_limit_bytes=12 * 2**20),
        cost_estimate=pl.CostEstimate(
            flops=0, bytes_accessed=8 * count * rows * width, transcendentals=0
        ),
    )(own, other)


def part_kernel(sizes, blocks_ref, sent_ref, kept_ref):
    core, place = lax.axis_index("dp") & 1, lax.axis_index("wide")
    for slot in range(sent_ref.shape[0]):
        source = (place ^ apart_of(sizes, 1 - core, slot)) * 2 + 1 - core
        sent_ref[slot] = blocks_ref[source].astype(sent_ref.dtype)
        kept_ref[slot] = blocks_ref[(place ^ apart_of(sizes, core, slot)) * 2 + core]


def part(sizes, blocks):
    _, rows, width = blocks.shape
    shape = (sizes[1], rows, width)
    return pl.pallas_call(
        functools.partial(part_kernel, sizes),
        in_specs=[pl.BlockSpec(memory_space=pltpu.VMEM)],
        out_specs=[pl.BlockSpec(memory_space=pltpu.VMEM)] * 2,
        out_shape=[
            jax.ShapeDtypeStruct(shape, jnp.bfloat16),
            jax.ShapeDtypeStruct(shape, jnp.float32),
        ],
        compiler_params=pltpu.CompilerParams(
            vmem_limit_bytes=14 * sizes[1] * rows * width + 2**21
        ),
        cost_estimate=pl.CostEstimate(
            flops=0, bytes_accessed=14 * sizes[1] * rows * width, transcendentals=0
        ),
    )(blocks)


def join_kernel(held_ref, got_ref, sent_ref, kept_ref):
    half = sent_ref.shape[0]
    for slot in range(half):
        kept_ref[slot] = held_ref[slot] + got_ref[slot].astype(jnp.float32)
        sent_ref[slot] = (
            held_ref[half + slot] + got_ref[half + slot].astype(jnp.float32)
        ).astype(sent_ref.dtype)


def join(held, got):
    count, rows, width = got.shape
    shape = (count // 2, rows, width)
    return pl.pallas_call(
        join_kernel,
        in_specs=[pl.BlockSpec(memory_space=pltpu.VMEM)] * 2,
        out_specs=[pl.BlockSpec(memory_space=pltpu.VMEM)] * 2,
        out_shape=[
            jax.ShapeDtypeStruct(shape, jnp.bfloat16),
            jax.ShapeDtypeStruct(shape, jnp.float32),
        ],
        compiler_params=pltpu.CompilerParams(vmem_limit_bytes=9 * count * rows * width + 2**21),
        cost_estimate=pl.CostEstimate(
            flops=count * rows * width, bytes_accessed=9 * count * rows * width, transcendentals=0
        ),
    )(held, got)


class Scatter:
    def __init__(self, sizes, grads):
        self.sizes, self.step = sizes, len(bits_of(sizes[1]))
        count, rows, width = grads.shape
        self.sent, self.held = part(sizes, grads.reshape(count * 2, rows // 2, width))
        self.got = swap_dp(sizes, self.sent, 1)

    def go(self, token=None):
        got = self.got if token is None else after(token, self.got)
        self.sent, self.held = join(self.held, got)
        self.step -= 1
        self.got = ring_step(self.sizes, self.sent, self.step)
        return self.sent

    def cross(self, token):
        while self.step:
            self.go()
        got = after(token, self.got)
        self.held = (self.held[0] + got[0].astype(jnp.float32)).astype(jnp.bfloat16)
        self.others = bits_of(self.sizes[0])[1:]
        self.got = swap_dp(self.sizes, self.held, self.others[0])

    def close(self):
        held, got = self.held, self.got
        for bit in self.others[1:]:
            held = (held.astype(jnp.float32) + got.astype(jnp.float32)).astype(jnp.bfloat16)
            got = swap_dp(self.sizes, held, bit)
        held = held.astype(jnp.float32) + got.astype(jnp.float32)
        other = swap_dp(self.sizes, held, 1)
        return jnp.where(
            lax.axis_index("dp") & 1 == 0,
            jnp.concatenate([held, other], axis=0),
            jnp.concatenate([other, held], axis=0),
        )


def neighbours(rows, image_slots, crop_slots):
    width = rows.shape[1]
    cut = image_slots * SIDE * SIDE
    images = jnp.pad(
        rows[:cut].reshape(SIDE, SIDE, image_slots, width), ((1, 1), (1, 1), (0, 0), (0, 0))
    )
    crops = jnp.pad(
        rows[cut:].reshape(CROP_SIDE, CROP_SIDE, crop_slots, width),
        ((1, 1), (1, 1), (0, 0), (0, 0)),
    )
    return [
        jnp.concatenate(
            [
                images[oy : oy + SIDE, ox : ox + SIDE].reshape(-1, width),
                crops[oy : oy + CROP_SIDE, ox : ox + CROP_SIDE].reshape(-1, width),
            ],
            axis=0,
        )
        for oy in range(3)
        for ox in range(3)
    ]


def conv_back(rows, weights, side, slots):
    width = rows.shape[1]
    got = lax.conv_general_dilated(
        rows.reshape(side, side, slots, width),
        weights.reshape(3, 3, width, width)[::-1, ::-1],
        (1, 1),
        "SAME",
        dimension_numbers=("HWNC", "HWOI", "HWNC"),
        preferred_element_type=jnp.float32,
    )
    return got.reshape(side * side * slots, width)


def drop_kernel(cot_ref, heads_ref, thresh_ref, *rest):
    out_ref = rest[-1]
    half_scale, half_temper = 0.5 / soft_scale, 0.5 / purity_temper
    together, magnitude, leaning = 0.0, 0.0, 0.0
    for task in range(TASKS):
        columns = slice(task * HEAD, (task + 1) * HEAD)
        part = lax.dot_general(
            cot_ref[:, columns],
            heads_ref[:, columns],
            (((1,), (1,)), ((), ())),
            preferred_element_type=jnp.float32,
        )
        square = part * part + soft_scale * soft_scale
        together = together + part
        magnitude = magnitude + square * lax.rsqrt(square)
        leaning = leaning + part * jnp.tanh(part * half_scale)
    lean = (
        thresh_ref[...].astype(jnp.float32) * -half_temper
        + 0.5 * half_temper
        + (together * (0.5 * half_temper)) / magnitude
    )
    out_ref[...] = 0.5 * (together + jnp.tanh(lean) * leaning)


DROP_TILE = 256


def soft_drop(cot_live, heads_full, thresh, skip, first, count, into=None):
    rows, width = thresh.shape[0], heads_full.shape[0]
    more = [] if into is None else [into]
    return pl.pallas_call(
        drop_kernel,
        grid=(count,),
        in_specs=[
            pl.BlockSpec((rows, TASKS * HEAD), lambda i: (0, 0)),
            pl.BlockSpec((DROP_TILE, TASKS * HEAD), lambda i: (first + i, 0)),
            pl.BlockSpec((rows, DROP_TILE), lambda i: (0, skip + i)),
        ]
        + [pl.BlockSpec(memory_space=pl.ANY)] * len(more),
        out_specs=pl.BlockSpec((rows, DROP_TILE), lambda i: (0, first + i)),
        out_shape=jax.ShapeDtypeStruct((rows, width), jnp.float32),
        input_output_aliases={3: 0} if more else {},
        compiler_params=pltpu.CompilerParams(vmem_limit_bytes=16 * 2**20),
        cost_estimate=pl.CostEstimate(
            flops=2 * rows * count * DROP_TILE * TASKS * HEAD,
            bytes_accessed=6 * rows * count * DROP_TILE,
            transcendentals=8 * rows * count * DROP_TILE,
        ),
    )(cot_live, heads_full, thresh, *more)


def slot_source(image_slots, crop_slots):
    def part(slots, pixels, start):
        return (jnp.arange(slots)[None, :] * pixels + jnp.arange(pixels)[:, None]).reshape(-1) + start

    images = image_slots * SIDE * SIDE
    return jnp.concatenate(
        [part(image_slots, SIDE * SIDE, 0), part(crop_slots, CROP_SIDE * CROP_SIDE, images)]
    )


def local(
    sizes,
    images,
    crop_pixels,
    thresholds,
    cotangent,
    image_count,
    crop_count,
    reduce_weight,
    spatial_weight,
    expand_weight,
    heads_weight,
    norm_gains,
    norm_shifts,
    first_reduce,
    first_spatial,
    first_expand,
    first_heads,
    first_norm,
    second_reduce,
    second_spatial,
    second_expand,
    second_heads,
    second_norm,
):
    low = jnp.bfloat16
    image_slots, crop_slots = images.shape[0], crop_pixels.shape[0]
    image_rows = image_slots * SIDE * SIDE
    rows = image_rows + crop_slots * CROP_SIDE * CROP_SIDE
    places = sizes[1]
    reorder = (
        slot_source(image_slots, crop_slots)[:, None] == jnp.arange(rows)[None, :]
    ).astype(low)

    norm_width = norm_gains.shape[0]
    norms = jnp.pad(
        jnp.stack([norm_gains, norm_shifts]).astype(low)[:, None],
        ((0, 0), (0, 15), (0, C_MID - norm_width)),
    )
    device = lax.axis_index("dp")
    third_own = third_halves(expand_weight.astype(low), heads_weight.astype(low))
    third_held = pick(
        third_own.reshape(4, third_own.shape[1] // 2, third_own.shape[2]),
        (device & 1) * 2 + (device >> 1 & 1),
    )
    first_shards = [halves_of(reduce_weight.astype(low)), norms]
    first_held = ring_own(first_shards)
    second_held = ring_own([halves_of(spatial_weight.astype(low))])

    live_mask = jnp.concatenate(
        [
            jnp.tile(jnp.arange(image_slots) < image_count[0], SIDE * SIDE),
            jnp.tile(jnp.arange(crop_slots) < crop_count[0], CROP_SIDE * CROP_SIDE),
        ]
    ).astype(jnp.float32)[:, None]
    live_count = jnp.broadcast_to(
        (image_count * (SIDE * SIDE) + crop_count * (CROP_SIDE * CROP_SIDE)).astype(jnp.float32)[
            None, :
        ],
        (1, LANES),
    )
    made = {}

    def make_inputs(token):
        image_part, crop_part = after(token, (images, crop_pixels))
        made["inputs"] = jnp.concatenate(
            [
                image_part.transpose(1, 2, 0, 3).reshape(image_rows, C_IN),
                crop_part.transpose(1, 2, 0, 3).reshape(-1, C_IN),
            ],
            axis=0,
        )
        return made["inputs"]

    def make_cotangent(token):
        made["cot"] = jnp.dot(
            reorder, after(token, cotangent), preferred_element_type=jnp.float32
        ).astype(low) * live_mask.astype(low)
        return made["cot"]

    def make_thresh(first, count):
        def job(token):
            columns = slice(first * DROP_TILE, (first + count) * DROP_TILE)
            made["thresh", first] = jnp.dot(
                reorder, after(token, thresholds[:, columns]), preferred_element_type=jnp.float32
            ).astype(low)
            return made["thresh", first]

        return job

    steps = len(bits_of(sizes[1]))
    for step in range(steps):
        job = {0: make_inputs, 1: make_cotangent}.get(step)
        first_got = beside(job, first_held, ring_step(sizes, first_held, step))
        if step == 0:
            second_held = after(first_got, second_held)
            second_got = ring_step(sizes, second_held, 0)
        if step < steps - 1:
            first_held = jnp.concatenate([first_held, first_got], axis=0)
    inputs, cot_live = made["inputs"], made["cot"]
    second_held = jnp.concatenate([second_held, after(first_got, second_got)], axis=0)
    inputs, second_held = lax.optimization_barrier((inputs, second_held))
    second_got = ring_step(sizes, second_held, 1)
    reduce_full, norms_full = ring_end(
        sizes, first_held, first_got, [shard.shape[1] for shard in first_shards]
    )
    reduce_full = reduce_full.reshape(C_IN, C_MID)
    norms_full = norms_full[:, 0, :norm_width].reshape(places, 2, norm_width)
    gain_full = norms_full[:, 0].reshape(-1).astype(jnp.float32)
    shift_full = norms_full[:, 1].reshape(-1).astype(jnp.float32)
    first_act = jnp.dot(inputs, reduce_full, preferred_element_type=jnp.float32)
    second_got = after(first_act, second_got)
    third_held = after(second_got, third_held)
    third_got = ring_step(sizes, third_held, 0)
    for step in range(2, steps):
        second_held = jnp.concatenate([second_held, second_got], axis=0)
        second_got = ring_step(sizes, second_held, step)

    def make_spatial(token):
        made["got"], made["third"] = after(token, (second_got, third_got))
        return (made["got"], made["third"])

    centre_one, inv_one, counted, counts = batch_norm(
        sizes,
        own_moments(first_act, live_mask, live_count),
        live_count,
        None,
        [None, None, make_spatial],
    )
    normed_one = (first_act - centre_one) * inv_one
    (spatial_full,) = ring_end(sizes, second_held, made["got"], [second_held.shape[1]])
    spatial_full = spatial_full.reshape(9 * C_MID, C_MID)
    pre_one = normed_one * gain_full[:C_MID] + shift_full[:C_MID]
    hidden_one = jax.nn.silu(pre_one).astype(low)
    third_held = jnp.concatenate([third_held, made["third"]], axis=0)
    third_got = ring_step(sizes, third_held, 1)
    hidden_one, spatial_full, third_got = lax.optimization_barrier(
        (hidden_one, spatial_full, third_got)
    )
    shifted = neighbours(hidden_one, image_slots, crop_slots)
    shifted = lax.optimization_barrier(shifted)
    for step in range(2, steps):
        third_held = jnp.concatenate([third_held, third_got], axis=0)
        third_got = ring_step(sizes, third_held, step)
    second_act = jnp.dot(
        jnp.concatenate(shifted, axis=1), spatial_full, preferred_element_type=jnp.float32
    )
    third_near = swap_dp(sizes, third_held, 2)
    second_act, third_got, third_near = lax.optimization_barrier(
        (second_act, third_got, third_near)
    )

    def cross_third(token):
        made["far"] = swap_dp(sizes, after(token, third_got), 2)
        return third_near

    def swap_third(token):
        near, far = after(token, (third_near, made["far"]))
        made["own"] = jnp.concatenate([third_held, third_got, near, far], axis=0)
        made["other"] = swap_dp(sizes, made["own"], 1)
        return made["own"]

    def make_drop(first, count):
        def job(token):
            cot, into = after(token, (cot_live, made.get("drop")))
            start = max(part for part in (0, 3, 6) if part <= first)
            made["drop"] = soft_drop(
                cot, heads_full, made["thresh", start], first - start, first, count, into
            )
            return made["drop"]

        return job

    centre_two, inv_two, counted, _ = batch_norm(
        sizes,
        own_moments(second_act, live_mask, live_count),
        live_count,
        counts,
        [
            both_jobs(cross_third, make_thresh(0, 3)),
            make_thresh(3, 3),
            both_jobs(swap_third, make_thresh(6, 2)),
        ],
    )
    normed_two = (second_act - centre_two) * inv_two
    pre_two = normed_two * gain_full[C_MID : 2 * C_MID] + shift_full[C_MID : 2 * C_MID]
    hidden_two = jax.nn.silu(pre_two).astype(low)
    expand_full, heads_full = settle_third(sizes, made["own"], made["other"])
    expand_full = expand_full.reshape(C_MID, C_IN)
    heads_full = heads_full.reshape(C_IN, TASKS * HEAD)
    def third_product(token):
        return jnp.dot(after(token, hidden_two), expand_full, preferred_element_type=jnp.float32)

    moments = []
    for part in range(4):
        act = jnp.dot(
            hidden_two,
            expand_full[:, part * C_MID : (part + 1) * C_MID],
            preferred_element_type=jnp.float32,
        )
        moments.append(own_moments(act, live_mask, live_count))
    centre_three, inv_three, counted, _ = batch_norm(
        sizes,
        [jnp.concatenate(sums) for sums in zip(*moments)],
        live_count,
        counts,
        [make_drop(0, 3), make_drop(3, 3), make_drop(6, 2)],
    )
    normed_three = (third_product(inv_three) - centre_three) * inv_three
    combined = made["drop"]
    summed = (
        normed_three * gain_full[2 * C_MID :] + shift_full[2 * C_MID :] + inputs.astype(jnp.float32)
    )
    trunk = jax.nn.silu(summed).astype(low)
    upstream = combined * silu_slope(summed)

    def make_heads(token):
        made["heads"] = jnp.dot(
            after(token, trunk).T, cot_live, preferred_element_type=jnp.float32
        )
        return made["heads"]

    def make_predictions(token):
        made["predictions"] = (
            jnp.dot(after(token, trunk), heads_full, preferred_element_type=jnp.float32) * live_mask
        ).astype(low)
        return made["predictions"]

    grad_three, gain_three, shift_three = norm_back(
        sizes,
        upstream,
        normed_three,
        gain_full[2 * C_MID :],
        inv_three,
        live_mask,
        counted,
        [None, make_heads, make_predictions],
        lambda token: (third_product(token) - centre_three) * inv_three,
    )
    heads = Scatter(sizes, made["heads"].reshape(places, -1, TASKS * HEAD))
    grad_three, _ = lax.optimization_barrier((grad_three, heads.go()))
    back_two = jnp.dot(grad_three, expand_full.T, preferred_element_type=jnp.float32) * silu_slope(
        pre_two
    )

    def make_expand(token):
        grad_expand = jnp.dot(
            hidden_two.T, after(token, grad_three), preferred_element_type=jnp.float32
        )
        made["expand"] = Scatter(sizes, grad_expand.reshape(places, -1, C_IN))
        return made["expand"].sent

    grad_two, gain_two, shift_two = norm_back(
        sizes,
        back_two,
        normed_two,
        gain_full[C_MID : 2 * C_MID],
        inv_two,
        live_mask,
        counted,
        [make_expand, heads.go, heads.go],
    )
    expand = made["expand"]
    grad_two, _ = lax.optimization_barrier((grad_two, expand.go()))
    grad_spatial = [
        jnp.dot(piece.T, grad_two, preferred_element_type=jnp.float32) for piece in shifted[:5]
    ]
    grad_spatial, heads.got = lax.optimization_barrier((grad_spatial, heads.got))
    grad_late = after(heads.got, grad_two)
    grad_spatial += [
        jnp.dot(piece.T, grad_late, preferred_element_type=jnp.float32) for piece in shifted[5:]
    ]
    grad_spatial = jnp.concatenate(grad_spatial, axis=0)
    spatial = Scatter(sizes, grad_spatial.reshape(places, -1, C_MID))
    grad_two, _ = lax.optimization_barrier((grad_two, spatial.sent))
    crop_back = conv_back(grad_two[image_rows:], spatial_full, CROP_SIDE, crop_slots)
    crop_back, image_grad, _ = lax.optimization_barrier(
        (crop_back, grad_two[:image_rows], spatial.go(crop_back))
    )
    image_back = conv_back(image_grad, spatial_full, SIDE, image_slots)
    back_one = jnp.concatenate([image_back, crop_back], axis=0) * silu_slope(pre_one)
    back_one, _ = lax.optimization_barrier((back_one, expand.go(image_back)))
    grad_one, gain_one, shift_one = norm_back(
        sizes,
        back_one,
        normed_one,
        gain_full[:C_MID],
        inv_one,
        live_mask,
        counted,
        [None, None, spatial.go],
    )
    grad_reduce = jnp.dot(inputs.T, grad_one, preferred_element_type=jnp.float32)

    grad_reduce, spatial.got, expand.got = lax.optimization_barrier(
        (grad_reduce, spatial.got, expand.got)
    )
    spatial.go()
    expand.go()
    grad_reduce = after(spatial.sent, grad_reduce)
    reduce = Scatter(sizes, grad_reduce.reshape(places, -1, C_MID))
    reduce.go()

    heads.cross(reduce.sent)
    back = reduce_full.T
    grad_late, upstream_late = after(reduce.sent, (grad_one, upstream))
    grad_images = (
        jnp.dot(grad_late[:image_rows], back, preferred_element_type=jnp.float32)
        + upstream_late[:image_rows]
    ).astype(low)
    reduce.got, heads.got, grad_images = lax.optimization_barrier(
        (reduce.got, heads.got, grad_images)
    )
    grad_images = grad_images.reshape(SIDE, SIDE, image_slots, C_IN).transpose(2, 0, 1, 3)
    reduce.go()

    predictions = lax.dot_general(
        reorder,
        after(reduce.sent, made["predictions"]),
        (((0,), (0,)), ((), ())),
        preferred_element_type=jnp.float32,
    ).astype(low)
    reduce.got, predictions = lax.optimization_barrier((reduce.got, predictions))
    reduce.go()
    expand.cross(reduce.sent)
    spatial.cross(reduce.sent)

    grad_late, upstream_late = after(reduce.sent, (grad_one, upstream))
    grad_crops = (
        jnp.dot(grad_late[image_rows:], back, preferred_element_type=jnp.float32)
        + upstream_late[image_rows:]
    ).astype(low)
    grad_crops = grad_crops.reshape(CROP_SIDE, CROP_SIDE, crop_slots, C_IN).transpose(2, 0, 1, 3)
    reduce.got, expand.got, spatial.got, grad_crops = lax.optimization_barrier(
        (reduce.got, expand.got, spatial.got, grad_crops)
    )
    reduce.cross(reduce.sent)
    heads.got, expand.got, spatial.got = after(
        reduce.held, (heads.got, expand.got, spatial.got)
    )
    shard_heads, shard_expand = heads.close(), expand.close()
    shard_spatial, shard_reduce = spatial.close(), reduce.close()

    norm_gains, norm_shifts = after(reduce.held, (norm_gains, norm_shifts))
    gain_one, gain_two, gain_three, shift_one, shift_two, shift_three = after(
        reduce.held, (gain_one, gain_two, gain_three, shift_one, shift_two, shift_three)
    )
    norm_grads = jnp.stack(
        [
            jnp.concatenate([gain_one, gain_two, gain_three]),
            jnp.concatenate([shift_one, shift_two, shift_three]),
        ]
    )
    norm_shard = lax.dynamic_slice_in_dim(
        norm_grads, lax.axis_index("wide") * norm_width, norm_width, 1
    )
    local_squares = (
        jnp.sum(jnp.square(shard_reduce), axis=0)
        + jnp.sum(jnp.square(shard_spatial), axis=0)
        + jnp.sum(jnp.square(shard_expand).reshape(-1, C_MID), axis=0)
        + jnp.pad(jnp.sum(jnp.square(shard_heads), axis=0), (0, C_MID - TASKS * HEAD))
    )
    squares = jnp.sum(
        sum_rounds(
            sizes,
            local_squares.reshape(-1, LANES),
            [(swap_wide, masks) for masks in rounds_of(sizes[1])],
        ),
        keepdims=True,
    ) + jnp.sum(jnp.square(norm_grads), keepdims=True)
    norm_row = jnp.sqrt(squares)
    norm_before = norm_row[0, 0]
    factor = lax.optimization_barrier(
        jnp.broadcast_to(clip_bound / jnp.maximum(norm_row, clip_bound), (1, LANES))
    )[:, :1]
    new_reduce, moment_reduce, square_reduce = adamw_step(
        reduce_weight, shard_reduce * factor, first_reduce, second_reduce, weight_rate, weight_decay
    )
    new_spatial, moment_spatial, square_spatial = adamw_step(
        spatial_weight,
        shard_spatial * factor,
        first_spatial,
        second_spatial,
        weight_rate,
        weight_decay,
    )
    new_expand, moment_expand, square_expand = adamw_step(
        expand_weight, shard_expand * factor, first_expand, second_expand, weight_rate, weight_decay
    )
    new_heads, moment_heads, square_heads = adamw_step(
        heads_weight, shard_heads * factor, first_heads, second_heads, weight_rate, weight_decay
    )
    new_norm, moment_norm, square_norm = adamw_step(
        jnp.stack([norm_gains, norm_shifts]),
        norm_shard * factor,
        first_norm,
        second_norm,
        norm_rate,
        0.0,
    )
    return (
        norm_before,
        predictions,
        grad_images,
        grad_crops,
        new_reduce,
        new_spatial,
        new_expand,
        new_heads,
        new_norm,
        moment_reduce,
        moment_spatial,
        moment_expand,
        moment_heads,
        moment_norm,
        square_reduce,
        square_spatial,
        square_expand,
        square_heads,
        square_norm,
    )


def solution(mesh):
    sizes = (mesh.shape["dp"], mesh.shape["wide"])
    return jax.shard_map(
        functools.partial(local, sizes),
        mesh=mesh,
        in_specs=(
            P(("dp", "wide"), None, None, None),
            P(("dp", "wide"), None, None, None),
            P(("dp", "wide"), None),
            P(("dp", "wide"), None),
            P(("dp", "wide")),
            P(("dp", "wide")),
            P("wide", None),
            P("wide", None),
            P("wide", None),
            P("wide", None),
            P("wide"),
            P("wide"),
            P("wide", None),
            P("wide", None),
            P("wide", None),
            P("wide", None),
            P(None, "wide"),
            P("wide", None),
            P("wide", None),
            P("wide", None),
            P("wide", None),
            P(None, "wide"),
        ),
        out_specs=(
            P(),
            P(("dp", "wide"), None),
            P(("dp", "wide"), None, None, None),
            P(("dp", "wide"), None, None, None),
            P("wide", None),
            P("wide", None),
            P("wide", None),
            P("wide", None),
            P(None, "wide"),
            P("wide", None),
            P("wide", None),
            P("wide", None),
            P("wide", None),
            P(None, "wide"),
            P("wide", None),
            P("wide", None),
            P("wide", None),
            P("wide", None),
            P(None, "wide"),
        ),
        check_vma=False,
    )
```
